32 devices in a mesh: sta: 4 (over y, x), clu: 8 (over z, core).
Axes of the slice: x: 2, y: 2, z: 4, core: 2. Of those that a mesh axis runs over, the one named last changes fastest.
Arguments:
- spectra: bfloat16 [256, 256, 128], P('clu', 'sta'), may hold values from -6 to 6
- partials: bfloat16 [256, 4, 256], P('clu', None, 'sta')
- pair_list: int32 [256, 50], P('clu'), may hold values from -1 to 103, as said below
- station_mask: int32 [256, 50, 256], P('clu', None, 'sta'), may hold values 0 or 1
- exports: int32 [48, 12], P('clu'), may hold values from 0 to 31
Outputs:
- normal_blocks: float32 [16, 51, 256], P('sta', None, 'clu')
- right_sides: float32 [4, 256], P('sta', 'clu')
The draws below stay inside these ranges and needn't reach their ends.
Inputs may be any that keep to these rules, and one draw needn't show every extreme that they name: `pair_list`: each event's valid entries come first and the rest are -1; every event has 25 to 50 valid entries and the first event of every cluster has all 50. A valid entry below 32 names an event of the same cluster; entry 32 + h * 12 + c names the c-th event sent to this cluster by the cluster at cycle offset -o(h) from it, o(h) as for exports.
All inputs are finite; a program needn't handle non-finite values. No bound on the sum of `station_mask` on one device may be relied on, other than what follows from the above.
Results may differ from the reference program's by a relative error of at most 0.0047.
Values may be sent and summed in bfloat16 or wider, within the bound.
No kernel may reach another device: no remote copies, remote signals or barrier semaphores. Data moves between devices by JAX's collectives and lax.ppermute only.
A program may use at most 64 MiB of HBM per device.

```python
import math
import jax
import jax.numpy as jnp
from jax import lax

F = 64
NB = 50
HALF = 3
CAP = 12
E_DEV = 32
EVENTS = 256
STATIONS = 256
CANDS = 104
N_CLU = 8


def draw_partials(key, part):
    station_part = jax.random.normal(jax.random.fold_in(key, 11), (1, 4, STATIONS), jnp.float32)
    own_part = jax.random.normal(jax.random.fold_in(key, 12), (EVENTS, 4, STATIONS), jnp.float32)
    return (station_part + 0.6 * own_part).astype(jnp.bfloat16)


def draw_pair_list(key, part):
    counts = jax.random.randint(jax.random.fold_in(key, 21), (EVENTS,), NB // 2, NB + 1)
    firsts = jnp.arange(EVENTS, dtype=jnp.int32) % E_DEV == 0
    counts = jnp.where(firsts, NB, counts)
    near_pick = jax.random.randint(jax.random.fold_in(key, 22), (EVENTS, NB), 0, E_DEV)
    far_pick = jax.random.randint(jax.random.fold_in(key, 23), (EVENTS, NB), E_DEV, CANDS)
    coin = jax.random.randint(jax.random.fold_in(key, 24), (EVENTS, NB), 0, 5)
    chosen = jnp.where(coin < 3, near_pick, far_pick)
    slot_ids = jnp.arange(NB, dtype=jnp.int32)[None, :]
    return jnp.where(slot_ids < counts[:, None], chosen, -1).astype(jnp.int32)


def plant(array, own_key, least, high):
    place = [jax.random.randint(jax.random.fold_in(own_key, axis), (), 0, length) for axis, length in enumerate(array.shape)]
    longest = array.shape.index(max(array.shape))
    neighbour = place[:longest] + [(place[longest] + 1) % array.shape[longest]] + place[longest + 1:]
    return array.at[tuple(place)].set(least).at[tuple(neighbour)].set(high)


def level_of(stream_key, extent, pieces, smallest, high):
    gain = 1.0
    for dim, parts in pieces:
        steps = jax.random.uniform(jax.random.fold_in(jax.random.fold_in(stream_key, 6), dim), (parts,), jnp.float32, smallest / len(pieces), high / len(pieces))
        gain = gain * jnp.repeat(jnp.exp(steps), extent[dim] // parts).reshape((-1,) + (1,) * (len(extent) - 1 - dim))
    return gain


def scatter_about(key, extent, spread, most, pieces=(), held_as=jnp.bfloat16):
    entries = spread * jax.random.normal(key, extent, jnp.float32)
    if pieces:
        entries = entries * level_of(key, extent, pieces, -0.22, 0.18)
    return jnp.clip(entries, -most, most).astype(held_as)


def setup_inputs(seed: int = 0) -> dict:
    streams_of = jax.random.split(jax.random.key(seed), 6)
    spectra = scatter_about(streams_of[0], (EVENTS, STATIONS, 2 * F), 1.0, 6.0, ((0, 8), (1, 4)))
    partials = draw_partials(jax.random.fold_in(streams_of[5], 71), 0)
    pair_list = draw_pair_list(jax.random.fold_in(streams_of[5], 71), 0)
    station_mask = plant((jax.random.randint(streams_of[3], (EVENTS, NB, STATIONS), 0, 4) < 3).astype(jnp.int32), jax.random.fold_in(streams_of[3], 1), 0, 1)
    exports = plant(jax.random.randint(streams_of[4], (N_CLU * 2 * HALF, CAP), 0, E_DEV), jax.random.fold_in(streams_of[4], 1), 0, E_DEV - 1).astype(jnp.int32)
    return {"spectra": spectra, "partials": partials, "pair_list": pair_list, "station_mask": station_mask, "exports": exports}


def lag_tables(freq_count):
    freq_values = jnp.arange(freq_count, dtype=jnp.float32) * (math.pi / freq_count)
    lag_values = jnp.arange(2 * freq_count - 1, dtype=jnp.float32) - (freq_count - 1)
    phase_grid = freq_values[:, None] * lag_values[None, :]
    cosine_grid = jnp.cos(phase_grid)
    sine_grid = jnp.sin(phase_grid)
    real_rows = jnp.concatenate([cosine_grid, -freq_values[:, None] * sine_grid], axis=1)
    imag_rows = jnp.concatenate([-sine_grid, -freq_values[:, None] * cosine_grid], axis=1)
    lag_table = jnp.concatenate([real_rows, imag_rows], axis=0).astype(jnp.bfloat16)
    return (lag_table, lag_values)

def pair_weights(spec_one, spec_two, energy_one, energy_two, lag_table, lag_values, freq_count):
    first_vals = spec_one.astype(jnp.float32)
    second_vals = spec_two.astype(jnp.float32)
    real_a = first_vals[..., :freq_count]
    imag_a = first_vals[..., freq_count:]
    real_b = second_vals[..., :freq_count]
    imag_b = second_vals[..., freq_count:]
    cross_spec = jnp.concatenate([real_a * real_b + imag_a * imag_b, imag_a * real_b - real_a * imag_b], axis=-1).astype(jnp.bfloat16)
    lead_shape = cross_spec.shape[:-1]
    lagged = jnp.dot(cross_spec.reshape(-1, 2 * freq_count), lag_table, preferred_element_type=jnp.float32)
    lag_count = lag_values.shape[0]
    inverse = lax.rsqrt((energy_one * energy_two).reshape(-1) + 1e-06)
    correlation = lagged[:, :lag_count] * inverse[:, None]
    slope_fn = lagged[:, lag_count:] * inverse[:, None]
    power_sum = lax.optimization_barrier(jnp.sum(correlation * correlation, axis=1))
    rough_sum = lax.optimization_barrier(jnp.sum(slope_fn * slope_fn, axis=1))
    delay_lag = lax.optimization_barrier(jnp.sum(correlation * correlation * lag_values[None, :], axis=1)) / (power_sum + 1e-06)
    weight = power_sum / (power_sum + 0.125 * rough_sum + 1e-06)
    return (weight.reshape(lead_shape), delay_lag.reshape(lead_shape))

def reference(spectra, partials, pair_list, station_mask, exports):
    highest = lax.Precision.HIGHEST
    lag_table, lag_values = lag_tables(F)
    energy = lax.optimization_barrier(jnp.sum(jnp.square(spectra.astype(jnp.float32)), axis=-1))
    event_ids = jnp.arange(EVENTS, dtype=jnp.int32)
    owner_ids = (event_ids // E_DEV)[:, None]
    clipped = jnp.maximum(pair_list, 0)
    local_ids = owner_ids * E_DEV + jnp.minimum(clipped, E_DEV - 1)
    far_slot = jnp.maximum(clipped - E_DEV, 0)
    slot_group = far_slot // CAP
    cycle_offset = slot_group - HALF + (slot_group >= HALF).astype(jnp.int32)
    source = jnp.mod(owner_ids - cycle_offset + N_CLU, N_CLU)
    far_ids = source * E_DEV + exports[source * (2 * HALF) + slot_group, far_slot % CAP]
    partner = jnp.where(clipped < E_DEV, local_ids, far_ids).astype(jnp.int32)
    live_pairs = (pair_list >= 0).astype(jnp.float32)[..., None] * station_mask.astype(jnp.float32)
    block_size = max(E_DEV // 16, 1)
    group_count = EVENTS // block_size

    def one_block(inputs):
        spec_a, geo_a, energy_a, partner_b, live_b = inputs
        weight, delay_lag = pair_weights(spec_a[:, None], spectra[partner_b], energy_a[:, None], energy[partner_b], lag_table, lag_values, F)
        scaled = weight * live_b / STATIONS
        geo_one = geo_a.astype(jnp.float32)
        geo_two = partials[partner_b].astype(jnp.float32)
        diag_one = jnp.einsum('rks,ris,rjs->ijr', scaled, geo_one, geo_one, precision=highest).reshape(16, -1)
        off_diag = -jnp.einsum('rks,ris,rkjs->ijkr', scaled, geo_one, geo_two, precision=highest).reshape(16, NB, -1)
        right_one = jnp.einsum('rks,ris->ir', scaled * delay_lag, geo_one, precision=highest)
        diag_two = jnp.einsum('rks,rkis,rkjs->rkij', scaled, geo_two, geo_two, precision=highest).reshape(-1, 16)
        right_two = -jnp.einsum('rks,rkis->rki', scaled * delay_lag, geo_two, precision=highest).reshape(-1, 4)
        return (diag_one, off_diag, right_one, diag_two, right_two)
    blocked = (spectra.reshape(group_count, block_size, STATIONS, 2 * F), partials.reshape(group_count, block_size, 4, STATIONS), energy.reshape(group_count, block_size, STATIONS), partner.reshape(group_count, block_size, NB), live_pairs.reshape(group_count, block_size, NB, STATIONS))
    diag_one, off_diag, right_one, diag_two, right_two = lax.map(one_block, blocked)
    targets = partner.reshape(-1)
    diagonal = diag_one.transpose(1, 0, 2).reshape(16, EVENTS)
    diagonal = diagonal + jax.ops.segment_sum(diag_two.reshape(EVENTS * NB, 16), targets, num_segments=EVENTS).T
    off_blocks = off_diag.transpose(1, 2, 0, 3).reshape(16, NB, EVENTS)
    right_hand = right_one.transpose(1, 0, 2).reshape(4, EVENTS)
    right_hand = right_hand + jax.ops.segment_sum(right_two.reshape(EVENTS * NB, 4), targets, num_segments=EVENTS).T
    normal_blocks = jnp.concatenate([diagonal[:, None, :], off_blocks], axis=1)
    return (normal_blocks, right_hand)
```

```python
import functools
import math

import jax
import jax.numpy as jnp
import numpy as np
from jax import lax
from jax.experimental import pallas as pl
from jax.experimental.pallas import tpu as pltpu
from jax.sharding import PartitionSpec as P

F32 = jnp.float32
BF16 = jnp.bfloat16
VMEM_LIMIT = 56 * 1024 * 1024
SLOT_ROWS = 64
GROUP_ROWS = 16


def shifted(block, axis, distance):
    devices = range(lax.axis_size(axis))
    route = [((i - distance) % len(devices), i) for i in devices]
    return lax.ppermute(block, axis, route)


def moment_table(freq_count):
    f = np.arange(freq_count)

    def edge(k):
        out = np.zeros(k.shape)
        live = (k % (2 * freq_count)) != 0
        sign = 1.0 - 2.0 * (k[live] % 2)
        out[live] = -freq_count * sign / np.tan(np.pi * k[live] / (2 * freq_count))
        return out

    table = np.zeros((freq_count + 16, 2 * freq_count), np.float32)
    table[:freq_count, :freq_count] = -(edge(f[:, None] + f[None, :]) + edge(f[None, :] - f[:, None]))
    w = f * math.pi / freq_count
    table[freq_count, :freq_count] = (1.0 - 2.0 * (f % 2)) * w
    high = jnp.asarray(w * w, F32).astype(BF16)
    low = (jnp.asarray(w * w, F32) - high.astype(F32)).astype(BF16)
    table = jnp.asarray(table, F32).astype(BF16)
    table = table.at[freq_count + 1, freq_count:].set(high)
    return table.at[freq_count + 2, freq_count:].set(low)


def low_half(shape):
    return lax.broadcasted_iota(jnp.int32, shape, len(shape) - 1) < shape[-1] // 2


def outgoing_kernel(cap, exports_ref, spec_ref, geo_ref, *refs):
    outs, rows = refs[:-1], refs[-1]
    stations = spec_ref.shape[1]
    half = cap // 2
    body = cap * stations
    for h, out in enumerate(outs):
        rows[...] = jnp.zeros_like(rows)
        for c in range(cap):
            event = exports_ref[h, c]
            out[c * stations : (c + 1) * stations, :] = spec_ref[event]
            place = (c % 2) * half + c // 2
            rows[place : place + 1, :] = geo_ref[0, pl.ds(event, 1), :]
            rows[GROUP_ROWS + place : GROUP_ROWS + place + 1, :] = geo_ref[1, pl.ds(event, 1), :]
        out[body : body + 2 * GROUP_ROWS, :] = rows[...].astype(BF16)


def fold(x):
    rows = x.shape[0] // 8
    total = x[0:8]
    for r in range(1, rows):
        total = total + x[8 * r : 8 * r + 8]
    return total


def prepare(natural, bp, bb, eb, pairs, freq):
    for j in range(pairs):
        turned = natural(j).astype(F32).T
        bp[j] = turned
        re, im = turned[:freq], turned[freq:]
        square = re * re + im * im
        bb[j] = square
        eb[j : j + 1, :] = jnp.sum(square, axis=0, keepdims=True)


def dense_pairs(da, ea, bp, bb, eb, table, rm, rs, rt, rz, out, pairs, columns, freq, events, scale, batch):
    lead = lax.broadcasted_iota(jnp.int32, (8, 1), 0) == 0

    def one_event(e, js):
        a = da[e].astype(F32)
        ar, ai = a[:freq], a[freq:]
        square = ar * ar + ai * ai
        xs, reals, totals, alternates = [], [], [], []
        for j in js:
            br, bi = bp[j, :freq, :], bp[j, freq:, :]
            cr = ar * br + ai * bi
            ci = ai * br - ar * bi
            both = square * bb[j]
            xs.append(jnp.concatenate([ci.astype(BF16), both.astype(BF16)], axis=0))
            reals.append(cr.astype(BF16))
            edge = cr[0:8] * cr[0:8] - ci[0:8] * ci[0:8]
            totals.append(fold(both) + jnp.where(lead, edge, 0.0))
            alternates.append(fold(cr))
        z = jnp.dot(table[...], jnp.concatenate(xs, axis=1), preferred_element_type=F32)
        for i, j in enumerate(js):
            part = z[:, i * 128 : (i + 1) * 128]
            row = pl.ds(pl.multiple_of((j * events + e) * 8, 8), 8)
            rm[row, :] = fold(reals[i].astype(F32) * part[:freq])
            rs[row, :] = totals[i]
            rt[row, :] = alternates[i]
            rz[row, :] = part[freq : freq + 8]

    @pl.loop(0, events)
    def _(e):
        for start in range(0, pairs, batch):
            one_event(e, list(range(start, min(start + batch, pairs))))

    low = low_half((8, 128))

    @pl.loop(0, pairs)
    def _(j):
        energy_b = eb[pl.ds(j, 1), :]
        for e0 in range(0, events, 8):
            base = (j * events + e0) * 8

            def pick(ref, k):
                return ref[pl.ds(base + k, 8, stride=8), :]

            moment, total, alternate = pick(rm, 0), pick(rs, 0), pick(rt, 0)
            for k in range(1, 8):
                moment = moment + pick(rm, k)
                total = total + pick(rs, k)
                alternate = alternate + (1 - 2 * (k % 2)) * pick(rt, k)
            tilt = pick(rz, 0)
            bend = pick(rz, 1) + pick(rz, 2)
            inverse = 1.0 / (ea[e0 : e0 + 8, :] * energy_b + 1e-06)
            power = (freq * total - alternate * alternate) * inverse
            rough = (freq * bend - tilt * tilt) * inverse
            weight = power / (power + 0.125 * rough + 1e-06) * scale
            moved = weight * (moment * inverse / (power + 1e-06))
            even = jnp.where(low, weight, pltpu.roll(moved, 64, 1))
            odd = jnp.where(low, pltpu.roll(weight, 64, 1), moved)
            out[pl.ds(e0 * columns + j, 8, stride=columns), :] = even
            out[pl.ds(e0 * columns + pairs + j, 8, stride=columns), :] = odd


def local_kernel(freq, events, scale, spec_ref, table, out, da, ea, bp, bb, eb, rm, rs, rt, rz):
    pairs = events // 2
    prepare(lambda j: spec_ref[j], bp, bb, eb, pairs, freq)
    low = low_half((128, 128))
    for j in range(pairs):
        both = bp[j]
        other = pltpu.roll(both, 64, 1)
        da[2 * j] = jnp.where(low, both, other).astype(BF16)
        da[2 * j + 1] = jnp.where(low, other, both).astype(BF16)
    energy = eb[...]
    other = pltpu.roll(energy, 64, 1)
    low = low_half(energy.shape)
    ea[pl.ds(0, pairs, stride=2), :] = jnp.where(low, energy, other)
    ea[pl.ds(1, pairs, stride=2), :] = jnp.where(low, other, energy)
    dense_pairs(da, ea, bp, bb, eb, table, rm, rs, rt, rz, out, pairs, events, freq, events, scale, 4)


def import_kernel(freq, events, cap, scale, got_ref, da, ea, table, out, tail, bp, bb, eb, rm, rs, rt, rz):
    pairs = cap // 2
    prepare(lambda j: got_ref[j * 128 : (j + 1) * 128, :], bp, bb, eb, pairs, freq)
    out[...] = jnp.zeros_like(out)
    tail[...] = got_ref[cap // 2 * 128 :, :]
    dense_pairs(da, ea, bp, bb, eb, table, rm, rs, rt, rz, out, pairs, GROUP_ROWS, freq, events, scale, pairs)


def weight_scratch(pairs, events, freq):
    rows = pairs * events * 8
    return [
        pltpu.VMEM((pairs, 2 * freq, 128), F32),
        pltpu.VMEM((pairs, freq, 128), F32),
        pltpu.VMEM((-(-pairs // 8) * 8, 128), F32),
    ] + [pltpu.VMEM((rows, 128), F32)] * 4


def candidate_geo(own0, own1, tails):
    first = jnp.concatenate([own0] + [t[:GROUP_ROWS, :] for t in tails], axis=0)
    second = jnp.concatenate([own1] + [t[GROUP_ROWS:, :] for t in tails], axis=0)
    return first, second


def sums_kernel(groups, events, hot, hot_turned, mask, own_geo, *refs):
    tables, tails = refs[: groups + 1], refs[groups + 1 : 2 * groups + 1]
    slots_out, terms_out, geo_out, own = refs[2 * groups + 1 :]
    cands = hot.shape[1]

    @pl.loop(0, events)
    def _(e):
        parts = [tables[0][pl.ds(pl.multiple_of(e * events, 8), events), :]]
        for t in tables[1:]:
            parts.append(t[pl.ds(pl.multiple_of(e * GROUP_ROWS, 8), GROUP_ROWS), :])
        every = jnp.concatenate(parts, axis=0).astype(BF16)
        rows = pl.ds(pl.multiple_of(e * SLOT_ROWS, SLOT_ROWS), SLOT_ROWS)
        slots = jnp.dot(hot[rows, :], every, preferred_element_type=F32) * mask[rows, :].astype(F32)
        slots_out[rows, :] = slots.astype(BF16)
        place = (e % 2) * (events // 2) + e // 2
        own[pl.ds(place, 1), :] = jnp.sum(slots, axis=0, keepdims=True)

    gathered = jnp.dot(hot_turned[...], slots_out[...], preferred_element_type=F32)
    low = low_half((cands, 128))
    gathered = jnp.where(low, gathered, -gathered)
    totals = jnp.concatenate([gathered[:events] + own[...], gathered[events:]], axis=0)
    turned = pltpu.roll(totals, 64, 1)
    weights = jnp.where(low, totals, turned)
    moves = jnp.where(low, turned, totals)
    first, second = candidate_geo(own_geo[0], own_geo[1], [t[...] for t in tails])
    geo_out[:, :128] = first
    geo_out[:, 128:] = second
    blocks = [first.astype(F32), second.astype(F32)]
    singles = []
    for block in blocks:
        other = pltpu.roll(block, 64, 1)
        singles += [jnp.where(low, block, other), jnp.where(low, other, block)]
    half_row = lax.broadcasted_iota(jnp.int32, (8, 128), 0)
    half_lane = lax.broadcasted_iota(jnp.int32, (8, 128), 1) // 64
    picker = jnp.where(half_row == half_lane, 1.0, 0.0).astype(F32)

    def halves(values):
        return lax.dot_general(
            picker, values, (((1,), (1,)), ((), ())), precision=lax.Precision.HIGHEST, preferred_element_type=F32
        )[:2]

    rows = []
    for i in range(4):
        left = weights * singles[i]
        rows += [halves(left * blocks[0]), halves(left * blocks[1])]
    rows += [halves(moves * blocks[0]), halves(moves * blocks[1])]
    rows.append(jnp.zeros((4, 128), F32))
    terms_out[...] = jnp.concatenate(rows, axis=0)


def blocks_kernel(events, hot, slots, geo, left, out, turned):
    turned[...] = jnp.zeros_like(turned)
    low = low_half((SLOT_ROWS, 128))

    @pl.loop(0, events)
    def _(e):
        rows = pl.ds(pl.multiple_of(e * SLOT_ROWS, SLOT_ROWS), SLOT_ROWS)
        partner = jnp.dot(hot[rows, :], geo[...], preferred_element_type=F32)
        pair = slots[rows, :].astype(F32)
        weights = jnp.where(low, pair, pltpu.roll(pair, 64, 1))
        weighted = jnp.concatenate([weights * partner[:, :128], weights * partner[:, 128:]], axis=1).astype(BF16)
        entry = lax.dot_general(left[e], weighted, (((1,), (1,)), ((), ())), preferred_element_type=F32)
        turned[pl.ds(e, 16, stride=events), 0:SLOT_ROWS] = entry

    for i in range(4):
        out[i] = turned[i * 4 * events : (i + 1) * 4 * events, :].T[:SLOT_ROWS]


def message_kernel(groups, events, slots, place, blocks, owners, *refs):
    terms, outs, rows = refs[: groups + 1], refs[groups + 1 : -1], refs[-1]
    stacked = jnp.concatenate([t[...] for t in terms], axis=1)
    spread = jnp.dot(stacked, owners[...], precision=lax.Precision.HIGHEST, preferred_element_type=F32)
    block = lax.broadcasted_iota(jnp.int32, (1, 128), 1) // events
    for i in range(4):
        diagonal = jnp.zeros((1, 128), F32)
        for j in range(4):
            diagonal = jnp.where(block == j, spread[4 * i + j : 4 * i + j + 1], diagonal)
        rows[i, 0:1, :] = diagonal
        rows[i, 1:2, :] = spread[16 + i : 17 + i]
    for d, out in enumerate(outs):
        share = lax.rem(place[0] + d, 4)
        out[...] = blocks[share, 0 : out.shape[0], :]
        out[0:1, :] = rows[share, 0:1, :]
        out[slots + 1 : slots + 2, :] = rows[share, 1:2, :]


def total_kernel(events, slots, *refs):
    parts, normal, right = refs[:4], refs[4], refs[5]
    total = (parts[0][...] + parts[1][...]) + (parts[2][...] + parts[3][...])
    for j in range(4):
        moved = total if j == 0 else pltpu.roll(total, 128 - j * events, 1)
        normal[j] = moved[: slots + 1, :events]
    right[...] = total[slots + 1 : slots + 2, :events]


def vmem(n):
    return [pl.BlockSpec(memory_space=pltpu.VMEM)] * n


def call(kernel, outs, inputs, scratch=(), specs=None, micros=1.0):
    shapes = [jax.ShapeDtypeStruct(s, t) for s, t in outs]
    return pl.pallas_call(
        kernel,
        out_shape=shapes,
        in_specs=specs if specs is not None else vmem(len(inputs)),
        out_specs=vmem(len(outs)),
        scratch_shapes=list(scratch),
        compiler_params=pltpu.CompilerParams(vmem_limit_bytes=VMEM_LIMIT),
        cost_estimate=pl.CostEstimate(flops=int(micros * 1e9), bytes_accessed=1024, transcendentals=0),
    )(*inputs)


def on_device(spectra, partials, pair_list, station_mask, exports):
    events, stations, two_freq = spectra.shape
    freq = two_freq // 2
    groups, cap = exports.shape
    half_span = groups // 2
    slots = pair_list.shape[1]
    sta_groups = lax.axis_size("sta")
    scale = 1.0 / (stations * sta_groups)
    offsets = [h - half_span + (1 if h >= half_span else 0) for h in range(groups)]
    cands = events + groups * GROUP_ROWS
    half = cap // 2
    table = moment_table(freq)
    smem = pl.BlockSpec(memory_space=pltpu.SMEM)

    geo_rows = partials.reshape(events, 2, 2 * stations).transpose(1, 0, 2)
    out_rows = cap * stations + 2 * GROUP_ROWS
    outgoing = call(
        functools.partial(outgoing_kernel, cap),
        [((out_rows, 128), BF16)] * groups,
        (exports, spectra, geo_rows.astype(F32)),
        scratch=[pltpu.VMEM((2 * GROUP_ROWS, 128), F32)],
        specs=[smem] + vmem(2),
        micros=2.0,
    )
    order = sorted(range(groups), key=lambda h: -abs(offsets[h]))
    got = [None] * groups
    for h in order:
        got[h] = shifted(outgoing[h], "clu", offsets[h])

    local, dup, energy = call(
        functools.partial(local_kernel, freq, events, scale),
        [((events * events, 128), F32), ((events, 128, 128), BF16), ((events, 128), F32)],
        (spectra.reshape(events // 2, 2 * stations, two_freq), table),
        scratch=weight_scratch(events // 2, events, freq),
        micros=8.0,
    )

    m = pair_list
    near = (m % 2) * (events // 2) + m // 2
    far = jnp.maximum(m - events, 0)
    entry = far % cap
    far = events + GROUP_ROWS * (far // cap) + (entry % 2) * half + entry // 2
    column = jnp.where(m < 0, -1, jnp.where(m < events, near, far))
    column = jnp.pad(column, ((0, 0), (1, SLOT_ROWS - 1 - slots)), constant_values=-1).reshape(-1)
    cand_ids = jnp.arange(cands, dtype=jnp.int32)
    hot = (column[:, None] == cand_ids[None, :]).astype(BF16)
    hot_turned = (cand_ids[:, None] == column[None, :]).astype(BF16)
    mask = jnp.pad(station_mask, ((0, 0), (1, SLOT_ROWS - 1 - slots), (0, 0))).astype(BF16)
    mask = jnp.concatenate([mask, mask], axis=2).reshape(events * SLOT_ROWS, 128)
    own_geo = geo_rows.reshape(2, events // 2, 2, 128).transpose(0, 2, 1, 3).reshape(2, events, 128)
    eye = jnp.eye(4, dtype=BF16)
    left = -(partials[:, :, None, None, :] * eye[None, None, :, :, None]).reshape(events, 16, 4 * stations)
    cand_rank = np.arange(GROUP_ROWS)
    cand_entry = np.where(cand_rank < cap, 2 * (cand_rank % half) + cand_rank // half, 0)
    owner = jnp.where(jnp.asarray(cand_rank < cap)[None, :], exports[:, cand_entry], -1)
    local_rank = np.arange(cands)
    local_owner = np.where(local_rank < events, 2 * (local_rank % (events // 2)) + local_rank // (events // 2), -1)
    owner_rows = [jnp.asarray(local_owner, jnp.int32)]
    for h in range(groups):
        start = events + GROUP_ROWS * h
        owner_rows.append(jnp.pad(owner[h], (start, cands - start - GROUP_ROWS), constant_values=-1))
    owners = jnp.concatenate(owner_rows)[:, None] == (jnp.arange(128, dtype=jnp.int32) % events)[None, :]
    owners = owners.astype(F32)

    tables, tails = [None] * groups, [None] * groups
    for h in order[::-1]:
        tables[h], tails[h] = call(
            functools.partial(import_kernel, freq, events, cap, scale),
            [((events * GROUP_ROWS, 128), F32), ((2 * GROUP_ROWS, 128), BF16)],
            (got[h], dup, energy, table),
            scratch=weight_scratch(half, events, freq),
            micros=3.0,
        )

    weights, terms, geo = call(
        functools.partial(sums_kernel, groups, events),
        [((events * SLOT_ROWS, 128), BF16), ((24, 128), F32), ((cands, 256), BF16)],
        (hot, hot_turned, mask, own_geo, local, *tables, *tails),
        scratch=[pltpu.VMEM((events, 128), F32)],
        micros=2.0,
    )
    back = [shifted(terms, "clu", -offsets[h]) for h in range(groups)]
    (blocks,) = call(
        functools.partial(blocks_kernel, events),
        [((4, SLOT_ROWS, 128), F32)],
        (hot, weights, geo, left),
        scratch=[pltpu.VMEM((16 * events, 128), F32)],
        micros=3.0,
    )
    message_rows = -(-(slots + 2) // 8) * 8
    place = lax.axis_index("sta").astype(jnp.int32).reshape(1)
    messages = call(
        functools.partial(message_kernel, groups, events, slots),
        [((message_rows, 128), F32)] * 4,
        (place, blocks, owners, terms, *back),
        scratch=[pltpu.VMEM((4, 8, 128), F32)],
        specs=[smem] + vmem(3 + groups),
    )
    shares = [messages[0]] + [shifted(messages[d], "sta", d) for d in range(1, 4)]
    normal, right = call(
        functools.partial(total_kernel, events, slots),
        [((4, slots + 1, events), F32), ((1, events), F32)],
        shares,
    )
    return (normal, right)


def solution(mesh):
    return jax.shard_map(
        on_device,
        mesh=mesh,
        in_specs=(
            P("clu", "sta", None),
            P("clu", None, "sta"),
            P("clu", None),
            P("clu", None, "sta"),
            P("clu", None),
        ),
        out_specs=(P("sta", None, "clu"), P("sta", "clu")),
        check_vma=False,
    )
```

```python
import functools
import math

import jax
import jax.numpy as jnp
import numpy as np
from jax import lax
from jax.experimental import pallas as pl
from jax.experimental.pallas import tpu as pltpu
from jax.sharding import PartitionSpec as P

F32 = jnp.float32
BF16 = jnp.bfloat16
VMEM_LIMIT = 24 * 1024 * 1024
SLOT_ROWS = 64
GROUP_ROWS = 16
BATCH = 8
WIDE = 4
PAIR_BASE = 64
UNROLL = 4


def shifted(block, axis, distance):
    devices = range(lax.axis_size(axis))
    route = [((i - distance) % len(devices), i) for i in devices]
    return lax.ppermute(block, axis, route)


def moment_table(freq_count):
    f = np.arange(freq_count)

    def edge(k):
        out = np.zeros(k.shape)
        live = (k % (2 * freq_count)) != 0
        sign = 1.0 - 2.0 * (k[live] % 2)
        out[live] = -freq_count * sign / np.tan(np.pi * k[live] / (2 * freq_count))
        return out

    table = np.zeros((freq_count + 16, 2 * freq_count), np.float32)
    table[:freq_count, :freq_count] = -(edge(f[:, None] + f[None, :]) + edge(f[None, :] - f[:, None]))
    w = f * math.pi / freq_count
    table[freq_count, :freq_count] = (1.0 - 2.0 * (f % 2)) * w
    high = jnp.asarray(w * w, F32).astype(BF16)
    low = (jnp.asarray(w * w, F32) - high.astype(F32)).astype(BF16)
    table = jnp.asarray(table, F32).astype(BF16)
    table = table.at[freq_count + 1, freq_count:].set(high)
    return table.at[freq_count + 2, freq_count:].set(low)


def low_half(shape):
    return lax.broadcasted_iota(jnp.int32, shape, len(shape) - 1) < shape[-1] // 2


def outgoing_kernel(cap, exports_ref, spec_ref, geo_ref, *refs):
    outs, rows = refs[:-1], refs[-1]
    stations = spec_ref.shape[1]
    half = cap // 2
    body = cap * stations
    rows[...] = jnp.zeros_like(rows)
    for h, out in enumerate(outs):
        for c in range(cap):
            event = exports_ref[h, c]
            out[c * stations : (c + 1) * stations, :] = spec_ref[event]
            place = (c % 2) * half + c // 2
            geo = geo_ref[event].astype(F32)
            rows[place : place + 1, :] = jnp.concatenate([geo[0:1], geo[1:2]], axis=1)
            place += GROUP_ROWS
            rows[place : place + 1, :] = jnp.concatenate([geo[2:3], geo[3:4]], axis=1)
        out[body : body + 2 * GROUP_ROWS, :] = rows[...].astype(BF16)


def fold(x):
    rows = x.shape[0] // 8
    total = x[0:8]
    for r in range(1, rows):
        total = total + x[8 * r : 8 * r + 8]
    return total


def prepare(natural, bp, bb, eb, pairs, freq):
    for j in range(pairs):
        turned = natural(j).astype(F32).T
        bp[j] = turned
        re, im = turned[:freq], turned[freq:]
        square = re * re + im * im
        bb[j] = square
        eb[j : j + 1, :] = jnp.sum(square, axis=0, keepdims=True)


def listed_pairs(ids, batches, da, sq, ea, bp, bb, eb, table, work, store, freq, scale):
    xs, reals, rm, rs, rt, rz, re = work
    lead = lax.broadcasted_iota(jnp.int32, (8, 1), 0) == 0

    def split(t, u):
        code = ids[t * BATCH + u]
        return code >> 6, code & (PAIR_BASE - 1)

    def rows_of(t, u):
        return pl.ds(pl.multiple_of((t * BATCH + u) * 8, 8), 8)

    def cross_stage(t, slot):
        for u in range(BATCH):
            e, j = split(t, u)
            ar, ai = da[e, :freq, :], da[e, freq:, :]
            br, bi = bp[j, :freq, :], bp[j, freq:, :]
            cr = ar * br + ai * bi
            ci = ai * br - ar * bi
            both = sq[e] * bb[j]
            lanes = slice(u * 128, (u + 1) * 128)
            xs[slot, :freq, lanes] = ci.astype(BF16)
            xs[slot, freq:, lanes] = both.astype(BF16)
            reals[slot, :, lanes] = cr.astype(BF16)
            edge = cr[0:8] * cr[0:8] - ci[0:8] * ci[0:8]
            rs[rows_of(t, u), :] = fold(both) + jnp.where(lead, edge, 0.0)
            rt[rows_of(t, u), :] = fold(cr)
            re[pl.ds(t * BATCH + u, 1), :] = ea[pl.ds(e, 1), :] * eb[pl.ds(j, 1), :]

    def moment_stage(t, slot):
        for start in range(0, BATCH, WIDE):
            lanes = slice(start * 128, (start + WIDE) * 128)
            z = jnp.dot(table[...], xs[slot, :, lanes], preferred_element_type=F32)
            for i in range(WIDE):
                part = z[:, i * 128 : (i + 1) * 128]
                real = reals[slot, :, (start + i) * 128 : (start + i + 1) * 128].astype(F32)
                rm[rows_of(t, start + i), :] = fold(real * part[:freq])
                rz[rows_of(t, start + i), :] = part[freq : freq + 8]

    cross_stage(0, 0)

    @pl.loop(0, (batches + 1) // 2)
    def _(i):
        cross_stage(2 * i + 1, 1)
        moment_stage(2 * i, 0)
        cross_stage(2 * i + 2, 0)
        moment_stage(2 * i + 1, 1)

    low = low_half((8, 128))

    @pl.loop(0, batches)
    def _(t):
        base = t * BATCH * 8

        def pick(ref, k):
            return ref[pl.ds(base + k, 8, stride=8), :]

        moment, total, alternate = pick(rm, 0), pick(rs, 0), pick(rt, 0)
        for k in range(1, 8):
            moment = moment + pick(rm, k)
            total = total + pick(rs, k)
            alternate = alternate + (1 - 2 * (k % 2)) * pick(rt, k)
        tilt = pick(rz, 0)
        bend = pick(rz, 1) + pick(rz, 2)
        inverse = 1.0 / (re[pl.ds(pl.multiple_of(t * BATCH, 8), 8), :] + 1e-06)
        power = (freq * total - alternate * alternate) * inverse
        rough = (freq * bend - tilt * tilt) * inverse
        weight = power / (power + 0.125 * rough + 1e-06) * scale
        moved = weight * (moment * inverse / (power + 1e-06))
        even = jnp.where(low, weight, pltpu.roll(moved, 64, 1))
        odd = jnp.where(low, pltpu.roll(weight, 64, 1), moved)
        for u in range(BATCH):
            e, j = split(t, u)
            store(e, j, even[u : u + 1], odd[u : u + 1])


def local_kernel(freq, events, scale, items, ids, spec_ref, table, out, da, sq, ea, bp, bb, eb, *work):
    pairs = events // 2
    prepare(lambda j: spec_ref[j], bp, bb, eb, pairs, freq)
    low = low_half((128, 128))
    for j in range(pairs):
        both = bp[j]
        other = pltpu.roll(both, 64, 1)
        da[2 * j] = jnp.where(low, both, other)
        da[2 * j + 1] = jnp.where(low, other, both)
        both = bb[j]
        other = pltpu.roll(both, 64, 1)
        sq[2 * j] = jnp.where(low[:freq], both, other)
        sq[2 * j + 1] = jnp.where(low[:freq], other, both)
    energy = eb[...]
    other = pltpu.roll(energy, 64, 1)
    low = low_half(energy.shape)
    ea[pl.ds(0, pairs, stride=2), :] = jnp.where(low, energy, other)
    ea[pl.ds(1, pairs, stride=2), :] = jnp.where(low, other, energy)
    row = low_half((1, 128))

    def store(e, j, even, odd):
        own = (e & 1) * pairs + (e >> 1)
        out[pl.ds(e * events + j, 1), :] = even
        out[pl.ds(e * events + pairs + j, 1), :] = odd
        out[pl.ds(2 * j * events + own, 1), :] = jnp.where(row, even, -even)
        out[pl.ds((2 * j + 1) * events + own, 1), :] = jnp.where(row, odd, -odd)

    listed_pairs(ids, items // BATCH, da, sq, ea, bp, bb, eb, table, work, store, freq, scale)


def import_kernel(group, freq, events, cap, scale, ids, counts, got_ref, da, sq, ea, table, out, tail, bp, bb, eb, *work):
    pairs = cap // 2
    prepare(lambda j: got_ref[j * 128 : (j + 1) * 128, :], bp, bb, eb, pairs, freq)
    out[...] = jnp.zeros_like(out)
    tail[...] = got_ref[cap // 2 * 128 :, :]

    def store(e, j, even, odd):
        out[pl.ds(e * GROUP_ROWS + j, 1), :] = even
        out[pl.ds(e * GROUP_ROWS + pairs + j, 1), :] = odd

    batches = (counts[group] + BATCH - 1) // BATCH
    listed_pairs(ids.at[group], batches, da, sq, ea, bp, bb, eb, table, work, store, freq, scale)


def weight_scratch(pairs, items, freq):
    items = items + 2 * BATCH
    return [
        pltpu.VMEM((pairs, 2 * freq, 128), F32),
        pltpu.VMEM((pairs, freq, 128), F32),
        pltpu.VMEM((-(-pairs // 8) * 8, 128), F32),
        pltpu.VMEM((2, 2 * freq, BATCH * 128), BF16),
        pltpu.VMEM((2, freq, BATCH * 128), BF16),
    ] + [pltpu.VMEM((items * 8, 128), F32)] * 4 + [pltpu.VMEM((items, 128), F32)]


def candidate_geo(own0, own1, tails):
    first = jnp.concatenate([own0] + [t[:GROUP_ROWS, :] for t in tails], axis=0)
    second = jnp.concatenate([own1] + [t[GROUP_ROWS:, :] for t in tails], axis=0)
    return first, second


def sums_kernel(groups, events, hot, hot_turned, mask, own_geo, *refs):
    tables, tails = refs[: groups + 1], refs[groups + 1 : 2 * groups + 1]
    slots_out, terms_out, geo_out, own = refs[2 * groups + 1 :]
    cands = hot.shape[1]

    @pl.loop(0, events // UNROLL)
    def _(step):
        for u in range(UNROLL):
            e = step * UNROLL + u
            parts = [tables[0][pl.ds(pl.multiple_of(e * events, 8), events), :]]
            for t in tables[1:]:
                parts.append(t[pl.ds(pl.multiple_of(e * GROUP_ROWS, 8), GROUP_ROWS), :])
            every = jnp.concatenate(parts, axis=0).astype(BF16)
            rows = pl.ds(pl.multiple_of(e * SLOT_ROWS, SLOT_ROWS), SLOT_ROWS)
            slots = jnp.dot(hot[rows, :], every, preferred_element_type=F32) * mask[rows, :].astype(F32)
            slots_out[rows, :] = slots.astype(BF16)
            place = (u % 2) * (events // 2) + (e >> 1)
            own[pl.ds(place, 1), :] = jnp.sum(slots, axis=0, keepdims=True)

    gathered = jnp.dot(hot_turned[...], slots_out[...], preferred_element_type=F32)
    low = low_half((cands, 128))
    gathered = jnp.where(low, gathered, -gathered)
    totals = jnp.concatenate([gathered[:events] + own[...], gathered[events:]], axis=0)
    turned = pltpu.roll(totals, 64, 1)
    weights = jnp.where(low, totals, turned)
    moves = jnp.where(low, turned, totals)
    first, second = candidate_geo(own_geo[0], own_geo[1], [t[...] for t in tails])
    geo_out[:, :128] = first
    geo_out[:, 128:] = second
    blocks = [first.astype(F32), second.astype(F32)]
    singles = []
    for block in blocks:
        other = pltpu.roll(block, 64, 1)
        singles += [jnp.where(low, block, other), jnp.where(low, other, block)]
    half_row = lax.broadcasted_iota(jnp.int32, (8, 128), 0)
    half_lane = lax.broadcasted_iota(jnp.int32, (8, 128), 1) // 64
    picker = jnp.where(half_row == half_lane, 1.0, 0.0).astype(F32)

    def halves(values):
        return lax.dot_general(
            picker, values, (((1,), (1,)), ((), ())), precision=lax.Precision.HIGHEST, preferred_element_type=F32
        )[:2]

    rights = [halves(moves * blocks[0]), halves(moves * blocks[1])]
    for i in range(4):
        scaled = weights * singles[i]
        rows = [halves(scaled * blocks[0]), halves(scaled * blocks[1]), rights[i // 2][i % 2 : i % 2 + 1]]
        share = jnp.concatenate(rows + [jnp.zeros((3, 128), F32)], axis=0)
        for q in range(terms_out.shape[1]):
            terms_out[i, q] = share


def blocks_kernel(events, hot, slots, geo, left, out, turned):
    turned[...] = jnp.zeros_like(turned)
    low = low_half((SLOT_ROWS, 128))

    @pl.loop(0, events // UNROLL)
    def _(step):
        for u in range(UNROLL):
            e = step * UNROLL + u
            rows = pl.ds(pl.multiple_of(e * SLOT_ROWS, SLOT_ROWS), SLOT_ROWS)
            partner = jnp.dot(hot[rows, :], geo[...], preferred_element_type=F32)
            pair = slots[rows, :].astype(F32)
            weights = jnp.where(low, pair, pltpu.roll(pair, 64, 1))
            weighted = jnp.concatenate([weights * partner[:, :128], weights * partner[:, 128:]], axis=1).astype(BF16)
            entry = lax.dot_general(left[e], weighted, (((1,), (1,)), ((), ())), preferred_element_type=F32)
            turned[pl.ds(e, 16, stride=events), 0:SLOT_ROWS] = entry

    for i in range(4):
        out[i] = turned[i * 4 * events : (i + 1) * 4 * events, :].T[: out.shape[1]]


def total_kernel(groups, events, slots, clusters, blocks, received, owners, normal, right):
    parts = []
    for g in range(groups + 1):
        part = received[clusters[g]]
        for t in range(1, 4):
            part = part + received[t * (received.shape[0] // 4) + clusters[g]]
        parts.append(part)
    spread = jnp.dot(
        jnp.concatenate(parts, axis=1), owners[...], precision=lax.Precision.HIGHEST, preferred_element_type=F32
    )
    block = lax.broadcasted_iota(jnp.int32, (1, 128), 1) // events
    diagonal = jnp.zeros((1, 128), F32)
    for j in range(4):
        diagonal = jnp.where(block == j, spread[j : j + 1], diagonal)
    right[...] = spread[4:5, :events]
    total = (blocks[0] + blocks[1]) + (blocks[2] + blocks[3])
    top = lax.broadcasted_iota(jnp.int32, total.shape, 0) == 0
    total = jnp.where(top, diagonal, total)
    turned = total.T
    for j in range(4):
        normal[j] = turned[j * events : (j + 1) * events, : slots + 1]


def vmem(n):
    return [pl.BlockSpec(memory_space=pltpu.VMEM)] * n


def call(kernel, outs, inputs, scratch=(), specs=None, micros=1.0):
    shapes = [jax.ShapeDtypeStruct(s, t) for s, t in outs]
    return pl.pallas_call(
        kernel,
        out_shape=shapes,
        in_specs=specs if specs is not None else vmem(len(inputs)),
        out_specs=vmem(len(outs)),
        scratch_shapes=list(scratch),
        compiler_params=pltpu.CompilerParams(vmem_limit_bytes=VMEM_LIMIT),
        cost_estimate=pl.CostEstimate(flops=int(micros * 1e9), bytes_accessed=1024, transcendentals=0),
    )(*inputs)


def on_device(spectra, partials, pair_list, station_mask, exports):
    events, stations, two_freq = spectra.shape
    freq = two_freq // 2
    groups, cap = exports.shape
    half_span = groups // 2
    slots = pair_list.shape[1]
    sta_groups = lax.axis_size("sta")
    scale = 1.0 / (stations * sta_groups)
    offsets = [h - half_span + (1 if h >= half_span else 0) for h in range(groups)]
    cands = events + groups * GROUP_ROWS
    half = cap // 2
    table = moment_table(freq)
    smem = pl.BlockSpec(memory_space=pltpu.SMEM)
    clusters = lax.axis_size("clu")

    out_rows = cap * stations + 2 * GROUP_ROWS
    outgoing = call(
        functools.partial(outgoing_kernel, cap),
        [((out_rows, 128), BF16)] * groups,
        (exports, spectra, partials),
        scratch=[pltpu.VMEM((2 * GROUP_ROWS, 128), F32)],
        specs=[smem] + vmem(2),
        micros=2.0,
    )
    order = sorted(range(groups), key=lambda h: -abs(offsets[h]))
    got = [None] * groups
    for h in order:
        got[h] = shifted(outgoing[h], "clu", offsets[h])

    codes = [e * PAIR_BASE + j for e in range(events) for j in range(e // 2, events // 2)]
    items = -(-len(codes) // (2 * BATCH)) * 2 * BATCH
    codes = codes + [0] * (items + 2 * BATCH - len(codes))
    local, dup, square, energy = call(
        functools.partial(local_kernel, freq, events, scale, items),
        [
            ((events * events, 128), F32),
            ((events, 128, 128), F32),
            ((events, freq, 128), F32),
            ((events, 128), F32),
        ],
        (jnp.asarray(codes, jnp.int32), spectra.reshape(events // 2, 2 * stations, two_freq), table),
        scratch=weight_scratch(events // 2, items, freq),
        specs=[smem] + vmem(2),
        micros=8.0,
    )

    far = jnp.maximum(pair_list - events, 0)
    named = jnp.where(pair_list < events, -1, (far // cap) * half + (far % cap) // 2)
    wanted = jnp.any(named[:, :, None] == jnp.arange(groups * half, dtype=jnp.int32)[None, None, :], axis=1)
    wanted = wanted.reshape(events, groups, half).transpose(1, 0, 2).reshape(groups, events * half)
    item = np.arange(events * half)
    before = jnp.asarray(item[:, None] < item[None, :], BF16)
    rank = jnp.dot(wanted.astype(BF16), before, preferred_element_type=F32).astype(jnp.int32)
    item_code = jnp.asarray((item // half) * PAIR_BASE + item % half, jnp.int32)
    spot = jnp.where(wanted, rank, -1)
    longest = events * half + 3 * BATCH
    lists = jnp.sum(
        jnp.where(spot[:, None, :] == jnp.arange(longest, dtype=jnp.int32)[None, :, None], item_code[None, None, :], 0),
        axis=2,
    ).astype(jnp.int32)
    counts = jnp.sum(wanted.astype(jnp.int32), axis=1)

    m = pair_list
    near = (m % 2) * (events // 2) + m // 2
    entry = far % cap
    far = events + GROUP_ROWS * (far // cap) + (entry % 2) * half + entry // 2
    column = jnp.where(m < 0, -1, jnp.where(m < events, near, far))
    column = jnp.pad(column, ((0, 0), (1, SLOT_ROWS - 1 - slots)), constant_values=-1).reshape(-1)
    cand_ids = jnp.arange(cands, dtype=jnp.int32)
    hot = (column[:, None] == cand_ids[None, :]).astype(BF16)
    hot_turned = (cand_ids[:, None] == column[None, :]).astype(BF16)
    mask = jnp.pad(station_mask, ((0, 0), (1, SLOT_ROWS - 1 - slots), (0, 0))).astype(BF16)
    mask = jnp.concatenate([mask, mask], axis=2).reshape(events * SLOT_ROWS, 128)
    own_geo = partials.reshape(events // 2, 2, 2, 128).transpose(2, 1, 0, 3).reshape(2, events, 128)
    eye = jnp.eye(4, dtype=BF16)
    left = -(partials[:, :, None, None, :] * eye[None, None, :, :, None]).reshape(events, 16, 4 * stations)
    cand_rank = np.arange(GROUP_ROWS)
    cand_entry = np.where(cand_rank < cap, 2 * (cand_rank % half) + cand_rank // half, 0)
    owner = jnp.where(jnp.asarray(cand_rank < cap)[None, :], exports[:, cand_entry], -1)
    local_rank = np.arange(cands)
    local_owner = np.where(local_rank < events, 2 * (local_rank % (events // 2)) + local_rank // (events // 2), -1)
    owner_rows = [jnp.asarray(local_owner, jnp.int32)]
    for h in range(groups):
        start = events + GROUP_ROWS * h
        owner_rows.append(jnp.pad(owner[h], (start, cands - start - GROUP_ROWS), constant_values=-1))
    owners = jnp.concatenate(owner_rows)[:, None] == (jnp.arange(128, dtype=jnp.int32) % events)[None, :]
    owners = owners.astype(F32)

    tables, tails = [None] * groups, [None] * groups
    for h in order[::-1]:
        tables[h], tails[h] = call(
            functools.partial(import_kernel, h, freq, events, cap, scale),
            [((events * GROUP_ROWS, 128), F32), ((2 * GROUP_ROWS, 128), BF16)],
            (lists, counts, got[h], dup, square, energy, table),
            scratch=weight_scratch(half, events * half, freq),
            specs=[smem] * 2 + vmem(5),
            micros=3.0,
        )

    weights, terms, geo = call(
        functools.partial(sums_kernel, groups, events),
        [((events * SLOT_ROWS, 128), BF16), ((4, clusters, 8, 128), F32), ((cands, 256), BF16)],
        (hot, hot_turned, mask, own_geo, local, *tables, *tails),
        scratch=[pltpu.VMEM((events, 128), F32)],
        micros=2.0,
    )
    terms = lax.all_to_all(
        terms.reshape(4 * clusters, 8, 128), ("sta", "clu"), split_axis=0, concat_axis=0, tiled=True
    )
    message_rows = -(-(slots + 1) // 8) * 8
    (blocks,) = call(
        functools.partial(blocks_kernel, events),
        [((4, message_rows, 128), F32)],
        (hot, weights, geo, left),
        scratch=[pltpu.VMEM((16 * events, 128), F32)],
        micros=3.0,
    )
    blocks = lax.all_to_all(blocks, "sta", split_axis=0, concat_axis=0, tiled=True)
    sources = (lax.axis_index("clu") + jnp.asarray([0] + offsets, jnp.int32)) % clusters
    normal, right = call(
        functools.partial(total_kernel, groups, events, slots),
        [((4, events, slots + 1), F32), ((1, events), F32)],
        (sources.astype(jnp.int32), blocks, terms, owners),
        specs=[smem] + vmem(3),
    )
    return (normal.transpose(0, 2, 1), right)


def solution(mesh):
    return jax.shard_map(
        on_device,
        mesh=mesh,
        in_specs=(
            P("clu", "sta", None),
            P("clu", None, "sta"),
            P("clu", None),
            P("clu", None, "sta"),
            P("clu", None),
        ),
        out_specs=(P("sta", None, "clu"), P("sta", "clu")),
        check_vma=False,
    )
```

```python
import functools
import math

import jax
import jax.numpy as jnp
import numpy as np
from jax import lax
from jax.experimental import pallas as pl
from jax.experimental.pallas import tpu as pltpu
from jax.sharding import PartitionSpec as P

F32 = jnp.float32
BF16 = jnp.bfloat16
VMEM_LIMIT = 24 * 1024 * 1024
SLOT_ROWS = 64
GROUP_ROWS = 16
BATCH = 8
WIDE = 4
PAIR_BASE = 64
UNROLL = 4


def shifted(block, axis, distance):
    devices = range(lax.axis_size(axis))
    route = [((i - distance) % len(devices), i) for i in devices]
    return lax.ppermute(block, axis, route)


def moment_table(freq_count):
    f = np.arange(freq_count)

    def edge(k):
        out = np.zeros(k.shape)
        live = (k % (2 * freq_count)) != 0
        sign = 1.0 - 2.0 * (k[live] % 2)
        out[live] = -freq_count * sign / np.tan(np.pi * k[live] / (2 * freq_count))
        return out

    table = np.zeros((freq_count + 16, 2 * freq_count), np.float32)
    table[:freq_count, :freq_count] = -(edge(f[:, None] + f[None, :]) + edge(f[None, :] - f[:, None]))
    w = f * math.pi / freq_count
    table[freq_count, :freq_count] = (1.0 - 2.0 * (f % 2)) * w
    high = jnp.asarray(w * w, F32).astype(BF16)
    low = (jnp.asarray(w * w, F32) - high.astype(F32)).astype(BF16)
    table = jnp.asarray(table, F32).astype(BF16)
    table = table.at[freq_count + 1, freq_count:].set(high)
    return table.at[freq_count + 2, freq_count:].set(low)


def low_half(shape):
    return lax.broadcasted_iota(jnp.int32, shape, len(shape) - 1) < shape[-1] // 2


def outgoing_kernel(cap, exports_ref, spec_ref, geo_ref, *refs):
    outs, rows = refs[:-1], refs[-1]
    stations = spec_ref.shape[1]
    body = cap * stations
    rows[...] = jnp.zeros_like(rows)
    for h, out in enumerate(outs):
        for c in range(cap):
            event = exports_ref[h, c]
            out[c * stations : (c + 1) * stations, :] = spec_ref[event]
            place = c
            geo = geo_ref[event].astype(F32)
            rows[place : place + 1, :] = jnp.concatenate([geo[0:1], geo[1:2]], axis=1)
            place += GROUP_ROWS
            rows[place : place + 1, :] = jnp.concatenate([geo[2:3], geo[3:4]], axis=1)
        out[body : body + 2 * GROUP_ROWS, :] = rows[...].astype(BF16)


def fold(x):
    rows = x.shape[0] // 8
    total = x[0:8]
    for r in range(1, rows):
        total = total + x[8 * r : 8 * r + 8]
    return total


def prepare(natural, bp, bb, eb, pairs, freq):
    for j in range(pairs):
        turned = natural(j).astype(F32).T
        bp[j] = turned
        re, im = turned[:freq], turned[freq:]
        square = re * re + im * im
        bb[j] = square
        eb[j : j + 1, :] = jnp.sum(square, axis=0, keepdims=True)


def listed_pairs(ids, batches, da, sq, ea, bp, bb, eb, table, work, store, freq, scale):
    xs, reals, rm, rs, rt, rz, re = work
    lead = lax.broadcasted_iota(jnp.int32, (8, 1), 0) == 0
    low = low_half((8, 128))

    def split(t, u):
        code = ids[t * BATCH + u]
        return code >> 6, code & (PAIR_BASE - 1)

    def cross_stage(t, slot):
        for u in range(BATCH):
            e, j = split(t, u)
            ar, ai = da[e, :freq, :], da[e, freq:, :]
            br, bi = bp[j, :freq, :], bp[j, freq:, :]
            cr = ar * br + ai * bi
            ci = ai * br - ar * bi
            both = sq[e] * bb[j]
            lanes = slice(u * 128, (u + 1) * 128)
            rows = slice(u * 8, (u + 1) * 8)
            xs[slot, :freq, lanes] = ci.astype(BF16)
            xs[slot, freq:, lanes] = both.astype(BF16)
            reals[slot, :, lanes] = cr.astype(BF16)
            edge = cr[0:8] * cr[0:8] - ci[0:8] * ci[0:8]
            rs[slot, rows, :] = fold(both) + jnp.where(lead, edge, 0.0)
            rt[slot, rows, :] = fold(cr)
            re[slot, u : u + 1, :] = ea[pl.ds(e, 1), :] * eb[pl.ds(j, 1), :]

    def moment_stage(slot):
        for start in range(0, BATCH, WIDE):
            lanes = slice(start * 128, (start + WIDE) * 128)
            z = jnp.dot(table[...], xs[slot, :, lanes], preferred_element_type=F32)
            for i in range(WIDE):
                part = z[:, i * 128 : (i + 1) * 128]
                real = reals[slot, :, (start + i) * 128 : (start + i + 1) * 128].astype(F32)
                rows = slice((start + i) * 8, (start + i + 1) * 8)
                rm[slot, rows, :] = fold(real * part[:freq])
                rz[slot, rows, :] = part[freq : freq + 8]

    def finish_stage(t, slot):
        def pick(ref, k):
            return ref[slot, pl.ds(k, 8, stride=8), :]

        moment, total, alternate = pick(rm, 0), pick(rs, 0), pick(rt, 0)
        for k in range(1, 8):
            moment = moment + pick(rm, k)
            total = total + pick(rs, k)
            alternate = alternate + pick(rt, k) if k % 2 == 0 else alternate - pick(rt, k)
        tilt = pick(rz, 0)
        bend = pick(rz, 1) + pick(rz, 2)
        inverse = 1.0 / (re[slot] + 1e-06)
        power = (freq * total - alternate * alternate) * inverse
        rough = (freq * bend - tilt * tilt) * inverse
        weight = power / (power + 0.125 * rough + 1e-06) * scale
        moved = weight * (moment * inverse / (power + 1e-06))
        even = jnp.where(low, weight, pltpu.roll(moved, 64, 1))
        odd = jnp.where(low, pltpu.roll(weight, 64, 1), moved)
        for u in range(BATCH):
            e, j = split(t, u)
            store(e, j, even[u : u + 1], odd[u : u + 1])

    cross_stage(0, 0)

    @pl.loop(0, (batches + 1) // 2)
    def _(i):
        cross_stage(2 * i + 1, 1)
        moment_stage(0)
        finish_stage(2 * i, 0)
        cross_stage(2 * i + 2, 0)
        moment_stage(1)
        finish_stage(2 * i + 1, 1)


def local_kernel(freq, events, scale, items, ids, spec_ref, table, out, da, sq, ea, bp, bb, eb, *work):
    pairs = events // 2
    prepare(lambda j: spec_ref[j], bp, bb, eb, pairs, freq)
    low = low_half((128, 128))
    for j in range(pairs):
        both = bp[j]
        other = pltpu.roll(both, 64, 1)
        da[2 * j] = jnp.where(low, both, other)
        da[2 * j + 1] = jnp.where(low, other, both)
        both = bb[j]
        other = pltpu.roll(both, 64, 1)
        sq[2 * j] = jnp.where(low[:freq], both, other)
        sq[2 * j + 1] = jnp.where(low[:freq], other, both)
    energy = eb[...]
    other = pltpu.roll(energy, 64, 1)
    low = low_half(energy.shape)
    ea[pl.ds(0, pairs, stride=2), :] = jnp.where(low, energy, other)
    ea[pl.ds(1, pairs, stride=2), :] = jnp.where(low, other, energy)
    row = low_half((1, 128))

    def store(e, j, even, odd):
        out[pl.ds(e * events + 2 * j, 1), :] = even
        out[pl.ds(e * events + 2 * j + 1, 1), :] = odd
        out[pl.ds(2 * j * events + e, 1), :] = jnp.where(row, even, -even)
        out[pl.ds((2 * j + 1) * events + e, 1), :] = jnp.where(row, odd, -odd)

    listed_pairs(ids, items // BATCH, da, sq, ea, bp, bb, eb, table, work, store, freq, scale)


def import_kernel(group, freq, events, cap, scale, ids, counts, got_ref, da, sq, ea, table, out, tail, bp, bb, eb, *work):
    pairs = cap // 2
    prepare(lambda j: got_ref[j * 128 : (j + 1) * 128, :], bp, bb, eb, pairs, freq)
    out[...] = jnp.zeros_like(out)
    tail[...] = got_ref[cap // 2 * 128 :, :]

    def store(e, j, even, odd):
        out[pl.ds(e * GROUP_ROWS + 2 * j, 1), :] = even
        out[pl.ds(e * GROUP_ROWS + 2 * j + 1, 1), :] = odd

    batches = (counts[group] + BATCH - 1) // BATCH
    listed_pairs(ids.at[group], batches, da, sq, ea, bp, bb, eb, table, work, store, freq, scale)


def weight_scratch(pairs, freq):
    return (
        [
            pltpu.VMEM((pairs, 2 * freq, 128), F32),
            pltpu.VMEM((pairs, freq, 128), F32),
            pltpu.VMEM((-(-pairs // 8) * 8, 128), F32),
            pltpu.VMEM((2, 2 * freq, BATCH * 128), BF16),
            pltpu.VMEM((2, freq, BATCH * 128), BF16),
        ]
        + [pltpu.VMEM((2, BATCH * 8, 128), F32)] * 4
        + [pltpu.VMEM((2, BATCH, 128), F32)]
    )


def sums_kernel(groups, events, slots, hot, hot_turned, mask, partials, *refs):
    tables, tails = refs[: groups + 1], refs[groups + 1 : 2 * groups + 1]
    slots_out, terms_out, geo_out, own, own_geo = refs[2 * groups + 1 :]
    cands = hot.shape[1]
    rest = jnp.zeros((SLOT_ROWS - slots, 128), F32)

    @pl.loop(0, events // UNROLL)
    def _(step):
        for u in range(UNROLL):
            e = step * UNROLL + u
            parts = [tables[0][pl.ds(pl.multiple_of(e * events, 8), events), :]]
            for t in tables[1:]:
                parts.append(t[pl.ds(pl.multiple_of(e * GROUP_ROWS, 8), GROUP_ROWS), :])
            every = jnp.concatenate(parts, axis=0).astype(BF16)
            rows = pl.ds(pl.multiple_of(e * SLOT_ROWS, SLOT_ROWS), SLOT_ROWS)
            live = mask[pl.ds(e, slots, stride=events), :].astype(F32)
            live = jnp.concatenate([jnp.concatenate([live, live], axis=1), rest], axis=0)
            picked = jnp.dot(hot[rows, :], every, preferred_element_type=F32) * live
            slots_out[rows, :] = picked.astype(BF16)
            own[pl.ds(e, 1), :] = jnp.sum(picked, axis=0, keepdims=True)
            geo = partials[e].astype(F32)
            own_geo[pl.ds(e, 1), :] = jnp.concatenate([geo[0:1], geo[1:2]], axis=1)
            own_geo[pl.ds(events + e, 1), :] = jnp.concatenate([geo[2:3], geo[3:4]], axis=1)

    gathered = jnp.dot(hot_turned[...], slots_out[...], preferred_element_type=F32)
    low = low_half((cands, 128))
    gathered = jnp.where(low, gathered, -gathered)
    totals = jnp.concatenate([gathered[:events] + own[...], gathered[events:]], axis=0)
    turned = pltpu.roll(totals, 64, 1)
    weights = jnp.where(low, totals, turned)
    moves = jnp.where(low, turned, totals)
    ends = [t[...] for t in tails]
    first = jnp.concatenate([own_geo[:events].astype(BF16)] + [t[:GROUP_ROWS] for t in ends], axis=0)
    second = jnp.concatenate([own_geo[events:].astype(BF16)] + [t[GROUP_ROWS:] for t in ends], axis=0)
    geo_out[:, :128] = first
    geo_out[:, 128:] = second
    blocks = [first.astype(F32), second.astype(F32)]
    singles = []
    for block in blocks:
        other = pltpu.roll(block, 64, 1)
        singles += [jnp.where(low, block, other), jnp.where(low, other, block)]
    half_row = lax.broadcasted_iota(jnp.int32, (8, 128), 0)
    half_lane = lax.broadcasted_iota(jnp.int32, (8, 128), 1) // 64
    picker = jnp.where(half_row == half_lane, 1.0, 0.0).astype(F32)

    def halves(values):
        return lax.dot_general(
            picker, values, (((1,), (1,)), ((), ())), precision=lax.Precision.HIGHEST, preferred_element_type=F32
        )[:2]

    rights = [halves(moves * blocks[0]), halves(moves * blocks[1])]
    for i in range(4):
        scaled = weights * singles[i]
        rows = [halves(scaled * blocks[0]), halves(scaled * blocks[1]), rights[i // 2][i % 2 : i % 2 + 1]]
        share = jnp.concatenate(rows + [jnp.zeros((3, 128), F32)], axis=0)
        for q in range(terms_out.shape[1]):
            terms_out[i, q] = share


def blocks_kernel(events, place, hot, slots, geo, partials, *refs):
    outs, turned = refs[:-1], refs[-1]
    turned[...] = jnp.zeros_like(turned)
    low = low_half((SLOT_ROWS, 128))
    column = lax.broadcasted_iota(jnp.int32, (16, 128), 0) % 4
    block = lax.broadcasted_iota(jnp.int32, (16, 128), 1) // 64

    @pl.loop(0, events // UNROLL)
    def _(step):
        for u in range(UNROLL):
            e = step * UNROLL + u
            rows = pl.ds(pl.multiple_of(e * SLOT_ROWS, SLOT_ROWS), SLOT_ROWS)
            partner = jnp.dot(hot[rows, :], geo[...], preferred_element_type=F32)
            pair = slots[rows, :].astype(F32)
            weights = jnp.where(low, pair, pltpu.roll(pair, 64, 1))
            weighted = jnp.concatenate([weights * partner[:, :128], weights * partner[:, 128:]], axis=1).astype(BF16)
            own = partials[e].astype(F32)
            own = jnp.concatenate([own, own], axis=1)
            own = jnp.concatenate([jnp.broadcast_to(-own[i : i + 1], (4, 128)) for i in range(4)], axis=0)
            left = [jnp.where(column == block, own, 0.0), jnp.where(column == block + 2, own, 0.0)]
            left = jnp.concatenate(left, axis=1).astype(BF16)
            entry = lax.dot_general(left, weighted, (((1,), (1,)), ((), ())), preferred_element_type=F32)
            turned[pl.ds(e, 16, stride=events), 0:SLOT_ROWS] = entry

    for d, out in enumerate(outs):
        share = lax.rem(place[0] + d, 4)
        rows = pl.ds(pl.multiple_of(share * 4 * events, 128), 4 * events)
        out[...] = turned[rows, :].T[: out.shape[0]]


def total_kernel(groups, events, slots, clusters, own, one, two, three, received, owners, normal, right):
    parts = []
    for g in range(groups + 1):
        part = received[clusters[g]]
        for t in range(1, 4):
            part = part + received[t * (received.shape[0] // 4) + clusters[g]]
        parts.append(part)
    spread = jnp.dot(
        jnp.concatenate(parts, axis=1), owners[...], precision=lax.Precision.HIGHEST, preferred_element_type=F32
    )
    block = lax.broadcasted_iota(jnp.int32, (1, 128), 1) // events
    diagonal = jnp.zeros((1, 128), F32)
    for j in range(4):
        diagonal = jnp.where(block == j, spread[j : j + 1], diagonal)
    right[...] = spread[4:5, :events]
    total = pltpu.roll((own[...] + one[...]) + (two[...] + three[...]), 1, 0)
    top = lax.broadcasted_iota(jnp.int32, total.shape, 0) == 0
    total = jnp.where(top, diagonal, total)
    turned = total.T
    for j in range(4):
        normal[j] = turned[j * events : (j + 1) * events, : slots + 1]


def vmem(n):
    return [pl.BlockSpec(memory_space=pltpu.VMEM)] * n


def call(kernel, outs, inputs, scratch=(), specs=None, micros=1.0):
    shapes = [jax.ShapeDtypeStruct(s, t) for s, t in outs]
    return pl.pallas_call(
        kernel,
        out_shape=shapes,
        in_specs=specs if specs is not None else vmem(len(inputs)),
        out_specs=vmem(len(outs)),
        scratch_shapes=list(scratch),
        compiler_params=pltpu.CompilerParams(vmem_limit_bytes=VMEM_LIMIT),
        cost_estimate=pl.CostEstimate(flops=int(micros * 1e9), bytes_accessed=1024, transcendentals=0),
    )(*inputs)


def on_device(spectra, partials, pair_list, station_mask, exports):
    events, stations, two_freq = spectra.shape
    freq = two_freq // 2
    groups, cap = exports.shape
    half_span = groups // 2
    slots = pair_list.shape[1]
    sta_groups = lax.axis_size("sta")
    scale = 1.0 / (stations * sta_groups)
    offsets = [h - half_span + (1 if h >= half_span else 0) for h in range(groups)]
    cands = events + groups * GROUP_ROWS
    half = cap // 2
    table = moment_table(freq)
    smem = pl.BlockSpec(memory_space=pltpu.SMEM)
    clusters = lax.axis_size("clu")

    out_rows = cap * stations + 2 * GROUP_ROWS
    outgoing = call(
        functools.partial(outgoing_kernel, cap),
        [((out_rows, 128), BF16)] * groups,
        (exports, spectra, partials),
        scratch=[pltpu.VMEM((2 * GROUP_ROWS, 128), F32)],
        specs=[smem] + vmem(2),
        micros=2.0,
    )
    order = sorted(range(groups), key=lambda h: abs(offsets[h]))
    got = [None] * groups
    for h in order:
        got[h] = shifted(outgoing[h], "clu", offsets[h])

    codes = [e * PAIR_BASE + j for e in range(events) for j in range(e // 2, events // 2)]
    items = -(-len(codes) // (2 * BATCH)) * 2 * BATCH
    codes = codes + [0] * (items + 2 * BATCH - len(codes))
    natural, got[order[0]] = lax.optimization_barrier((spectra, got[order[0]]))
    local, dup, square, energy = call(
        functools.partial(local_kernel, freq, events, scale, items),
        [
            ((events * events, 128), F32),
            ((events, 128, 128), F32),
            ((events, freq, 128), F32),
            ((events, 128), F32),
        ],
        (jnp.asarray(codes, jnp.int32), natural.reshape(events // 2, 2 * stations, two_freq), table),
        scratch=weight_scratch(events // 2, freq),
        specs=[smem] + vmem(2),
        micros=8.0,
    )

    far = jnp.maximum(pair_list - events, 0)
    named = jnp.where(pair_list < events, -1, (far // cap) * half + (far % cap) // 2)
    wanted = jnp.any(named[:, :, None] == jnp.arange(groups * half, dtype=jnp.int32)[None, None, :], axis=1)
    wanted = wanted.reshape(events, groups, half).transpose(1, 0, 2).reshape(groups, events * half)
    item = np.arange(events * half)
    before = jnp.asarray(item[:, None] < item[None, :], BF16)
    rank = jnp.dot(wanted.astype(BF16), before, preferred_element_type=F32).astype(jnp.int32)
    item_code = jnp.asarray((item // half) * PAIR_BASE + item % half, jnp.int32)
    spot = jnp.where(wanted, rank, -1)
    longest = events * half + 3 * BATCH
    lists = jnp.sum(
        jnp.where(spot[:, None, :] == jnp.arange(longest, dtype=jnp.int32)[None, :, None], item_code[None, None, :], 0),
        axis=2,
    ).astype(jnp.int32)
    counts = jnp.sum(wanted.astype(jnp.int32), axis=1)

    column = jnp.where(pair_list < events, pair_list, events + GROUP_ROWS * (far // cap) + far % cap)
    column = jnp.pad(column, ((0, 0), (0, SLOT_ROWS - slots)), constant_values=-1).reshape(-1)
    cand_ids = jnp.arange(cands, dtype=jnp.int32)
    hot = (column[:, None] == cand_ids[None, :]).astype(BF16)
    hot_turned = (cand_ids[:, None] == column[None, :]).astype(BF16)
    mask = station_mask.transpose(1, 0, 2).reshape(slots * events, stations)
    owner_rows = [jnp.asarray(np.where(np.arange(cands) < events, np.arange(cands), -1), jnp.int32)]
    for h in range(groups):
        start = events + GROUP_ROWS * h
        owner_rows.append(jnp.pad(exports[h], (start, cands - start - cap), constant_values=-1))
    owners = jnp.concatenate(owner_rows)[:, None] == (jnp.arange(128, dtype=jnp.int32) % events)[None, :]
    owners = owners.astype(F32)

    tables, tails = [None] * groups, [None] * groups
    for h in order:
        tables[h], tails[h] = call(
            functools.partial(import_kernel, h, freq, events, cap, scale),
            [((events * GROUP_ROWS, 128), F32), ((2 * GROUP_ROWS, 128), BF16)],
            (lists, counts, got[h], dup, square, energy, table),
            scratch=weight_scratch(half, freq),
            specs=[smem] * 2 + vmem(5),
            micros=3.0,
        )

    weights, terms, geo = call(
        functools.partial(sums_kernel, groups, events, slots),
        [((events * SLOT_ROWS, 128), BF16), ((4, clusters, 8, 128), F32), ((cands, 256), BF16)],
        (hot, hot_turned, mask, partials, local, *tables, *tails),
        scratch=[pltpu.VMEM((events, 128), F32), pltpu.VMEM((2 * events, 128), F32)],
        micros=2.0,
    )
    terms = lax.all_to_all(
        terms.reshape(4 * clusters, 8, 128), ("sta", "clu"), split_axis=0, concat_axis=0, tiled=True
    )
    message_rows = -(-(slots + 1) // 8) * 8
    place = lax.axis_index("sta").astype(jnp.int32).reshape(1)
    shares = call(
        functools.partial(blocks_kernel, events),
        [((message_rows, 128), F32)] * 4,
        (place, hot, weights, geo, partials),
        scratch=[pltpu.VMEM((16 * events, 128), F32)],
        specs=[smem] + vmem(4),
        micros=3.0,
    )
    shares = [shares[0]] + [shifted(shares[d], "sta", d) for d in range(1, 4)]
    sources = (lax.axis_index("clu") + jnp.asarray([0] + offsets, jnp.int32)) % clusters
    normal, right = call(
        functools.partial(total_kernel, groups, events, slots),
        [((4, events, slots + 1), F32), ((1, events), F32)],
        (sources.astype(jnp.int32), *shares, terms, owners),
        specs=[smem] + vmem(6),
    )
    return (normal.transpose(0, 2, 1), right)


def solution(mesh):
    return jax.shard_map(
        on_device,
        mesh=mesh,
        in_specs=(
            P("clu", "sta", None),
            P("clu", None, "sta"),
            P("clu", None),
            P("clu", None, "sta"),
            P("clu", None),
        ),
        out_specs=(P("sta", None, "clu"), P("sta", "clu")),
        check_vma=False,
    )
```

```python
import functools
import math

import jax
import jax.numpy as jnp
import numpy as np
from jax import lax
from jax.experimental import pallas as pl
from jax.experimental.pallas import tpu as pltpu
from jax.sharding import PartitionSpec as P

F32 = jnp.float32
BF16 = jnp.bfloat16
VMEM_LIMIT = 24 * 1024 * 1024
SLOT_ROWS = 64
GROUP_ROWS = 16
BATCH = 8
WIDE = 4
PAIR_BASE = 64
UNROLL = 4


def shifted(block, axis, distance):
    devices = range(lax.axis_size(axis))
    route = [((i - distance) % len(devices), i) for i in devices]
    return lax.ppermute(block, axis, route)


def moment_table(freq_count):
    f = np.arange(freq_count)

    def edge(k):
        out = np.zeros(k.shape)
        live = (k % (2 * freq_count)) != 0
        sign = 1.0 - 2.0 * (k[live] % 2)
        out[live] = -freq_count * sign / np.tan(np.pi * k[live] / (2 * freq_count))
        return out

    table = np.zeros((freq_count + 16, freq_count), np.float32)
    table[:freq_count] = -(edge(f[:, None] + f[None, :]) + edge(f[None, :] - f[:, None]))
    table[freq_count] = (1.0 - 2.0 * (f % 2)) * f * math.pi / freq_count
    return jnp.asarray(table, F32).astype(BF16)


def low_half(shape):
    return lax.broadcasted_iota(jnp.int32, shape, len(shape) - 1) < shape[-1] // 2


def outgoing_kernel(cap, send_group, exports_ref, spec_ref, geo_ref, *refs):
    outs, rows = refs[:-1], refs[-1]
    stations = spec_ref.shape[1]
    body = cap * stations
    rows[...] = jnp.zeros_like(rows)
    for g, out in enumerate(outs):
        h = send_group(g, lax.axis_index("clu"))
        for c in range(cap):
            event = exports_ref[h, c]
            out[c * stations : (c + 1) * stations, :] = spec_ref[event]
            place = c
            geo = geo_ref[event].astype(F32)
            rows[place : place + 1, :] = jnp.concatenate([geo[0:1], geo[1:2]], axis=1)
            place += GROUP_ROWS
            rows[place : place + 1, :] = jnp.concatenate([geo[2:3], geo[3:4]], axis=1)
        out[body : body + 2 * GROUP_ROWS, :] = rows[...].astype(BF16)


def fold(x):
    rows = x.shape[0] // 8
    total = x[0:8]
    for r in range(1, rows):
        total = total + x[8 * r : 8 * r + 8]
    return total


def prepare(natural, bp, bb, eb, pairs, freq):
    for j in range(pairs):
        turned = natural(j).astype(F32).T
        bp[j] = turned
        re, im = turned[:freq], turned[freq:]
        square = re * re + im * im
        bb[j] = square
        eb[j : j + 1, :] = jnp.sum(square, axis=0, keepdims=True)


def listed_pairs(ids, batches, da, sq, ea, bp, bb, eb, table, work, store, freq, scale):
    xs, reals, rm, rs, rt, rb, rz, re = work
    lead = lax.broadcasted_iota(jnp.int32, (8, 1), 0) == 0
    step = lax.broadcasted_iota(jnp.int32, (8, 1), 0).astype(F32)
    low = low_half((8, 128))
    unit = (math.pi / freq) ** 2

    def split(t, d):
        code = ids[t * (BATCH // 2) + d]
        return code >> 12, ((code >> 6) & 63, code & 63)

    def cross_stage(t, slot):
        for d in range(BATCH // 2):
            j, duo = split(t, d)
            squares, sums = [[], []], [None, None]
            for v in range(0, freq, 16):
                br, bi = bp[j, v : v + 16, :], bp[j, freq + v : freq + v + 16, :]
                b2 = bb[j, v : v + 16, :]
                for i, e in enumerate(duo):
                    ar, ai = da[e, v : v + 16, :], da[e, freq + v : freq + v + 16, :]
                    cr = ar * br + ai * bi
                    ci = ai * br - ar * bi
                    both = sq[e, v : v + 16, :] * b2
                    u = 2 * d + i
                    lanes = slice(u * 128, (u + 1) * 128)
                    xs[slot, v : v + 16, lanes] = ci.astype(BF16)
                    reals[slot, v : v + 16, lanes] = cr.astype(BF16)
                    squares[i] += [both[:8], both[8:]]
                    part = cr[:8] + cr[8:]
                    sums[i] = part if v == 0 else sums[i] + part
                    if v == 0:
                        edge = cr[:8] * cr[:8] - ci[:8] * ci[:8]
                        rs[slot, u * 8 : u * 8 + 8, :] = jnp.where(lead, edge, 0.0)
            for i, e in enumerate(duo):
                u = 2 * d + i
                rows = slice(u * 8, u * 8 + 8)
                zero, one, two = squares[i][-1], squares[i][-1], squares[i][-1]
                for v in range(freq // 8 - 2, 0, -1):
                    zero = zero + squares[i][v]
                    one = one + zero
                    two = two + one
                zero = zero + squares[i][0]
                rs[slot, rows, :] += zero
                rb[slot, rows, :] = unit * (64.0 * (2.0 * two - one) + step * (16.0 * one + step * zero))
                rt[slot, rows, :] = sums[i]
                re[slot, u : u + 1, :] = ea[pl.ds(e, 1), :] * eb[pl.ds(j, 1), :]

    def moment_stage(slot):
        for start in range(0, BATCH, WIDE):
            lanes = slice(start * 128, (start + WIDE) * 128)
            z = jnp.dot(table[...], xs[slot, :, lanes], preferred_element_type=F32)
            for i in range(WIDE):
                part = z[:, i * 128 : (i + 1) * 128]
                real = reals[slot, :, (start + i) * 128 : (start + i + 1) * 128].astype(F32)
                rows = slice((start + i) * 8, (start + i + 1) * 8)
                rm[slot, rows, :] = fold(real * part[:freq])
                rz[slot, rows, :] = part[freq : freq + 8]

    def finish_stage(t, slot):
        def pick(ref, k):
            return ref[slot, pl.ds(k, 8, stride=8), :]

        moment, total, alternate, bend = pick(rm, 0), pick(rs, 0), pick(rt, 0), pick(rb, 0)
        for k in range(1, 8):
            moment = moment + pick(rm, k)
            total = total + pick(rs, k)
            bend = bend + pick(rb, k)
            alternate = alternate + pick(rt, k) if k % 2 == 0 else alternate - pick(rt, k)
        tilt = pick(rz, 0)
        inverse = 1.0 / (re[slot] + 1e-06)
        power = (freq * total - alternate * alternate) * inverse
        rough = (freq * bend - tilt * tilt) * inverse
        weight = power / (power + 0.125 * rough + 1e-06) * scale
        moved = weight * (moment * inverse / (power + 1e-06))
        even = jnp.where(low, weight, pltpu.roll(moved, 64, 1))
        odd = jnp.where(low, pltpu.roll(weight, 64, 1), moved)
        for d in range(BATCH // 2):
            j, duo = split(t, d)
            for i, e in enumerate(duo):
                u = 2 * d + i
                store(e, j, even[u : u + 1], odd[u : u + 1])

    cross_stage(0, 0)

    @pl.loop(0, (batches + 1) // 2)
    def _(i):
        cross_stage(2 * i + 1, 1)
        moment_stage(0)
        finish_stage(2 * i, 0)
        cross_stage(2 * i + 2, 0)
        moment_stage(1)
        finish_stage(2 * i + 1, 1)


def local_kernel(freq, events, scale, batches, ids, spec_ref, table, out, da, sq, ea, bp, bb, eb, *work):
    pairs = events // 2
    prepare(lambda j: spec_ref[j], bp, bb, eb, pairs, freq)
    low = low_half((128, 128))
    for j in range(pairs):
        both = bp[j]
        other = pltpu.roll(both, 64, 1)
        da[2 * j] = jnp.where(low, both, other)
        da[2 * j + 1] = jnp.where(low, other, both)
        both = bb[j]
        other = pltpu.roll(both, 64, 1)
        sq[2 * j] = jnp.where(low[:freq], both, other)
        sq[2 * j + 1] = jnp.where(low[:freq], other, both)
    energy = eb[...]
    other = pltpu.roll(energy, 64, 1)
    low = low_half(energy.shape)
    ea[pl.ds(0, pairs, stride=2), :] = jnp.where(low, energy, other)
    ea[pl.ds(1, pairs, stride=2), :] = jnp.where(low, other, energy)
    row = low_half((1, 128))

    def store(e, j, even, odd):
        out[pl.ds(e * events + 2 * j, 1), :] = even
        out[pl.ds(e * events + 2 * j + 1, 1), :] = odd
        out[pl.ds(2 * j * events + e, 1), :] = jnp.where(row, even, -even)
        out[pl.ds((2 * j + 1) * events + e, 1), :] = jnp.where(row, odd, -odd)

    listed_pairs(ids, batches, da, sq, ea, bp, bb, eb, table, work, store, freq, scale)


def import_kernel(group, freq, events, cap, scale, ids, counts, got_ref, da, sq, ea, table, out, tail, bp, bb, eb, *work):
    pairs = cap // 2
    prepare(lambda j: got_ref[j * 128 : (j + 1) * 128, :], bp, bb, eb, pairs, freq)
    out[...] = jnp.zeros_like(out)
    tail[...] = got_ref[cap // 2 * 128 :, :]

    def store(e, j, even, odd):
        out[pl.ds(e * GROUP_ROWS + 2 * j, 1), :] = even
        out[pl.ds(e * GROUP_ROWS + 2 * j + 1, 1), :] = odd

    batches = (counts[group] + BATCH // 2 - 1) // (BATCH // 2)
    listed_pairs(ids.at[group], batches, da, sq, ea, bp, bb, eb, table, work, store, freq, scale)


def weight_scratch(pairs, freq):
    return (
        [
            pltpu.VMEM((pairs, 2 * freq, 128), F32),
            pltpu.VMEM((pairs, freq, 128), F32),
            pltpu.VMEM((-(-pairs // 8) * 8, 128), F32),
            pltpu.VMEM((2, freq, BATCH * 128), BF16),
            pltpu.VMEM((2, freq, BATCH * 128), BF16),
        ]
        + [pltpu.VMEM((2, BATCH * 8, 128), F32)] * 5
        + [pltpu.VMEM((2, BATCH, 128), F32)]
    )


def sums_kernel(groups, events, slots, hot, hot_turned, mask, partials, *refs):
    tables, tails = refs[: groups + 1], refs[groups + 1 : 2 * groups + 1]
    slots_out, terms_out, geo_out, own, own_geo = refs[2 * groups + 1 :]
    cands = hot.shape[1]
    rest = jnp.zeros((SLOT_ROWS - slots, 128), F32)

    @pl.loop(0, events // UNROLL)
    def _(step):
        for u in range(UNROLL):
            e = step * UNROLL + u
            parts = [tables[0][pl.ds(pl.multiple_of(e * events, 8), events), :]]
            for t in tables[1:]:
                parts.append(t[pl.ds(pl.multiple_of(e * GROUP_ROWS, 8), GROUP_ROWS), :])
            every = jnp.concatenate(parts, axis=0).astype(BF16)
            rows = pl.ds(pl.multiple_of(e * SLOT_ROWS, SLOT_ROWS), SLOT_ROWS)
            live = mask[pl.ds(e, slots, stride=events), :].astype(F32)
            live = jnp.concatenate([jnp.concatenate([live, live], axis=1), rest], axis=0)
            picked = jnp.dot(hot[rows, :], every, preferred_element_type=F32) * live
            slots_out[rows, :] = picked.astype(BF16)
            own[pl.ds(e, 1), :] = jnp.sum(picked, axis=0, keepdims=True)
            geo = partials[e].astype(F32)
            own_geo[pl.ds(e, 1), :] = jnp.concatenate([geo[0:1], geo[1:2]], axis=1)
            own_geo[pl.ds(events + e, 1), :] = jnp.concatenate([geo[2:3], geo[3:4]], axis=1)

    gathered = jnp.dot(hot_turned[...], slots_out[...], preferred_element_type=F32)
    low = low_half((cands, 128))
    gathered = jnp.where(low, gathered, -gathered)
    totals = jnp.concatenate([gathered[:events] + own[...], gathered[events:]], axis=0)
    turned = pltpu.roll(totals, 64, 1)
    weights = jnp.where(low, totals, turned)
    moves = jnp.where(low, turned, totals)
    ends = [t[...] for t in tails]
    first = jnp.concatenate([own_geo[:events].astype(BF16)] + [t[:GROUP_ROWS] for t in ends], axis=0)
    second = jnp.concatenate([own_geo[events:].astype(BF16)] + [t[GROUP_ROWS:] for t in ends], axis=0)
    geo_out[:, :128] = first
    geo_out[:, 128:] = second
    blocks = [first.astype(F32), second.astype(F32)]
    singles = []
    for block in blocks:
        other = pltpu.roll(block, 64, 1)
        singles += [jnp.where(low, block, other), jnp.where(low, other, block)]
    half_row = lax.broadcasted_iota(jnp.int32, (8, 128), 0)
    half_lane = lax.broadcasted_iota(jnp.int32, (8, 128), 1) // 64
    picker = jnp.where(half_row == half_lane, 1.0, 0.0).astype(F32)

    def halves(values):
        return lax.dot_general(
            picker, values, (((1,), (1,)), ((), ())), precision=lax.Precision.HIGHEST, preferred_element_type=F32
        )[:2]

    rights = [halves(moves * blocks[0]), halves(moves * blocks[1])]
    for i in range(4):
        scaled = weights * singles[i]
        rows = [halves(scaled * blocks[0]), halves(scaled * blocks[1]), rights[i // 2][i % 2 : i % 2 + 1]]
        share = jnp.concatenate(rows + [jnp.zeros((3, 128), F32)], axis=0)
        for q in range(terms_out.shape[1]):
            terms_out[i, q] = share


def blocks_kernel(events, place, hot, slots, geo, partials, *refs):
    outs, turned = refs[:-1], refs[-1]
    turned[...] = jnp.zeros_like(turned)
    low = low_half((SLOT_ROWS, 128))
    column = lax.broadcasted_iota(jnp.int32, (16, 128), 0) % 4
    block = lax.broadcasted_iota(jnp.int32, (16, 128), 1) // 64

    @pl.loop(0, events // UNROLL)
    def _(step):
        for u in range(UNROLL):
            e = step * UNROLL + u
            rows = pl.ds(pl.multiple_of(e * SLOT_ROWS, SLOT_ROWS), SLOT_ROWS)
            partner = jnp.dot(hot[rows, :], geo[...], preferred_element_type=F32)
            pair = slots[rows, :].astype(F32)
            weights = jnp.where(low, pair, pltpu.roll(pair, 64, 1))
            weighted = jnp.concatenate([weights * partner[:, :128], weights * partner[:, 128:]], axis=1).astype(BF16)
            own = partials[e].astype(F32)
            own = jnp.concatenate([own, own], axis=1)
            own = jnp.concatenate([jnp.broadcast_to(-own[i : i + 1], (4, 128)) for i in range(4)], axis=0)
            left = [jnp.where(column == block, own, 0.0), jnp.where(column == block + 2, own, 0.0)]
            left = jnp.concatenate(left, axis=1).astype(BF16)
            entry = lax.dot_general(left, weighted, (((1,), (1,)), ((), ())), preferred_element_type=F32)
            turned[pl.ds(e, 16, stride=events), 0:SLOT_ROWS] = entry

    for d, out in enumerate(outs):
        share = lax.rem(place[0] + d, 4)
        rows = pl.ds(pl.multiple_of(share * 4 * events, 128), 4 * events)
        out[...] = turned[rows, :].T[: out.shape[0]]


def total_kernel(groups, events, slots, clusters, own, one, two, three, received, owners, normal, right):
    parts = []
    for g in range(groups + 1):
        part = received[clusters[g]]
        for t in range(1, 4):
            part = part + received[t * (received.shape[0] // 4) + clusters[g]]
        parts.append(part)
    spread = jnp.dot(
        jnp.concatenate(parts, axis=1), owners[...], precision=lax.Precision.HIGHEST, preferred_element_type=F32
    )
    block = lax.broadcasted_iota(jnp.int32, (1, 128), 1) // events
    diagonal = jnp.zeros((1, 128), F32)
    for j in range(4):
        diagonal = jnp.where(block == j, spread[j : j + 1], diagonal)
    right[...] = spread[4:5, :events]
    total = pltpu.roll((own[...] + one[...]) + (two[...] + three[...]), 1, 0)
    top = lax.broadcasted_iota(jnp.int32, total.shape, 0) == 0
    total = jnp.where(top, diagonal, total)
    turned = total.T
    for j in range(4):
        normal[j] = turned[j * events : (j + 1) * events, : slots + 1]


def vmem(n):
    return [pl.BlockSpec(memory_space=pltpu.VMEM)] * n


def call(kernel, outs, inputs, scratch=(), specs=None, micros=1.0, limit=VMEM_LIMIT):
    shapes = [jax.ShapeDtypeStruct(s, t) for s, t in outs]
    return pl.pallas_call(
        kernel,
        out_shape=shapes,
        in_specs=specs if specs is not None else vmem(len(inputs)),
        out_specs=vmem(len(outs)),
        scratch_shapes=list(scratch),
        compiler_params=pltpu.CompilerParams(vmem_limit_bytes=limit),
        cost_estimate=pl.CostEstimate(flops=int(micros * 1e9), bytes_accessed=1024, transcendentals=0),
    )(*inputs)


def on_device(spectra, partials, pair_list, station_mask, exports):
    events, stations, two_freq = spectra.shape
    freq = two_freq // 2
    groups, cap = exports.shape
    half_span = groups // 2
    slots = pair_list.shape[1]
    sta_groups = lax.axis_size("sta")
    scale = 1.0 / (stations * sta_groups)
    offsets = [h - half_span + (1 if h >= half_span else 0) for h in range(groups)]
    cands = events + groups * GROUP_ROWS
    half = cap // 2
    table = moment_table(freq)
    smem = pl.BlockSpec(memory_space=pltpu.SMEM)
    clusters = lax.axis_size("clu")

    paired = clusters == groups + 2 and clusters & (clusters - 1) == 0
    if paired:
        masks = [m for m in range(1, clusters) if m != clusters // 2]
        routes = [[(i, i ^ m) for i in range(clusters)] for m in masks]
    else:
        order = sorted(range(groups), key=lambda h: abs(offsets[h]))
        routes = [[(i, (i + offsets[h]) % clusters) for i in range(clusters)] for h in order]

    def group_of(offset):
        offset = offset & (clusters - 1)
        return jnp.where(offset < clusters // 2, offset + half_span - 1, offset - clusters + half_span)

    def send_group(g, p):
        return group_of((p ^ masks[g]) - p) if paired else order[g]

    def receive_group(g, p):
        return group_of(p - (p ^ masks[g])) if paired else order[g]

    def receiver(g, p):
        return p ^ masks[g] if paired else (p + offsets[order[g]]) % clusters

    out_rows = cap * stations + 2 * GROUP_ROWS
    outgoing = call(
        functools.partial(outgoing_kernel, cap, send_group),
        [((out_rows, 128), BF16)] * groups,
        (exports, spectra, partials),
        scratch=[pltpu.VMEM((2 * GROUP_ROWS, 128), F32)],
        specs=[smem] + vmem(2),
        micros=2.0,
        limit=60 * 1024 * 1024,
    )
    got = [None] * groups
    for g in [0] + list(range(groups - 1, 0, -1)):
        got[g] = lax.ppermute(outgoing[g], "clu", routes[g])
    me = lax.axis_index("clu").astype(jnp.int32)
    sent = jnp.stack([jnp.asarray(send_group(g, me), jnp.int32) for g in range(groups)])
    came = jnp.stack([jnp.asarray(receive_group(g, me), jnp.int32) for g in range(groups)])

    duos = [j << 12 | e << 6 | e + 1 for j in range(events // 2) for e in range(0, 2 * j + 2, 2)]
    batches = -(-len(duos) // BATCH) * 2
    duos = duos + [1] * ((batches + 2) * (BATCH // 2) - len(duos))
    natural, got[0] = lax.optimization_barrier((spectra, got[0]))
    local, dup, square, energy = call(
        functools.partial(local_kernel, freq, events, scale, batches),
        [
            ((events * events, 128), F32),
            ((events, 128, 128), F32),
            ((events, freq, 128), F32),
            ((events, 128), F32),
        ],
        (jnp.asarray(duos, jnp.int32), natural.reshape(events // 2, 2 * stations, two_freq), table),
        scratch=weight_scratch(events // 2, freq),
        specs=[smem] + vmem(2),
        micros=8.0,
    )

    far = jnp.maximum(pair_list - events, 0)
    far_group = far // cap
    arrival = jnp.sum(jnp.where(far_group[:, :, None] == came[None, None, :], jnp.arange(groups, dtype=jnp.int32), 0), axis=2)
    entry = far % cap
    named = jnp.where(pair_list < events, -1, arrival * half + entry // 2)
    wanted = jnp.any(named[:, :, None] == jnp.arange(groups * half, dtype=jnp.int32)[None, None, :], axis=1)
    wanted = wanted.astype(F32).T.reshape(groups, half, events)
    ranks = np.arange(events)
    rank = jnp.einsum("gje,ef->gjf", wanted, jnp.asarray(ranks[:, None] < ranks[None, :], F32))
    rounded = jnp.ceil(jnp.sum(wanted, axis=2) * 0.5)
    ranks = np.arange(half)
    start = jnp.sum(rounded[:, :, None] * jnp.asarray(ranks[:, None] < ranks[None, :], F32)[None], axis=1)
    rank = rank.astype(jnp.int32)
    spot = jnp.where(wanted > 0, start.astype(jnp.int32)[:, :, None] + (rank >> 1), -1).reshape(groups, half * events)
    event_ids = jnp.arange(events, dtype=jnp.int32)[None, None, :]
    pair_ids = jnp.arange(half, dtype=jnp.int32)[None, :, None]
    code = jnp.where(rank & 1 == 0, (pair_ids << 12) + (event_ids << 6), event_ids).reshape(groups, half * events)
    longest = half * events // 2 + 3 * BATCH // 2
    lists = jnp.sum(
        jnp.where(spot[:, None, :] == jnp.arange(longest, dtype=jnp.int32)[None, :, None], code[:, None, :], 0), axis=2
    )
    counts = jnp.sum(rounded, axis=1).astype(jnp.int32)

    column = jnp.where(pair_list < events, pair_list, events + GROUP_ROWS * arrival + entry)
    column = jnp.pad(column, ((0, 0), (0, SLOT_ROWS - slots)), constant_values=-1).reshape(-1)
    cand_ids = jnp.arange(cands, dtype=jnp.int32)
    hot = (column[:, None] == cand_ids[None, :]).astype(BF16)
    hot_turned = (cand_ids[:, None] == column[None, :]).astype(BF16)
    mask = station_mask.transpose(1, 0, 2).reshape(slots * events, stations)
    owner_rows = [jnp.asarray(np.where(np.arange(cands) < events, np.arange(cands), -1), jnp.int32)]
    hot_sent = sent[:, None] == jnp.arange(groups, dtype=jnp.int32)[None, :]
    rows_sent = jnp.sum(jnp.where(hot_sent[:, :, None], exports[None], 0), axis=1)
    for g in range(groups):
        start = events + GROUP_ROWS * g
        owner_rows.append(jnp.pad(rows_sent[g], (start, cands - start - cap), constant_values=-1))
    owners = jnp.concatenate(owner_rows)[:, None] == (jnp.arange(128, dtype=jnp.int32) % events)[None, :]
    owners = owners.astype(F32)

    tables, tails = [None] * groups, [None] * groups
    for h in range(groups):
        tables[h], tails[h] = call(
            functools.partial(import_kernel, h, freq, events, cap, scale),
            [((events * GROUP_ROWS, 128), F32), ((2 * GROUP_ROWS, 128), BF16)],
            (lists, counts, got[h], dup, square, energy, table),
            scratch=weight_scratch(half, freq),
            specs=[smem] * 2 + vmem(5),
            micros=3.0,
        )

    weights, terms, geo = call(
        functools.partial(sums_kernel, groups, events, slots),
        [((events * SLOT_ROWS, 128), BF16), ((4, clusters, 8, 128), F32), ((cands, 256), BF16)],
        (hot, hot_turned, mask, partials, local, *tables, *tails),
        scratch=[pltpu.VMEM((events, 128), F32), pltpu.VMEM((2 * events, 128), F32)],
        micros=2.0,
    )
    terms = lax.all_to_all(
        terms.reshape(4 * clusters, 8, 128), ("sta", "clu"), split_axis=0, concat_axis=0, tiled=True
    )
    message_rows = -(-(slots + 1) // 8) * 8
    place = lax.axis_index("sta").astype(jnp.int32).reshape(1)
    shares = call(
        functools.partial(blocks_kernel, events),
        [((message_rows, 128), F32)] * 4,
        (place, hot, weights, geo, partials),
        scratch=[pltpu.VMEM((16 * events, 128), F32)],
        specs=[smem] + vmem(4),
        micros=3.0,
    )
    shares = [shares[0]] + [shifted(shares[d], "sta", d) for d in range(1, 4)]
    sources = jnp.stack([me] + [jnp.asarray(receiver(g, me), jnp.int32) for g in range(groups)])
    normal, right = call(
        functools.partial(total_kernel, groups, events, slots),
        [((4, events, slots + 1), F32), ((1, events), F32)],
        (sources, *shares, terms, owners),
        specs=[smem] + vmem(6),
    )
    return (normal.transpose(0, 2, 1), right)


def solution(mesh):
    return jax.shard_map(
        on_device,
        mesh=mesh,
        in_specs=(
            P("clu", "sta", None),
            P("clu", None, "sta"),
            P("clu", None),
            P("clu", None, "sta"),
            P("clu", None),
        ),
        out_specs=(P("sta", None, "clu"), P("sta", "clu")),
        check_vma=False,
    )
```

```python
import functools
import math

import jax
import jax.numpy as jnp
import numpy as np
from jax import lax
from jax.experimental import pallas as pl
from jax.experimental.pallas import tpu as pltpu
from jax.sharding import PartitionSpec as P

F32 = jnp.float32
BF16 = jnp.bfloat16
VMEM_LIMIT = 24 * 1024 * 1024
SLOT_ROWS = 64
GROUP_ROWS = 16
BATCH = 8
WIDE = 4
UNROLL = 8
STAGES = 2


def moment_table(freq_count):
    f = np.arange(freq_count)

    def edge(k):
        out = np.zeros(k.shape)
        live = (k % (2 * freq_count)) != 0
        sign = 1.0 - 2.0 * (k[live] % 2)
        out[live] = -freq_count * sign / np.tan(np.pi * k[live] / (2 * freq_count))
        return out

    table = np.zeros((freq_count + 16, freq_count), np.float32)
    table[:freq_count] = -(edge(f[:, None] + f[None, :]) + edge(f[None, :] - f[:, None]))
    table[freq_count] = (1.0 - 2.0 * (f % 2)) * f * math.pi / freq_count
    return jnp.asarray(table, F32).astype(BF16)


def low_half(shape):
    return lax.broadcasted_iota(jnp.int32, shape, len(shape) - 1) < shape[-1] // 2


def outgoing_kernel(cap, send_group, exports_ref, spec_ref, geo_ref, *refs):
    outs, rows = refs[:-1], refs[-1]
    stations = spec_ref.shape[1]
    body = cap * stations
    rows[...] = jnp.zeros_like(rows)
    for g, out in enumerate(outs):
        h = send_group(g, lax.axis_index("clu"))
        for c in range(cap):
            event = exports_ref[h, c]
            out[c * stations : (c + 1) * stations, :] = spec_ref[event]
            place = c
            geo = geo_ref[event].astype(F32)
            rows[place : place + 1, :] = jnp.concatenate([geo[0:1], geo[1:2]], axis=1)
            place += GROUP_ROWS
            rows[place : place + 1, :] = jnp.concatenate([geo[2:3], geo[3:4]], axis=1)
        out[body : body + 2 * GROUP_ROWS, :] = rows[...].astype(BF16)


def fold(x):
    rows = x.shape[0] // 8
    total = x[0:8]
    for r in range(1, rows):
        total = total + x[8 * r : 8 * r + 8]
    return total


def prepare(natural, bp, bb, eb, pairs, freq):
    for j in range(pairs):
        turned = natural(j).astype(F32).T
        bp[j] = turned
        re, im = turned[:freq], turned[freq:]
        square = re * re + im * im
        bb[j] = square
        eb[j : j + 1, :] = jnp.sum(square, axis=0, keepdims=True)


def listed_pairs(ids, batches, da, sq, ea, bp, bb, eb, table, work, store, freq, scale):
    xs, reals, rm, rs, rt, rb, rz, re = work
    lead = lax.broadcasted_iota(jnp.int32, (8, 1), 0) == 0
    step = lax.broadcasted_iota(jnp.int32, (8, 1), 0).astype(F32)
    low = low_half((8, 128))
    unit = (math.pi / freq) ** 2

    def split(t, d):
        code = ids[t * (BATCH // 2) + d]
        return (code >> 12) & 31, code >> 17, ((code >> 6) & 63, code & 63)

    def cross_stage(t, slot):
        for d in range(BATCH // 2):
            j, _, duo = split(t, d)
            squares, sums = [[], []], [None, None]
            for v in range(0, freq, 16):
                br, bi = bp[j, v : v + 16, :], bp[j, freq + v : freq + v + 16, :]
                b2 = bb[j, v : v + 16, :]
                for i, e in enumerate(duo):
                    ar, ai = da[e, v : v + 16, :], da[e, freq + v : freq + v + 16, :]
                    cr = ar * br + ai * bi
                    ci = ai * br - ar * bi
                    both = sq[e, v : v + 16, :] * b2
                    u = 2 * d + i
                    lanes = slice(u * 128, (u + 1) * 128)
                    xs[slot, v : v + 16, lanes] = ci.astype(BF16)
                    reals[slot, v : v + 16, lanes] = cr.astype(BF16)
                    squares[i] += [both[:8], both[8:]]
                    part = cr[:8] + cr[8:]
                    sums[i] = part if v == 0 else sums[i] + part
                    if v == 0:
                        edge = cr[:8] * cr[:8] - ci[:8] * ci[:8]
                        rs[slot, u * 8 : u * 8 + 8, :] = jnp.where(lead, edge, 0.0)
            for i, e in enumerate(duo):
                u = 2 * d + i
                rows = slice(u * 8, u * 8 + 8)
                zero, one, two = squares[i][-1], squares[i][-1], squares[i][-1]
                for v in range(freq // 8 - 2, 0, -1):
                    zero = zero + squares[i][v]
                    one = one + zero
                    two = two + one
                zero = zero + squares[i][0]
                rs[slot, rows, :] += zero
                rb[slot, rows, :] = unit * (64.0 * (2.0 * two - one) + step * (16.0 * one + step * zero))
                rt[slot, rows, :] = sums[i]
                re[slot, u : u + 1, :] = ea[pl.ds(e, 1), :] * eb[pl.ds(j, 1), :]

    def moment_stage(slot):
        for start in range(0, BATCH, WIDE):
            lanes = slice(start * 128, (start + WIDE) * 128)
            z = jnp.dot(table[...], xs[slot, :, lanes], preferred_element_type=F32)
            for i in range(WIDE):
                part = z[:, i * 128 : (i + 1) * 128]
                real = reals[slot, :, (start + i) * 128 : (start + i + 1) * 128].astype(F32)
                rows = slice((start + i) * 8, (start + i + 1) * 8)
                rm[slot, rows, :] = fold(real * part[:freq])
                rz[slot, rows, :] = part[freq : freq + 8]

    def finish_stage(t, slot):
        def pick(ref, k):
            return ref[slot, pl.ds(k, 8, stride=8), :]

        moment, total, alternate, bend = pick(rm, 0), pick(rs, 0), pick(rt, 0), pick(rb, 0)
        for k in range(1, 8):
            moment = moment + pick(rm, k)
            total = total + pick(rs, k)
            bend = bend + pick(rb, k)
            alternate = alternate + pick(rt, k) if k % 2 == 0 else alternate - pick(rt, k)
        tilt = pick(rz, 0)
        inverse = 1.0 / (re[slot] + 1e-06)
        power = (freq * total - alternate * alternate) * inverse
        rough = (freq * bend - tilt * tilt) * inverse
        weight = power / (power + 0.125 * rough + 1e-06) * scale
        moved = weight * (moment * inverse / (power + 1e-06))
        even = jnp.where(low, weight, pltpu.roll(moved, 64, 1))
        odd = jnp.where(low, pltpu.roll(weight, 64, 1), moved)
        return even, odd

    def put(t, even, odd):
        for d in range(BATCH // 2):
            _, column, duo = split(t, d)
            for i, e in enumerate(duo):
                u = 2 * d + i
                store(e, column, even[u : u + 1], odd[u : u + 1])

    cross_stage(0, 0)
    moment_stage(0)
    cross_stage(1, 1)

    @pl.loop(0, (batches + 1) // 2)
    def _(i):
        first = finish_stage(2 * i, 0)
        cross_stage(2 * i + 2, 0)
        moment_stage(1)
        second = finish_stage(2 * i + 1, 1)
        cross_stage(2 * i + 3, 1)
        moment_stage(0)
        put(2 * i, *first)
        put(2 * i + 1, *second)


def local_kernel(freq, events, scale, batches, ids, spec_ref, table, out, da, sq, ea, bp, bb, eb, *work):
    pairs = events // 2
    prepare(lambda j: spec_ref[j], bp, bb, eb, pairs, freq)
    low = low_half((128, 128))
    for j in range(pairs):
        both = bp[j]
        other = pltpu.roll(both, 64, 1)
        da[2 * j] = jnp.where(low, both, other)
        da[2 * j + 1] = jnp.where(low, other, both)
        both = bb[j]
        other = pltpu.roll(both, 64, 1)
        sq[2 * j] = jnp.where(low[:freq], both, other)
        sq[2 * j + 1] = jnp.where(low[:freq], other, both)
    energy = eb[...]
    other = pltpu.roll(energy, 64, 1)
    low = low_half(energy.shape)
    ea[pl.ds(0, pairs, stride=2), :] = jnp.where(low, energy, other)
    ea[pl.ds(1, pairs, stride=2), :] = jnp.where(low, other, energy)
    row = low_half((1, 128))

    def store(e, column, even, odd):
        out[pl.ds(e * events + column, 1), :] = even
        out[pl.ds(e * events + column + 1, 1), :] = odd
        out[pl.ds(column * events + e, 1), :] = jnp.where(row, even, -even)
        out[pl.ds((column + 1) * events + e, 1), :] = jnp.where(row, odd, -odd)

    listed_pairs(ids, batches, da, sq, ea, bp, bb, eb, table, work, store, freq, scale)


def import_kernel(stage, arrivals, freq, events, cap, scale, ids, counts, *refs):
    got, (da, sq, ea, table, out, tail, bp, bb, eb), work = refs[:arrivals], refs[arrivals : arrivals + 9], refs[arrivals + 9 :]
    pairs = cap // 2

    def natural(j):
        return got[j // pairs][j % pairs * 128 : (j % pairs + 1) * 128, :]

    prepare(natural, bp, bb, eb, arrivals * pairs, freq)
    out[...] = jnp.zeros_like(out)
    for g in range(arrivals):
        tail[2 * GROUP_ROWS * g : 2 * GROUP_ROWS * (g + 1), :] = got[g][pairs * 128 :, :]

    def store(e, column, even, odd):
        out[pl.ds(e * arrivals * GROUP_ROWS + column, 1), :] = even
        out[pl.ds(e * arrivals * GROUP_ROWS + column + 1, 1), :] = odd

    batches = (counts[stage] + BATCH // 2 - 1) // (BATCH // 2)
    listed_pairs(ids.at[stage], batches, da, sq, ea, bp, bb, eb, table, work, store, freq, scale)


def weight_scratch(pairs, freq):
    return (
        [
            pltpu.VMEM((pairs, 2 * freq, 128), F32),
            pltpu.VMEM((pairs, freq, 128), F32),
            pltpu.VMEM((-(-pairs // 8) * 8, 128), F32),
            pltpu.VMEM((2, freq, BATCH * 128), BF16),
            pltpu.VMEM((2, freq, BATCH * 128), BF16),
        ]
        + [pltpu.VMEM((2, BATCH * 8, 128), F32)] * 5
        + [pltpu.VMEM((2, BATCH, 128), F32)]
    )


def two_parts(x):
    high = x.astype(BF16)
    return high, (x - high.astype(F32)).astype(BF16)


def sums_kernel(groups, events, slots, hot, hot_turned, mask, partials, *refs):
    tables, tails = refs[: STAGES + 1], refs[STAGES + 1 : 2 * STAGES + 1]
    slots_out, terms_out, geo_out, own, own_geo = refs[2 * STAGES + 1 :]
    import_rows = groups // STAGES * GROUP_ROWS
    cands = hot.shape[1]
    rest = jnp.zeros((SLOT_ROWS - slots, 128), F32)

    @pl.loop(0, events // UNROLL)
    def _(step):
        for u in range(UNROLL):
            e = step * UNROLL + u
            parts = [tables[0][pl.ds(pl.multiple_of(e * events, 8), events), :]]
            for t in tables[1:]:
                parts.append(t[pl.ds(pl.multiple_of(e * import_rows, 8), import_rows), :])
            every = jnp.concatenate(parts, axis=0).astype(BF16)
            rows = pl.ds(pl.multiple_of(e * SLOT_ROWS, SLOT_ROWS), SLOT_ROWS)
            live = mask[pl.ds(e, slots, stride=events), :].astype(F32)
            live = jnp.concatenate([jnp.concatenate([live, live], axis=1), rest], axis=0)
            picked = jnp.dot(hot[rows, :], every, preferred_element_type=F32) * live
            slots_out[rows, :] = picked.astype(BF16)
            own[pl.ds(e, 1), :] = jnp.sum(picked, axis=0, keepdims=True)
            geo = partials[e].astype(F32)
            own_geo[pl.ds(e, 1), :] = jnp.concatenate([geo[0:1], geo[1:2]], axis=1)
            own_geo[pl.ds(events + e, 1), :] = jnp.concatenate([geo[2:3], geo[3:4]], axis=1)

    gathered = jnp.dot(hot_turned[...], slots_out[...], preferred_element_type=F32)
    low = low_half((cands, 128))
    gathered = jnp.where(low, gathered, -gathered)
    totals = jnp.concatenate([gathered[:events] + own[...], gathered[events:]], axis=0)
    turned = pltpu.roll(totals, 64, 1)
    weights = jnp.where(low, totals, turned)
    moves = jnp.where(low, turned, totals)
    ends = [t[start : start + 2 * GROUP_ROWS, :] for t in tails for start in range(0, 2 * import_rows, 2 * GROUP_ROWS)]
    first = jnp.concatenate([own_geo[:events].astype(BF16)] + [t[:GROUP_ROWS] for t in ends], axis=0)
    second = jnp.concatenate([own_geo[events:].astype(BF16)] + [t[GROUP_ROWS:] for t in ends], axis=0)
    geo_out[:, :128] = first
    geo_out[:, 128:] = second
    blocks = [first.astype(F32), second.astype(F32)]
    singles = []
    for block in blocks:
        other = pltpu.roll(block, 64, 1)
        singles += [jnp.where(low, block, other), jnp.where(low, other, block)]
    half_row = lax.broadcasted_iota(jnp.int32, (8, 128), 0)
    half_lane = lax.broadcasted_iota(jnp.int32, (8, 128), 1) // 64
    picker = jnp.where(half_row == half_lane, 1.0, 0.0).astype(BF16)
    picker = jnp.concatenate([picker, picker], axis=1)

    def halves(values):
        both = jnp.concatenate(two_parts(values), axis=1)
        return lax.dot_general(picker, both, (((1,), (1,)), ((), ())), preferred_element_type=F32)[:2]

    rights = [halves(moves * blocks[0]), halves(moves * blocks[1])]
    for i in range(4):
        scaled = weights * singles[i]
        rows = [halves(scaled * blocks[0]), halves(scaled * blocks[1]), rights[i // 2][i % 2 : i % 2 + 1]]
        share = jnp.concatenate(rows + [jnp.zeros((3, 128), F32)], axis=0)
        for q in range(terms_out.shape[1]):
            terms_out[i, q] = share


def blocks_kernel(events, place, hot, slots, geo, partials, *refs):
    outs, turned = refs[:-1], refs[-1]
    turned[...] = jnp.zeros_like(turned)
    low = low_half((SLOT_ROWS, 128))
    column = lax.broadcasted_iota(jnp.int32, (16, 128), 0) % 4
    block = lax.broadcasted_iota(jnp.int32, (16, 128), 1) // 64

    @pl.loop(0, events // UNROLL)
    def _(step):
        for u in range(UNROLL):
            e = step * UNROLL + u
            rows = pl.ds(pl.multiple_of(e * SLOT_ROWS, SLOT_ROWS), SLOT_ROWS)
            partner = jnp.dot(hot[rows, :], geo[...], preferred_element_type=F32)
            pair = slots[rows, :].astype(F32)
            weights = jnp.where(low, pair, pltpu.roll(pair, 64, 1))
            weighted = jnp.concatenate([weights * partner[:, :128], weights * partner[:, 128:]], axis=1).astype(BF16)
            own = partials[e].astype(F32)
            own = jnp.concatenate([own, own], axis=1)
            own = jnp.concatenate([jnp.broadcast_to(-own[i : i + 1], (4, 128)) for i in range(4)], axis=0)
            left = [jnp.where(column == block, own, 0.0), jnp.where(column == block + 2, own, 0.0)]
            left = jnp.concatenate(left, axis=1).astype(BF16)
            entry = lax.dot_general(left, weighted, (((1,), (1,)), ((), ())), preferred_element_type=F32)
            turned[pl.ds(e, 16, stride=events), 0:SLOT_ROWS] = entry

    for d, out in enumerate(outs):
        share = place[0] ^ d
        rows = pl.ds(pl.multiple_of(share * 4 * events, 128), 4 * events)
        out[...] = turned[rows, :].T[: out.shape[0]]


def total_kernel(groups, events, slots, clusters, own, one, two, three, received, owners, normal, right):
    parts = []
    for g in range(groups + 1):
        part = received[clusters[g]]
        for t in range(1, 4):
            part = part + received[t * (received.shape[0] // 4) + clusters[g]]
        parts.append(part)
    high, low = two_parts(jnp.concatenate(parts, axis=1))
    spread = jnp.dot(high, owners[...], preferred_element_type=F32) + jnp.dot(low, owners[...], preferred_element_type=F32)
    block = lax.broadcasted_iota(jnp.int32, (1, 128), 1) // events
    diagonal = jnp.zeros((1, 128), F32)
    for j in range(4):
        diagonal = jnp.where(block == j, spread[j : j + 1], diagonal)
    right[...] = spread[4:5, :events]
    total = pltpu.roll((own[...] + one[...]) + (two[...] + three[...]), 1, 0)
    top = lax.broadcasted_iota(jnp.int32, total.shape, 0) == 0
    total = jnp.where(top, diagonal, total)
    turned = total.T
    for j in range(4):
        normal[j] = turned[j * events : (j + 1) * events, : slots + 1]


def vmem(n):
    return [pl.BlockSpec(memory_space=pltpu.VMEM)] * n


def call(kernel, outs, inputs, scratch=(), specs=None, micros=1.0, limit=VMEM_LIMIT):
    shapes = [jax.ShapeDtypeStruct(s, t) for s, t in outs]
    return pl.pallas_call(
        kernel,
        out_shape=shapes,
        in_specs=specs if specs is not None else vmem(len(inputs)),
        out_specs=vmem(len(outs)),
        scratch_shapes=list(scratch),
        compiler_params=pltpu.CompilerParams(vmem_limit_bytes=limit),
        cost_estimate=pl.CostEstimate(flops=int(micros * 1e9), bytes_accessed=1024, transcendentals=0),
    )(*inputs)


def on_device(spectra, partials, pair_list, station_mask, exports):
    events, stations, two_freq = spectra.shape
    freq = two_freq // 2
    groups, cap = exports.shape
    half_span = groups // 2
    slots = pair_list.shape[1]
    sta_groups = lax.axis_size("sta")
    scale = 1.0 / (stations * sta_groups)
    offsets = [h - half_span + (1 if h >= half_span else 0) for h in range(groups)]
    cands = events + groups * GROUP_ROWS
    half = cap // 2
    table = moment_table(freq)
    smem = pl.BlockSpec(memory_space=pltpu.SMEM)
    clusters = lax.axis_size("clu")

    paired = clusters == groups + 2 and clusters & (clusters - 1) == 0
    if paired:
        masks = [m for m in range(1, clusters) if m != clusters // 2]
        routes = [[(i, i ^ m) for i in range(clusters)] for m in masks]
    else:
        order = sorted(range(groups), key=lambda h: abs(offsets[h]))
        routes = [[(i, (i + offsets[h]) % clusters) for i in range(clusters)] for h in order]

    def group_of(offset):
        offset = offset & (clusters - 1)
        return jnp.where(offset < clusters // 2, offset + half_span - 1, offset - clusters + half_span)

    def send_group(g, p):
        return group_of((p ^ masks[g]) - p) if paired else order[g]

    def receive_group(g, p):
        return group_of(p - (p ^ masks[g])) if paired else order[g]

    def receiver(g, p):
        return p ^ masks[g] if paired else (p + offsets[order[g]]) % clusters

    out_rows = cap * stations + 2 * GROUP_ROWS
    outgoing = call(
        functools.partial(outgoing_kernel, cap, send_group),
        [((out_rows, 128), BF16)] * groups,
        (exports, spectra, partials),
        scratch=[pltpu.VMEM((2 * GROUP_ROWS, 128), F32)],
        specs=[smem] + vmem(2),
        micros=2.0,
        limit=60 * 1024 * 1024,
    )
    got = [None] * groups
    for g in [0] + list(range(groups - 1, 0, -1)):
        got[g] = lax.ppermute(outgoing[g], "clu", routes[g])
    me = lax.axis_index("clu").astype(jnp.int32)
    sent = jnp.stack([jnp.asarray(send_group(g, me), jnp.int32) for g in range(groups)])
    came = jnp.stack([jnp.asarray(receive_group(g, me), jnp.int32) for g in range(groups)])

    duos = [j << 18 | j << 12 | e << 6 | e + 1 for j in range(events // 2) for e in range(0, 2 * j + 2, 2)]
    batches = -(-len(duos) // BATCH) * 2
    duos = duos + [1] * ((batches + 3) * (BATCH // 2) - len(duos))
    natural, got[0] = lax.optimization_barrier((spectra, got[0]))
    local, dup, square, energy = call(
        functools.partial(local_kernel, freq, events, scale, batches),
        [
            ((events * events, 128), F32),
            ((events, 128, 128), F32),
            ((events, freq, 128), F32),
            ((events, 128), F32),
        ],
        (jnp.asarray(duos, jnp.int32), natural.reshape(events // 2, 2 * stations, two_freq), table),
        scratch=weight_scratch(events // 2, freq),
        specs=[smem] + vmem(2),
        micros=8.0,
    )

    far = jnp.maximum(pair_list - events, 0)
    far_group = far // cap
    arrival = jnp.sum(jnp.where(far_group[:, :, None] == came[None, None, :], jnp.arange(groups, dtype=jnp.int32), 0), axis=2)
    entry = far % cap
    named = jnp.where(pair_list < events, -1, arrival * half + entry // 2)
    wanted = jnp.any(named[:, :, None] == jnp.arange(groups * half, dtype=jnp.int32)[None, None, :], axis=1)
    arrivals = groups // STAGES
    pairs = arrivals * half
    wanted = wanted.astype(F32).T.reshape(STAGES, pairs, events)
    ranks = np.arange(events)
    rank = jnp.einsum("gje,ef->gjf", wanted, jnp.asarray(ranks[:, None] < ranks[None, :], F32))
    rounded = jnp.ceil(jnp.sum(wanted, axis=2) * 0.5)
    ranks = np.arange(pairs)
    start = jnp.sum(rounded[:, :, None] * jnp.asarray(ranks[:, None] < ranks[None, :], F32)[None], axis=1)
    rank = rank.astype(jnp.int32)
    spot = jnp.where(wanted > 0, start.astype(jnp.int32)[:, :, None] + (rank >> 1), -1).reshape(STAGES, pairs * events)
    event_ids = jnp.arange(events, dtype=jnp.int32)[None, None, :]
    pair_codes = jnp.asarray(((ranks // half * GROUP_ROWS + ranks % half * 2) << 17) + (ranks << 12), jnp.int32)
    code = jnp.where(rank & 1 == 0, pair_codes[None, :, None] + (event_ids << 6), event_ids).reshape(STAGES, pairs * events)
    longest = pairs * events // 2 + 3 * BATCH // 2
    lists = jnp.sum(
        jnp.where(spot[:, None, :] == jnp.arange(longest, dtype=jnp.int32)[None, :, None], code[:, None, :], 0), axis=2
    )
    counts = jnp.sum(rounded, axis=1).astype(jnp.int32)

    column = jnp.where(pair_list < events, pair_list, events + GROUP_ROWS * arrival + entry)
    column = jnp.pad(column, ((0, 0), (0, SLOT_ROWS - slots)), constant_values=-1).reshape(-1)
    cand_ids = jnp.arange(cands, dtype=jnp.int32)
    hot = (column[:, None] == cand_ids[None, :]).astype(BF16)
    hot_turned = (cand_ids[:, None] == column[None, :]).astype(BF16)
    mask = station_mask.transpose(1, 0, 2).reshape(slots * events, stations)
    owner_rows = [jnp.asarray(np.where(np.arange(cands) < events, np.arange(cands), -1), jnp.int32)]
    hot_sent = sent[:, None] == jnp.arange(groups, dtype=jnp.int32)[None, :]
    rows_sent = jnp.sum(jnp.where(hot_sent[:, :, None], exports[None], 0), axis=1)
    for g in range(groups):
        start = events + GROUP_ROWS * g
        owner_rows.append(jnp.pad(rows_sent[g], (start, cands - start - cap), constant_values=-1))
    owners = jnp.concatenate(owner_rows)[:, None] == (jnp.arange(128, dtype=jnp.int32) % events)[None, :]
    owners = owners.astype(BF16)

    tables, tails = [None] * STAGES, [None] * STAGES
    for g in range(STAGES):
        tables[g], tails[g] = call(
            functools.partial(import_kernel, g, arrivals, freq, events, cap, scale),
            [((events * arrivals * GROUP_ROWS, 128), F32), ((arrivals * 2 * GROUP_ROWS, 128), BF16)],
            (lists, counts, *got[g * arrivals : (g + 1) * arrivals], dup, square, energy, table),
            scratch=weight_scratch(pairs, freq),
            specs=[smem] * 2 + vmem(arrivals + 4),
            micros=8.0,
        )

    weights, terms, geo = call(
        functools.partial(sums_kernel, groups, events, slots),
        [((events * SLOT_ROWS, 128), BF16), ((4, clusters, 8, 128), F32), ((cands, 256), BF16)],
        (hot, hot_turned, mask, partials, local, *tables, *tails),
        scratch=[pltpu.VMEM((events, 128), F32), pltpu.VMEM((2 * events, 128), F32)],
        micros=2.0,
    )
    terms = lax.all_to_all(
        terms.reshape(4 * clusters, 8, 128), ("sta", "clu"), split_axis=0, concat_axis=0, tiled=True
    )
    message_rows = -(-(slots + 1) // 8) * 8
    place = lax.axis_index("sta").astype(jnp.int32).reshape(1)
    shares = call(
        functools.partial(blocks_kernel, events),
        [((message_rows, 128), F32)] * 4,
        (place, hot, weights, geo, partials),
        scratch=[pltpu.VMEM((16 * events, 128), F32)],
        specs=[smem] + vmem(4),
        micros=3.0,
    )
    shares = [shares[0]] + [lax.ppermute(shares[d], "sta", [(i, i ^ d) for i in range(4)]) for d in range(1, 4)]
    sources = jnp.stack([me] + [jnp.asarray(receiver(g, me), jnp.int32) for g in range(groups)])
    normal, right = call(
        functools.partial(total_kernel, groups, events, slots),
        [((4, events, slots + 1), F32), ((1, events), F32)],
        (sources, *shares, terms, owners),
        specs=[smem] + vmem(6),
    )
    return (normal.transpose(0, 2, 1), right)


def solution(mesh):
    return jax.shard_map(
        on_device,
        mesh=mesh,
        in_specs=(
            P("clu", "sta", None),
            P("clu", None, "sta"),
            P("clu", None),
            P("clu", None, "sta"),
            P("clu", None),
        ),
        out_specs=(P("sta", None, "clu"), P("sta", "clu")),
        check_vma=False,
    )
```

```python
import functools
import math

import jax
import jax.numpy as jnp
import numpy as np
from jax import lax
from jax.experimental import pallas as pl
from jax.experimental.pallas import tpu as pltpu
from jax.sharding import PartitionSpec as P

F32 = jnp.float32
BF16 = jnp.bfloat16
VMEM_LIMIT = 24 * 1024 * 1024
SLOT_ROWS = 64
GROUP_ROWS = 16
BATCH = 8
WIDE = 4
UNROLL = 8
STAGE_SIZES = (3, 2, 1)


def moment_table(freq_count):
    f = np.arange(freq_count)

    def edge(k):
        out = np.zeros(k.shape)
        live = (k % (2 * freq_count)) != 0
        sign = 1.0 - 2.0 * (k[live] % 2)
        out[live] = -freq_count * sign / np.tan(np.pi * k[live] / (2 * freq_count))
        return out

    w = f * math.pi / freq_count
    table = np.zeros((freq_count + 16, 2 * freq_count), np.float32)
    table[:freq_count, :freq_count] = -(edge(f[:, None] + f[None, :]) + edge(f[None, :] - f[:, None]))
    table[freq_count, :freq_count] = (1.0 - 2.0 * (f % 2)) * w
    high = (w * w).astype(jnp.bfloat16).astype(np.float64)
    table[freq_count + 1, freq_count:] = high
    table[freq_count + 2, freq_count:] = w * w - high
    return jnp.asarray(table, F32).astype(BF16)


def low_half(shape):
    return lax.broadcasted_iota(jnp.int32, shape, len(shape) - 1) < shape[-1] // 2


def outgoing_kernel(cap, send_group, exports_ref, spec_ref, geo_ref, *refs):
    outs, rows = refs[:-1], refs[-1]
    stations = spec_ref.shape[1]
    body = cap * stations
    rows[...] = jnp.zeros_like(rows)
    for g, out in enumerate(outs):
        h = send_group(g, lax.axis_index("clu"))
        for c in range(cap):
            event = exports_ref[h, c]
            out[c * stations : (c + 1) * stations, :] = spec_ref[event]
            place = c
            geo = geo_ref[event].astype(F32)
            rows[place : place + 1, :] = jnp.concatenate([geo[0:1], geo[1:2]], axis=1)
            place += GROUP_ROWS
            rows[place : place + 1, :] = jnp.concatenate([geo[2:3], geo[3:4]], axis=1)
        out[body : body + 2 * GROUP_ROWS, :] = rows[...].astype(BF16)


def fold(x):
    rows = x.shape[0] // 8
    total = x[0:8]
    for r in range(1, rows):
        total = total + x[8 * r : 8 * r + 8]
    return total


def prepare(natural, bp, bb, eb, pairs, freq):
    for j in range(pairs):
        turned = natural(j).astype(F32).T
        bp[j] = turned
        re, im = turned[:freq], turned[freq:]
        square = re * re + im * im
        bb[j] = square
        eb[j : j + 1, :] = jnp.sum(square, axis=0, keepdims=True)


def listed_pairs(fetch, batches, da, sq, ea, bp, bb, eb, table, work, store, freq, scale):
    xs, reals, rm, rs, rt, rz, re = work
    lead = lax.broadcasted_iota(jnp.int32, (8, 1), 0) == 0
    low = low_half((8, 128))

    def split(t, d):
        code = fetch(t * (BATCH // 2) + d)
        return (code >> 12) & 31, code >> 17, ((code >> 6) & 63, code & 63)

    def cross_stage(t, slot):
        for d in range(BATCH // 2):
            j, _, duo = split(t, d)
            totals, sums = [None, None], [None, None]
            for v in range(0, freq, 16):
                br, bi = bp[j, v : v + 16, :], bp[j, freq + v : freq + v + 16, :]
                b2 = bb[j, v : v + 16, :]
                for i, e in enumerate(duo):
                    ar, ai = da[e, v : v + 16, :], da[e, freq + v : freq + v + 16, :]
                    cr = ar * br + ai * bi
                    ci = ai * br - ar * bi
                    both = sq[e, v : v + 16, :] * b2
                    u = 2 * d + i
                    lanes = slice(u * 128, (u + 1) * 128)
                    xs[slot, v : v + 16, lanes] = ci.astype(BF16)
                    xs[slot, freq + v : freq + v + 16, lanes] = both.astype(BF16)
                    reals[slot, v : v + 16, lanes] = cr.astype(BF16)
                    square, real = both[:8] + both[8:], cr[:8] + cr[8:]
                    if v == 0:
                        edge = cr[:8] * cr[:8] - ci[:8] * ci[:8]
                        totals[i], sums[i] = square + jnp.where(lead, edge, 0.0), real
                    else:
                        totals[i], sums[i] = totals[i] + square, sums[i] + real
            for i, e in enumerate(duo):
                u = 2 * d + i
                rows = slice(u * 8, u * 8 + 8)
                rs[slot, rows, :] = totals[i]
                rt[slot, rows, :] = sums[i]
                re[slot, u : u + 1, :] = ea[pl.ds(e, 1), :] * eb[pl.ds(j, 1), :]

    def moment_stage(slot):
        for start in range(0, BATCH, WIDE):
            lanes = slice(start * 128, (start + WIDE) * 128)
            z = jnp.dot(table[...], xs[slot, :, lanes], preferred_element_type=F32)
            for i in range(WIDE):
                part = z[:, i * 128 : (i + 1) * 128]
                real = reals[slot, :, (start + i) * 128 : (start + i + 1) * 128].astype(F32)
                rows = slice((start + i) * 8, (start + i + 1) * 8)
                rm[slot, rows, :] = fold(real * part[:freq])
                rz[slot, rows, :] = part[freq : freq + 8]

    def finish_stage(t, slot):
        def pick(ref, k):
            return ref[slot, pl.ds(k, 8, stride=8), :]

        moment, total, alternate = pick(rm, 0), pick(rs, 0), pick(rt, 0)
        for k in range(1, 8):
            moment = moment + pick(rm, k)
            total = total + pick(rs, k)
            alternate = alternate + pick(rt, k) if k % 2 == 0 else alternate - pick(rt, k)
        tilt = pick(rz, 0)
        bend = pick(rz, 1) + pick(rz, 2)
        inverse = 1.0 / (re[slot] + 1e-06)
        power = (freq * total - alternate * alternate) * inverse
        rough = (freq * bend - tilt * tilt) * inverse
        weight = power / (power + 0.125 * rough + 1e-06) * scale
        moved = weight * (moment * inverse / (power + 1e-06))
        even = jnp.where(low, weight, pltpu.roll(moved, 64, 1))
        odd = jnp.where(low, pltpu.roll(weight, 64, 1), moved)
        return even, odd

    def put(t, even, odd):
        for d in range(BATCH // 2):
            _, column, duo = split(t, d)
            for i, e in enumerate(duo):
                u = 2 * d + i
                store(e, column, even[u : u + 1], odd[u : u + 1])

    cross_stage(0, 0)
    moment_stage(0)
    cross_stage(1, 1)

    @pl.loop(0, (batches + 1) // 2)
    def _(i):
        first = finish_stage(2 * i, 0)
        cross_stage(2 * i + 2, 0)
        moment_stage(1)
        second = finish_stage(2 * i + 1, 1)
        cross_stage(2 * i + 3, 1)
        moment_stage(0)
        put(2 * i, *first)
        put(2 * i + 1, *second)


def local_kernel(freq, events, scale, batches, ids, spec_ref, table, out, da, sq, ea, bp, bb, eb, *work):
    pairs = events // 2
    prepare(lambda j: spec_ref[j], bp, bb, eb, pairs, freq)
    low = low_half((128, 128))
    for j in range(pairs):
        both = bp[j]
        other = pltpu.roll(both, 64, 1)
        da[2 * j] = jnp.where(low, both, other)
        da[2 * j + 1] = jnp.where(low, other, both)
        both = bb[j]
        other = pltpu.roll(both, 64, 1)
        sq[2 * j] = jnp.where(low[:freq], both, other)
        sq[2 * j + 1] = jnp.where(low[:freq], other, both)
    energy = eb[...]
    other = pltpu.roll(energy, 64, 1)
    low = low_half(energy.shape)
    ea[pl.ds(0, pairs, stride=2), :] = jnp.where(low, energy, other)
    ea[pl.ds(1, pairs, stride=2), :] = jnp.where(low, other, energy)
    row = low_half((1, 128))

    def store(e, column, even, odd):
        out[pl.ds(e * events + column, 1), :] = even
        out[pl.ds(e * events + column + 1, 1), :] = odd
        out[pl.ds(column * events + e, 1), :] = jnp.where(row, even, -even)
        out[pl.ds((column + 1) * events + e, 1), :] = jnp.where(row, odd, -odd)

    listed_pairs(lambda n: ids[n], batches, da, sq, ea, bp, bb, eb, table, work, store, freq, scale)


def import_kernel(begin, arrivals, freq, events, cap, scale, ids, counts, *refs):
    got, (da, sq, ea, table, out, tail, bp, bb, eb), work = refs[:arrivals], refs[arrivals : arrivals + 9], refs[arrivals + 9 :]
    pairs = cap // 2

    def natural(j):
        return got[j // pairs][j % pairs * 128 : (j % pairs + 1) * 128, :]

    prepare(natural, bp, bb, eb, arrivals * pairs, freq)
    out[...] = jnp.zeros_like(out)
    for g in range(arrivals):
        tail[2 * GROUP_ROWS * g : 2 * GROUP_ROWS * (g + 1), :] = got[g][pairs * 128 :, :]

    def store(e, column, even, odd):
        out[pl.ds(e * arrivals * GROUP_ROWS + column, 1), :] = even
        out[pl.ds(e * arrivals * GROUP_ROWS + column + 1, 1), :] = odd

    ends = [counts[begin]]
    for g in range(1, arrivals):
        ends.append(ends[-1] + counts[begin + g])

    def fetch(n):
        group, start = 0, 0
        for end in ends[:-1]:
            group = group + jnp.where(n >= end, 1, 0)
            start = jnp.where(n >= end, end, start)
        return ids[begin + group, n - start]

    batches = (ends[-1] + BATCH // 2 - 1) // (BATCH // 2)
    listed_pairs(fetch, batches, da, sq, ea, bp, bb, eb, table, work, store, freq, scale)


def weight_scratch(pairs, freq):
    return (
        [
            pltpu.VMEM((pairs, 2 * freq, 128), F32),
            pltpu.VMEM((pairs, freq, 128), F32),
            pltpu.VMEM((-(-pairs // 8) * 8, 128), F32),
            pltpu.VMEM((2, 2 * freq, BATCH * 128), BF16),
            pltpu.VMEM((2, freq, BATCH * 128), BF16),
        ]
        + [pltpu.VMEM((2, BATCH * 8, 128), F32)] * 4
        + [pltpu.VMEM((2, BATCH, 128), F32)]
    )


def two_parts(x):
    high = x.astype(BF16)
    return high, (x - high.astype(F32)).astype(BF16)


def slots_kernel(events, slots, place, hot, mask, partials, *refs):
    stages = len(STAGE_SIZES)
    tables, tails = refs[: stages + 1], refs[stages + 1 : 2 * stages + 1]
    outs, (slots_out, geo_out, own, own_geo, turned) = refs[2 * stages + 1 : -5], refs[-5:]
    rest = jnp.zeros((SLOT_ROWS - slots, 128), F32)
    for e in range(events):
        geo = partials[e].astype(F32)
        own_geo[e : e + 1, :] = jnp.concatenate([geo[0:1], geo[1:2]], axis=1)
        own_geo[events + e : events + e + 1, :] = jnp.concatenate([geo[2:3], geo[3:4]], axis=1)
    ends = [t[start : start + 2 * GROUP_ROWS, :] for t in tails for start in range(0, t.shape[0], 2 * GROUP_ROWS)]
    geo_out[:, :128] = jnp.concatenate([own_geo[:events].astype(BF16)] + [t[:GROUP_ROWS] for t in ends], axis=0)
    geo_out[:, 128:] = jnp.concatenate([own_geo[events:].astype(BF16)] + [t[GROUP_ROWS:] for t in ends], axis=0)
    turned[...] = jnp.zeros_like(turned)
    low = low_half((SLOT_ROWS, 128))
    column = lax.broadcasted_iota(jnp.int32, (16, 128), 0) % 4
    block = lax.broadcasted_iota(jnp.int32, (16, 128), 1) // 64

    @pl.loop(0, events // UNROLL)
    def _(step):
        for u in range(UNROLL):
            e = step * UNROLL + u
            parts = [tables[0][pl.ds(pl.multiple_of(e * events, 8), events), :]]
            for t, size in zip(tables[1:], STAGE_SIZES):
                rows = size * GROUP_ROWS
                parts.append(t[pl.ds(pl.multiple_of(e * rows, 8), rows), :])
            every = jnp.concatenate(parts, axis=0).astype(BF16)
            rows = pl.ds(pl.multiple_of(e * SLOT_ROWS, SLOT_ROWS), SLOT_ROWS)
            live = mask[pl.ds(e, slots, stride=events), :].astype(F32)
            live = jnp.concatenate([jnp.concatenate([live, live], axis=1), rest], axis=0)
            picked = jnp.dot(hot[rows, :], every, preferred_element_type=F32) * live
            partner = jnp.dot(hot[rows, :], geo_out[...], preferred_element_type=F32)
            slots_out[rows, :] = picked.astype(BF16)
            own[pl.ds(e, 1), :] = jnp.sum(picked, axis=0, keepdims=True)
            weights = jnp.where(low, picked, pltpu.roll(picked, 64, 1))
            weighted = jnp.concatenate([weights * partner[:, :128], weights * partner[:, 128:]], axis=1).astype(BF16)
            geo = partials[e].astype(F32)
            geo = jnp.concatenate([geo, geo], axis=1)
            geo = jnp.concatenate([jnp.broadcast_to(-geo[i : i + 1], (4, 128)) for i in range(4)], axis=0)
            left = [jnp.where(column == block, geo, 0.0), jnp.where(column == block + 2, geo, 0.0)]
            left = jnp.concatenate(left, axis=1).astype(BF16)
            entry = lax.dot_general(left, weighted, (((1,), (1,)), ((), ())), preferred_element_type=F32)
            turned[pl.ds(e, 16, stride=events), 0:SLOT_ROWS] = entry

    for d, out in enumerate(outs):
        share = place[0] ^ d
        rows = pl.ds(pl.multiple_of(share * 4 * events, 128), 4 * events)
        out[...] = turned[rows, :].T[: out.shape[0]]


def terms_kernel(events, hot_turned, slots, geo, own, terms_out):
    cands = geo.shape[0]
    gathered = jnp.dot(hot_turned[...], slots[...], preferred_element_type=F32)
    low = low_half((cands, 128))
    gathered = jnp.where(low, gathered, -gathered)
    totals = jnp.concatenate([gathered[:events] + own[...], gathered[events:]], axis=0)
    turned = pltpu.roll(totals, 64, 1)
    weights = jnp.where(low, totals, turned)
    moves = jnp.where(low, turned, totals)
    blocks = [geo[:, :128].astype(F32), geo[:, 128:].astype(F32)]
    singles = []
    for block in blocks:
        other = pltpu.roll(block, 64, 1)
        singles += [jnp.where(low, block, other), jnp.where(low, other, block)]
    half_row = lax.broadcasted_iota(jnp.int32, (8, 128), 0)
    half_lane = lax.broadcasted_iota(jnp.int32, (8, 128), 1) // 64
    picker = jnp.where(half_row == half_lane, 1.0, 0.0).astype(BF16)
    picker = jnp.concatenate([picker, picker], axis=1)

    def halves(values):
        both = jnp.concatenate(two_parts(values), axis=1)
        return lax.dot_general(picker, both, (((1,), (1,)), ((), ())), preferred_element_type=F32)[:2]

    rights = [halves(moves * blocks[0]), halves(moves * blocks[1])]
    for i in range(4):
        scaled = weights * singles[i]
        rows = [halves(scaled * blocks[0]), halves(scaled * blocks[1]), rights[i // 2][i % 2 : i % 2 + 1]]
        share = jnp.concatenate(rows + [jnp.zeros((3, 128), F32)], axis=0)
        for q in range(terms_out.shape[1]):
            terms_out[i, q] = share


def total_kernel(groups, events, slots, clusters, own, one, two, three, received, owners, normal, right):
    parts = []
    for g in range(groups + 1):
        part = received[clusters[g]]
        for t in range(1, 4):
            part = part + received[t * (received.shape[0] // 4) + clusters[g]]
        parts.append(part)
    high, low = two_parts(jnp.concatenate(parts, axis=1))
    spread = jnp.dot(high, owners[...], preferred_element_type=F32) + jnp.dot(low, owners[...], preferred_element_type=F32)
    block = lax.broadcasted_iota(jnp.int32, (1, 128), 1) // events
    diagonal = jnp.zeros((1, 128), F32)
    for j in range(4):
        diagonal = jnp.where(block == j, spread[j : j + 1], diagonal)
    right[...] = spread[4:5, :events]
    total = pltpu.roll((own[...] + one[...]) + (two[...] + three[...]), 1, 0)
    top = lax.broadcasted_iota(jnp.int32, total.shape, 0) == 0
    total = jnp.where(top, diagonal, total)
    turned = total.T
    for j in range(4):
        normal[j] = turned[j * events : (j + 1) * events, : slots + 1]


def vmem(n):
    return [pl.BlockSpec(memory_space=pltpu.VMEM)] * n


def call(kernel, outs, inputs, scratch=(), specs=None, micros=1.0, limit=VMEM_LIMIT):
    shapes = [jax.ShapeDtypeStruct(s, t) for s, t in outs]
    return pl.pallas_call(
        kernel,
        out_shape=shapes,
        in_specs=specs if specs is not None else vmem(len(inputs)),
        out_specs=vmem(len(outs)),
        scratch_shapes=list(scratch),
        compiler_params=pltpu.CompilerParams(vmem_limit_bytes=limit),
        cost_estimate=pl.CostEstimate(flops=int(micros * 1e9), bytes_accessed=1024, transcendentals=0),
    )(*inputs)


def on_device(spectra, partials, pair_list, station_mask, exports):
    events, stations, two_freq = spectra.shape
    freq = two_freq // 2
    groups, cap = exports.shape
    half_span = groups // 2
    slots = pair_list.shape[1]
    sta_groups = lax.axis_size("sta")
    scale = 1.0 / (stations * sta_groups)
    offsets = [h - half_span + (1 if h >= half_span else 0) for h in range(groups)]
    cands = events + groups * GROUP_ROWS
    half = cap // 2
    table = moment_table(freq)
    smem = pl.BlockSpec(memory_space=pltpu.SMEM)
    clusters = lax.axis_size("clu")

    paired = clusters == groups + 2 and clusters & (clusters - 1) == 0
    if paired:
        masks = [m for m in range(1, clusters) if m != clusters // 2]
        routes = [[(i, i ^ m) for i in range(clusters)] for m in masks]
    else:
        order = sorted(range(groups), key=lambda h: abs(offsets[h]))
        routes = [[(i, (i + offsets[h]) % clusters) for i in range(clusters)] for h in order]

    def group_of(offset):
        offset = offset & (clusters - 1)
        return jnp.where(offset < clusters // 2, offset + half_span - 1, offset - clusters + half_span)

    def send_group(g, p):
        return group_of((p ^ masks[g]) - p) if paired else order[g]

    def receive_group(g, p):
        return group_of(p - (p ^ masks[g])) if paired else order[g]

    def receiver(g, p):
        return p ^ masks[g] if paired else (p + offsets[order[g]]) % clusters

    out_rows = cap * stations + 2 * GROUP_ROWS
    outgoing = call(
        functools.partial(outgoing_kernel, cap, send_group),
        [((out_rows, 128), BF16)] * groups,
        (exports, spectra, partials),
        scratch=[pltpu.VMEM((2 * GROUP_ROWS, 128), F32)],
        specs=[smem] + vmem(2),
        micros=2.0,
        limit=60 * 1024 * 1024,
    )
    got = [None] * groups
    for g in [0] + list(range(groups - 1, 0, -1)):
        got[g] = lax.ppermute(outgoing[g], "clu", routes[g])
    me = lax.axis_index("clu").astype(jnp.int32)
    sent = jnp.stack([jnp.asarray(send_group(g, me), jnp.int32) for g in range(groups)])
    came = jnp.stack([jnp.asarray(receive_group(g, me), jnp.int32) for g in range(groups)])

    duos = [j << 18 | j << 12 | e << 6 | e + 1 for j in range(events // 2) for e in range(0, 2 * j + 2, 2)]
    batches = -(-len(duos) // BATCH) * 2
    duos = duos + [1] * ((batches + 3) * (BATCH // 2) - len(duos))
    natural, got[0] = lax.optimization_barrier((spectra, got[0]))
    local, dup, square, energy = call(
        functools.partial(local_kernel, freq, events, scale, batches),
        [
            ((events * events, 128), F32),
            ((events, 128, 128), F32),
            ((events, freq, 128), F32),
            ((events, 128), F32),
        ],
        (jnp.asarray(duos, jnp.int32), natural.reshape(events // 2, 2 * stations, two_freq), table),
        scratch=weight_scratch(events // 2, freq),
        specs=[smem] + vmem(2),
        micros=8.0,
    )

    far = jnp.maximum(pair_list - events, 0)
    far_group = far // cap
    arrival = jnp.sum(jnp.where(far_group[:, :, None] == came[None, None, :], jnp.arange(groups, dtype=jnp.int32), 0), axis=2)
    entry = far % cap
    named = jnp.where(pair_list < events, -1, arrival * half + entry // 2)
    wanted = jnp.any(named[:, :, None] == jnp.arange(groups * half, dtype=jnp.int32)[None, None, :], axis=1)
    wanted = wanted.astype(F32).T.reshape(groups, half, events)
    ranks = np.arange(events)
    rank = jnp.einsum("gje,ef->gjf", wanted, jnp.asarray(ranks[:, None] < ranks[None, :], F32))
    rounded = jnp.ceil(jnp.sum(wanted, axis=2) * 0.5)
    ranks = np.arange(half)
    start = jnp.sum(rounded[:, :, None] * jnp.asarray(ranks[:, None] < ranks[None, :], F32)[None], axis=1)
    rank = rank.astype(jnp.int32)
    spot = jnp.where(wanted > 0, start.astype(jnp.int32)[:, :, None] + (rank >> 1), -1).reshape(groups, half * events)
    event_ids = jnp.arange(events, dtype=jnp.int32)[None, None, :]
    inside = np.concatenate([np.arange(size) for size in STAGE_SIZES])[:, None]
    pair_codes = jnp.asarray(((inside * GROUP_ROWS + 2 * ranks) << 17) + ((inside * half + ranks) << 12), jnp.int32)
    code = jnp.where(rank & 1 == 0, pair_codes[:, :, None] + (event_ids << 6), event_ids).reshape(groups, half * events)
    longest = half * events // 2 + 4 * BATCH // 2
    lists = jnp.sum(
        jnp.where(spot[:, None, :] == jnp.arange(longest, dtype=jnp.int32)[None, :, None], code[:, None, :], 0), axis=2
    )
    counts = jnp.sum(rounded, axis=1).astype(jnp.int32)

    column = jnp.where(pair_list < events, pair_list, events + GROUP_ROWS * arrival + entry)
    column = jnp.pad(column, ((0, 0), (0, SLOT_ROWS - slots)), constant_values=-1).reshape(-1)
    cand_ids = jnp.arange(cands, dtype=jnp.int32)
    hot = (column[:, None] == cand_ids[None, :]).astype(BF16)
    hot_turned = (cand_ids[:, None] == column[None, :]).astype(BF16)
    mask = station_mask.transpose(1, 0, 2).reshape(slots * events, stations)
    owner_rows = [jnp.asarray(np.where(np.arange(cands) < events, np.arange(cands), -1), jnp.int32)]
    hot_sent = sent[:, None] == jnp.arange(groups, dtype=jnp.int32)[None, :]
    rows_sent = jnp.sum(jnp.where(hot_sent[:, :, None], exports[None], 0), axis=1)
    for g in range(groups):
        start = events + GROUP_ROWS * g
        owner_rows.append(jnp.pad(rows_sent[g], (start, cands - start - cap), constant_values=-1))
    owners = jnp.concatenate(owner_rows)[:, None] == (jnp.arange(128, dtype=jnp.int32) % events)[None, :]
    owners = owners.astype(BF16)

    tables, tails, begin = [], [], 0
    for size in STAGE_SIZES:
        if tables:
            lists, tables[-1] = lax.optimization_barrier((lists, tables[-1]))
        table_part, tail_part = call(
            functools.partial(import_kernel, begin, size, freq, events, cap, scale),
            [((events * size * GROUP_ROWS, 128), F32), ((size * 2 * GROUP_ROWS, 128), BF16)],
            (lists, counts, *got[begin : begin + size], dup, square, energy, table),
            scratch=weight_scratch(size * half, freq),
            specs=[smem] * 2 + vmem(size + 4),
            micros=1.0 + 2.3 * size,
        )
        tables.append(table_part)
        tails.append(tail_part)
        begin += size

    message_rows = -(-(slots + 1) // 8) * 8
    place = lax.axis_index("sta").astype(jnp.int32).reshape(1)
    *shares, weights, geo, own = call(
        functools.partial(slots_kernel, events, slots),
        [((message_rows, 128), F32)] * 4
        + [((events * SLOT_ROWS, 128), BF16), ((cands, 256), BF16), ((events, 128), F32)],
        (place, hot, mask, partials, local, *tables, *tails),
        scratch=[pltpu.VMEM((2 * events, 128), F32), pltpu.VMEM((16 * events, 128), F32)],
        specs=[smem] + vmem(4 + 2 * len(STAGE_SIZES)),
        micros=3.0,
    )
    shares = [shares[0]] + [lax.ppermute(shares[d], "sta", [(i, i ^ d) for i in range(4)]) for d in range(1, 4)]
    (terms,) = call(
        functools.partial(terms_kernel, events),
        [((4, clusters, 8, 128), F32)],
        (hot_turned, weights, geo, own),
    )
    terms = lax.all_to_all(
        terms.reshape(4 * clusters, 8, 128), ("sta", "clu"), split_axis=0, concat_axis=0, tiled=True
    )
    sources = jnp.stack([me] + [jnp.asarray(receiver(g, me), jnp.int32) for g in range(groups)])
    normal, right = call(
        functools.partial(total_kernel, groups, events, slots),
        [((4, events, slots + 1), F32), ((1, events), F32)],
        (sources, *shares, terms, owners),
        specs=[smem] + vmem(6),
    )
    return (normal.transpose(0, 2, 1), right)


def solution(mesh):
    return jax.shard_map(
        on_device,
        mesh=mesh,
        in_specs=(
            P("clu", "sta", None),
            P("clu", None, "sta"),
            P("clu", None),
            P("clu", None, "sta"),
            P("clu", None),
        ),
        out_specs=(P("sta", None, "clu"), P("sta", "clu")),
        check_vma=False,
    )
```

```python
import functools
import math

import jax
import jax.numpy as jnp
import numpy as np
from jax import lax
from jax.experimental import pallas as pl
from jax.experimental.pallas import tpu as pltpu
from jax.sharding import PartitionSpec as P

F32 = jnp.float32
BF16 = jnp.bfloat16
VMEM_LIMIT = 24 * 1024 * 1024
SLOT_ROWS = 64
GROUP_ROWS = 16
BATCH = 8
WIDE = 4
UNROLL = 8
STAGE_SIZES = (2, 2, 2)


def moment_table(freq_count):
    f = np.arange(freq_count)

    def edge(k):
        out = np.zeros(k.shape)
        live = (k % (2 * freq_count)) != 0
        sign = 1.0 - 2.0 * (k[live] % 2)
        out[live] = -freq_count * sign / np.tan(np.pi * k[live] / (2 * freq_count))
        return out

    table = np.zeros((freq_count + 16, freq_count), np.float32)
    table[:freq_count] = -(edge(f[:, None] + f[None, :]) + edge(f[None, :] - f[:, None]))
    table[freq_count] = (1.0 - 2.0 * (f % 2)) * f * math.pi / freq_count
    return jnp.asarray(table, F32).astype(BF16)


def low_half(shape):
    return lax.broadcasted_iota(jnp.int32, shape, len(shape) - 1) < shape[-1] // 2


def outgoing_kernel(cap, send_group, exports_ref, spec_ref, geo_ref, *refs):
    outs, rows = refs[:-1], refs[-1]
    stations = spec_ref.shape[1]
    body = cap * stations
    rows[...] = jnp.zeros_like(rows)
    for g, out in enumerate(outs):
        h = send_group(g, lax.axis_index("clu"))
        for c in range(cap):
            event = exports_ref[h, c]
            out[c * stations : (c + 1) * stations, :] = spec_ref[event]
            place = c
            geo = geo_ref[event].astype(F32)
            rows[place : place + 1, :] = jnp.concatenate([geo[0:1], geo[1:2]], axis=1)
            place += GROUP_ROWS
            rows[place : place + 1, :] = jnp.concatenate([geo[2:3], geo[3:4]], axis=1)
        out[body : body + 2 * GROUP_ROWS, :] = rows[...].astype(BF16)


def fold(x):
    rows = x.shape[0] // 8
    total = x[0:8]
    for r in range(1, rows):
        total = total + x[8 * r : 8 * r + 8]
    return total


def prepare(natural, bp, bb, eb, pairs, freq):
    for j in range(pairs):
        turned = natural(j).astype(F32).T
        bp[j] = turned
        re, im = turned[:freq], turned[freq:]
        square = re * re + im * im
        bb[j] = square
        eb[j : j + 1, :] = jnp.sum(square, axis=0, keepdims=True)


def listed_pairs(fetch, batches, da, sq, ea, bp, bb, eb, table, work, store, freq, scale):
    xs, reals, rm, rs, rt, rb, rz, re = work
    lead = lax.broadcasted_iota(jnp.int32, (8, 1), 0) == 0
    step = lax.broadcasted_iota(jnp.int32, (8, 1), 0).astype(F32)
    low = low_half((8, 128))
    unit = (math.pi / freq) ** 2

    def split(t, d):
        code = fetch(t * (BATCH // 2) + d)
        return (code >> 12) & 31, code >> 17, ((code >> 6) & 63, code & 63)

    def cross_stage(t, slot):
        for d in range(BATCH // 2):
            j, _, duo = split(t, d)
            squares, sums = [[], []], [None, None]
            for v in range(0, freq, 16):
                br, bi = bp[j, v : v + 16, :], bp[j, freq + v : freq + v + 16, :]
                b2 = bb[j, v : v + 16, :]
                for i, e in enumerate(duo):
                    ar, ai = da[e, v : v + 16, :], da[e, freq + v : freq + v + 16, :]
                    cr = ar * br + ai * bi
                    ci = ai * br - ar * bi
                    both = sq[e, v : v + 16, :] * b2
                    u = 2 * d + i
                    lanes = slice(u * 128, (u + 1) * 128)
                    xs[slot, v : v + 16, lanes] = ci.astype(BF16)
                    reals[slot, v : v + 16, lanes] = cr.astype(BF16)
                    squares[i] += [both[:8], both[8:]]
                    part = cr[:8] + cr[8:]
                    sums[i] = part if v == 0 else sums[i] + part
                    if v == 0:
                        edge = cr[:8] * cr[:8] - ci[:8] * ci[:8]
                        rs[slot, u * 8 : u * 8 + 8, :] = jnp.where(lead, edge, 0.0)
            for i, e in enumerate(duo):
                u = 2 * d + i
                rows = slice(u * 8, u * 8 + 8)
                zero, one, two = squares[i][-1], squares[i][-1], squares[i][-1]
                for v in range(freq // 8 - 2, 0, -1):
                    zero = zero + squares[i][v]
                    one = one + zero
                    two = two + one
                zero = zero + squares[i][0]
                rs[slot, rows, :] += zero
                rb[slot, rows, :] = unit * (64.0 * (2.0 * two - one) + step * (16.0 * one + step * zero))
                rt[slot, rows, :] = sums[i]
                re[slot, u : u + 1, :] = ea[pl.ds(e, 1), :] * eb[pl.ds(j, 1), :]

    def moment_stage(slot):
        for start in range(0, BATCH, WIDE):
            lanes = slice(start * 128, (start + WIDE) * 128)
            z = jnp.dot(table[...], xs[slot, :, lanes], preferred_element_type=F32)
            for i in range(WIDE):
                part = z[:, i * 128 : (i + 1) * 128]
                real = reals[slot, :, (start + i) * 128 : (start + i + 1) * 128].astype(F32)
                rows = slice((start + i) * 8, (start + i + 1) * 8)
                rm[slot, rows, :] = fold(real * part[:freq])
                rz[slot, rows, :] = part[freq : freq + 8]

    def finish_stage(t, slot):
        def pick(ref, k):
            return ref[slot, pl.ds(k, 8, stride=8), :]

        moment, total, alternate, bend = pick(rm, 0), pick(rs, 0), pick(rt, 0), pick(rb, 0)
        for k in range(1, 8):
            moment = moment + pick(rm, k)
            total = total + pick(rs, k)
            bend = bend + pick(rb, k)
            alternate = alternate + pick(rt, k) if k % 2 == 0 else alternate - pick(rt, k)
        tilt = pick(rz, 0)
        inverse = 1.0 / (re[slot] + 1e-06)
        power = (freq * total - alternate * alternate) * inverse
        rough = (freq * bend - tilt * tilt) * inverse
        weight = power / (power + 0.125 * rough + 1e-06) * scale
        moved = weight * (moment * inverse / (power + 1e-06))
        even = jnp.where(low, weight, pltpu.roll(moved, 64, 1))
        odd = jnp.where(low, pltpu.roll(weight, 64, 1), moved)
        return even, odd

    def put(t, even, odd):
        for d in range(BATCH // 2):
            _, column, duo = split(t, d)
            for i, e in enumerate(duo):
                u = 2 * d + i
                store(e, column, even[u : u + 1], odd[u : u + 1])

    cross_stage(0, 0)
    moment_stage(0)
    cross_stage(1, 1)

    @pl.loop(0, (batches + 1) // 2)
    def _(i):
        first = finish_stage(2 * i, 0)
        cross_stage(2 * i + 2, 0)
        moment_stage(1)
        second = finish_stage(2 * i + 1, 1)
        cross_stage(2 * i + 3, 1)
        moment_stage(0)
        put(2 * i, *first)
        put(2 * i + 1, *second)


def local_kernel(freq, events, scale, batches, ids, spec_ref, table, out, da, sq, ea, bp, bb, eb, *work):
    pairs = events // 2
    prepare(lambda j: spec_ref[j], bp, bb, eb, pairs, freq)
    low = low_half((128, 128))
    for j in range(pairs):
        both = bp[j]
        other = pltpu.roll(both, 64, 1)
        da[2 * j] = jnp.where(low, both, other)
        da[2 * j + 1] = jnp.where(low, other, both)
        both = bb[j]
        other = pltpu.roll(both, 64, 1)
        sq[2 * j] = jnp.where(low[:freq], both, other)
        sq[2 * j + 1] = jnp.where(low[:freq], other, both)
    energy = eb[...]
    other = pltpu.roll(energy, 64, 1)
    low = low_half(energy.shape)
    ea[pl.ds(0, pairs, stride=2), :] = jnp.where(low, energy, other)
    ea[pl.ds(1, pairs, stride=2), :] = jnp.where(low, other, energy)
    row = low_half((1, 128))

    def store(e, column, even, odd):
        out[pl.ds(e * events + column, 1), :] = even
        out[pl.ds(e * events + column + 1, 1), :] = odd
        out[pl.ds(column * events + e, 1), :] = jnp.where(row, even, -even)
        out[pl.ds((column + 1) * events + e, 1), :] = jnp.where(row, odd, -odd)

    listed_pairs(lambda n: ids[n], batches, da, sq, ea, bp, bb, eb, table, work, store, freq, scale)


def import_kernel(begin, arrivals, freq, events, cap, scale, ids, counts, *refs):
    got, (da, sq, ea, table, out, tail, bp, bb, eb), work = refs[:arrivals], refs[arrivals : arrivals + 9], refs[arrivals + 9 :]
    pairs = cap // 2

    def natural(j):
        return got[j // pairs][j % pairs * 128 : (j % pairs + 1) * 128, :]

    prepare(natural, bp, bb, eb, arrivals * pairs, freq)
    out[...] = jnp.zeros_like(out)
    for g in range(arrivals):
        tail[2 * GROUP_ROWS * g : 2 * GROUP_ROWS * (g + 1), :] = got[g][pairs * 128 :, :]

    def store(e, column, even, odd):
        out[pl.ds(e * arrivals * GROUP_ROWS + column, 1), :] = even
        out[pl.ds(e * arrivals * GROUP_ROWS + column + 1, 1), :] = odd

    ends = [counts[begin]]
    for g in range(1, arrivals):
        ends.append(ends[-1] + counts[begin + g])

    def fetch(n):
        group, start = 0, 0
        for end in ends[:-1]:
            group = group + jnp.where(n >= end, 1, 0)
            start = jnp.where(n >= end, end, start)
        return ids[begin + group, n - start]

    batches = (ends[-1] + BATCH // 2 - 1) // (BATCH // 2)
    listed_pairs(fetch, batches, da, sq, ea, bp, bb, eb, table, work, store, freq, scale)


def weight_scratch(pairs, freq):
    return (
        [
            pltpu.VMEM((pairs, 2 * freq, 128), F32),
            pltpu.VMEM((pairs, freq, 128), F32),
            pltpu.VMEM((-(-pairs // 8) * 8, 128), F32),
            pltpu.VMEM((2, freq, BATCH * 128), BF16),
            pltpu.VMEM((2, freq, BATCH * 128), BF16),
        ]
        + [pltpu.VMEM((2, BATCH * 8, 128), F32)] * 5
        + [pltpu.VMEM((2, BATCH, 128), F32)]
    )


def two_parts(x):
    high = x.astype(BF16)
    return high, (x - high.astype(F32)).astype(BF16)


def sums_kernel(groups, events, slots, hot, hot_turned, mask, partials, *refs):
    stages = len(STAGE_SIZES)
    tables, tails = refs[: stages + 1], refs[stages + 1 : 2 * stages + 1]
    slots_out, terms_out, geo_out, own, own_geo = refs[2 * stages + 1 :]
    cands = hot.shape[1]
    rest = jnp.zeros((SLOT_ROWS - slots, 128), F32)

    @pl.loop(0, events // UNROLL)
    def _(step):
        for u in range(UNROLL):
            e = step * UNROLL + u
            parts = [tables[0][pl.ds(pl.multiple_of(e * events, 8), events), :]]
            for t, size in zip(tables[1:], STAGE_SIZES):
                rows = size * GROUP_ROWS
                parts.append(t[pl.ds(pl.multiple_of(e * rows, 8), rows), :])
            every = jnp.concatenate(parts, axis=0).astype(BF16)
            rows = pl.ds(pl.multiple_of(e * SLOT_ROWS, SLOT_ROWS), SLOT_ROWS)
            live = mask[pl.ds(e, slots, stride=events), :].astype(F32)
            live = jnp.concatenate([jnp.concatenate([live, live], axis=1), rest], axis=0)
            picked = jnp.dot(hot[rows, :], every, preferred_element_type=F32) * live
            slots_out[rows, :] = picked.astype(BF16)
            own[pl.ds(e, 1), :] = jnp.sum(picked, axis=0, keepdims=True)
            geo = partials[e].astype(F32)
            own_geo[pl.ds(e, 1), :] = jnp.concatenate([geo[0:1], geo[1:2]], axis=1)
            own_geo[pl.ds(events + e, 1), :] = jnp.concatenate([geo[2:3], geo[3:4]], axis=1)

    gathered = jnp.dot(hot_turned[...], slots_out[...], preferred_element_type=F32)
    low = low_half((cands, 128))
    gathered = jnp.where(low, gathered, -gathered)
    totals = jnp.concatenate([gathered[:events] + own[...], gathered[events:]], axis=0)
    turned = pltpu.roll(totals, 64, 1)
    weights = jnp.where(low, totals, turned)
    moves = jnp.where(low, turned, totals)
    ends = [t[start : start + 2 * GROUP_ROWS, :] for t in tails for start in range(0, t.shape[0], 2 * GROUP_ROWS)]
    first = jnp.concatenate([own_geo[:events].astype(BF16)] + [t[:GROUP_ROWS] for t in ends], axis=0)
    second = jnp.concatenate([own_geo[events:].astype(BF16)] + [t[GROUP_ROWS:] for t in ends], axis=0)
    geo_out[:, :128] = first
    geo_out[:, 128:] = second
    blocks = [first.astype(F32), second.astype(F32)]
    singles = []
    for block in blocks:
        other = pltpu.roll(block, 64, 1)
        singles += [jnp.where(low, block, other), jnp.where(low, other, block)]
    half_row = lax.broadcasted_iota(jnp.int32, (8, 128), 0)
    half_lane = lax.broadcasted_iota(jnp.int32, (8, 128), 1) // 64
    picker = jnp.where(half_row == half_lane, 1.0, 0.0).astype(BF16)
    picker = jnp.concatenate([picker, picker], axis=1)

    def halves(values):
        both = jnp.concatenate(two_parts(values), axis=1)
        return lax.dot_general(picker, both, (((1,), (1,)), ((), ())), preferred_element_type=F32)[:2]

    rights = [halves(moves * blocks[0]), halves(moves * blocks[1])]
    for i in range(4):
        scaled = weights * singles[i]
        rows = [halves(scaled * blocks[0]), halves(scaled * blocks[1]), rights[i // 2][i % 2 : i % 2 + 1]]
        share = jnp.concatenate(rows + [jnp.zeros((3, 128), F32)], axis=0)
        for q in range(terms_out.shape[1]):
            terms_out[i, q] = share


def blocks_kernel(events, place, hot, slots, geo, partials, *refs):
    outs, turned = refs[:-1], refs[-1]
    turned[...] = jnp.zeros_like(turned)
    low = low_half((SLOT_ROWS, 128))
    column = lax.broadcasted_iota(jnp.int32, (16, 128), 0) % 4
    block = lax.broadcasted_iota(jnp.int32, (16, 128), 1) // 64

    @pl.loop(0, events // UNROLL)
    def _(step):
        for u in range(UNROLL):
            e = step * UNROLL + u
            rows = pl.ds(pl.multiple_of(e * SLOT_ROWS, SLOT_ROWS), SLOT_ROWS)
            partner = jnp.dot(hot[rows, :], geo[...], preferred_element_type=F32)
            pair = slots[rows, :].astype(F32)
            weights = jnp.where(low, pair, pltpu.roll(pair, 64, 1))
            weighted = jnp.concatenate([weights * partner[:, :128], weights * partner[:, 128:]], axis=1).astype(BF16)
            own = partials[e].astype(F32)
            own = jnp.concatenate([own, own], axis=1)
            own = jnp.concatenate([jnp.broadcast_to(-own[i : i + 1], (4, 128)) for i in range(4)], axis=0)
            left = [jnp.where(column == block, own, 0.0), jnp.where(column == block + 2, own, 0.0)]
            left = jnp.concatenate(left, axis=1).astype(BF16)
            entry = lax.dot_general(left, weighted, (((1,), (1,)), ((), ())), preferred_element_type=F32)
            turned[pl.ds(e, 16, stride=events), 0:SLOT_ROWS] = entry

    for d, out in enumerate(outs):
        share = place[0] ^ d
        rows = pl.ds(pl.multiple_of(share * 4 * events, 128), 4 * events)
        out[...] = turned[rows, :].T[: out.shape[0]]


def total_kernel(groups, events, slots, clusters, own, one, two, three, received, owners, normal, right):
    parts = []
    for g in range(groups + 1):
        part = received[clusters[g]]
        for t in range(1, 4):
            part = part + received[t * (received.shape[0] // 4) + clusters[g]]
        parts.append(part)
    high, low = two_parts(jnp.concatenate(parts, axis=1))
    spread = jnp.dot(high, owners[...], preferred_element_type=F32) + jnp.dot(low, owners[...], preferred_element_type=F32)
    block = lax.broadcasted_iota(jnp.int32, (1, 128), 1) // events
    diagonal = jnp.zeros((1, 128), F32)
    for j in range(4):
        diagonal = jnp.where(block == j, spread[j : j + 1], diagonal)
    right[...] = spread[4:5, :events]
    total = pltpu.roll((own[...] + one[...]) + (two[...] + three[...]), 1, 0)
    top = lax.broadcasted_iota(jnp.int32, total.shape, 0) == 0
    total = jnp.where(top, diagonal, total)
    turned = total.T
    for j in range(4):
        normal[j] = turned[j * events : (j + 1) * events, : slots + 1]


def vmem(n):
    return [pl.BlockSpec(memory_space=pltpu.VMEM)] * n


def call(kernel, outs, inputs, scratch=(), specs=None, micros=1.0, limit=VMEM_LIMIT):
    shapes = [jax.ShapeDtypeStruct(s, t) for s, t in outs]
    return pl.pallas_call(
        kernel,
        out_shape=shapes,
        in_specs=specs if specs is not None else vmem(len(inputs)),
        out_specs=vmem(len(outs)),
        scratch_shapes=list(scratch),
        compiler_params=pltpu.CompilerParams(vmem_limit_bytes=limit),
        cost_estimate=pl.CostEstimate(flops=int(micros * 1e9), bytes_accessed=1024, transcendentals=0),
    )(*inputs)


def on_device(spectra, partials, pair_list, station_mask, exports):
    events, stations, two_freq = spectra.shape
    freq = two_freq // 2
    groups, cap = exports.shape
    half_span = groups // 2
    slots = pair_list.shape[1]
    sta_groups = lax.axis_size("sta")
    scale = 1.0 / (stations * sta_groups)
    offsets = [h - half_span + (1 if h >= half_span else 0) for h in range(groups)]
    cands = events + groups * GROUP_ROWS
    half = cap // 2
    table = moment_table(freq)
    smem = pl.BlockSpec(memory_space=pltpu.SMEM)
    clusters = lax.axis_size("clu")

    paired = clusters == groups + 2 and clusters & (clusters - 1) == 0
    if paired:
        masks = [m for m in range(1, clusters) if m != clusters // 2]
        routes = [[(i, i ^ m) for i in range(clusters)] for m in masks]
    else:
        order = sorted(range(groups), key=lambda h: abs(offsets[h]))
        routes = [[(i, (i + offsets[h]) % clusters) for i in range(clusters)] for h in order]

    def group_of(offset):
        offset = offset & (clusters - 1)
        return jnp.where(offset < clusters // 2, offset + half_span - 1, offset - clusters + half_span)

    def send_group(g, p):
        return group_of((p ^ masks[g]) - p) if paired else order[g]

    def receive_group(g, p):
        return group_of(p - (p ^ masks[g])) if paired else order[g]

    def receiver(g, p):
        return p ^ masks[g] if paired else (p + offsets[order[g]]) % clusters

    out_rows = cap * stations + 2 * GROUP_ROWS
    outgoing = call(
        functools.partial(outgoing_kernel, cap, send_group),
        [((out_rows, 128), BF16)] * groups,
        (exports, spectra, partials),
        scratch=[pltpu.VMEM((2 * GROUP_ROWS, 128), F32)],
        specs=[smem] + vmem(2),
        micros=2.0,
        limit=60 * 1024 * 1024,
    )
    got = [None] * groups
    for g in [0] + list(range(groups - 1, 0, -1)):
        got[g] = lax.ppermute(outgoing[g], "clu", routes[g])
    me = lax.axis_index("clu").astype(jnp.int32)
    sent = jnp.stack([jnp.asarray(send_group(g, me), jnp.int32) for g in range(groups)])
    came = jnp.stack([jnp.asarray(receive_group(g, me), jnp.int32) for g in range(groups)])

    duos = [j << 18 | j << 12 | e << 6 | e + 1 for j in range(events // 2) for e in range(0, 2 * j + 2, 2)]
    batches = -(-len(duos) // BATCH) * 2
    duos = duos + [1] * ((batches + 3) * (BATCH // 2) - len(duos))
    natural, got[0] = lax.optimization_barrier((spectra, got[0]))
    local, dup, square, energy = call(
        functools.partial(local_kernel, freq, events, scale, batches),
        [
            ((events * events, 128), F32),
            ((events, 128, 128), F32),
            ((events, freq, 128), F32),
            ((events, 128), F32),
        ],
        (jnp.asarray(duos, jnp.int32), natural.reshape(events // 2, 2 * stations, two_freq), table),
        scratch=weight_scratch(events // 2, freq),
        specs=[smem] + vmem(2),
        micros=8.0,
    )

    far = jnp.maximum(pair_list - events, 0)
    far_group = far // cap
    arrival = jnp.sum(jnp.where(far_group[:, :, None] == came[None, None, :], jnp.arange(groups, dtype=jnp.int32), 0), axis=2)
    entry = far % cap
    named = jnp.where(pair_list < events, -1, arrival * half + entry // 2)
    wanted = jnp.any(named[:, :, None] == jnp.arange(groups * half, dtype=jnp.int32)[None, None, :], axis=1)
    wanted = wanted.astype(F32).T.reshape(groups, half, events)
    ranks = np.arange(events)
    rank = jnp.einsum("gje,ef->gjf", wanted, jnp.asarray(ranks[:, None] < ranks[None, :], F32))
    rounded = jnp.ceil(jnp.sum(wanted, axis=2) * 0.5)
    ranks = np.arange(half)
    start = jnp.sum(rounded[:, :, None] * jnp.asarray(ranks[:, None] < ranks[None, :], F32)[None], axis=1)
    rank = rank.astype(jnp.int32)
    spot = jnp.where(wanted > 0, start.astype(jnp.int32)[:, :, None] + (rank >> 1), -1).reshape(groups, half * events)
    event_ids = jnp.arange(events, dtype=jnp.int32)[None, None, :]
    inside = np.concatenate([np.arange(size) for size in STAGE_SIZES])[:, None]
    pair_codes = jnp.asarray(((inside * GROUP_ROWS + 2 * ranks) << 17) + ((inside * half + ranks) << 12), jnp.int32)
    code = jnp.where(rank & 1 == 0, pair_codes[:, :, None] + (event_ids << 6), event_ids).reshape(groups, half * events)
    longest = half * events // 2 + 4 * BATCH // 2
    lists = jnp.sum(
        jnp.where(spot[:, None, :] == jnp.arange(longest, dtype=jnp.int32)[None, :, None], code[:, None, :], 0), axis=2
    )
    counts = jnp.sum(rounded, axis=1).astype(jnp.int32)

    column = jnp.where(pair_list < events, pair_list, events + GROUP_ROWS * arrival + entry)
    column = jnp.pad(column, ((0, 0), (0, SLOT_ROWS - slots)), constant_values=-1).reshape(-1)
    cand_ids = jnp.arange(cands, dtype=jnp.int32)
    hot = (column[:, None] == cand_ids[None, :]).astype(BF16)
    hot_turned = (cand_ids[:, None] == column[None, :]).astype(BF16)
    mask = station_mask.transpose(1, 0, 2).reshape(slots * events, stations)
    owner_rows = [jnp.asarray(np.where(np.arange(cands) < events, np.arange(cands), -1), jnp.int32)]
    hot_sent = sent[:, None] == jnp.arange(groups, dtype=jnp.int32)[None, :]
    rows_sent = jnp.sum(jnp.where(hot_sent[:, :, None], exports[None], 0), axis=1)
    for g in range(groups):
        start = events + GROUP_ROWS * g
        owner_rows.append(jnp.pad(rows_sent[g], (start, cands - start - cap), constant_values=-1))
    owners = jnp.concatenate(owner_rows)[:, None] == (jnp.arange(128, dtype=jnp.int32) % events)[None, :]
    owners = owners.astype(BF16)

    tables, tails, begin = [], [], 0
    for size in STAGE_SIZES:
        if tables:
            lists, tables[-1] = lax.optimization_barrier((lists, tables[-1]))
        table_part, tail_part = call(
            functools.partial(import_kernel, begin, size, freq, events, cap, scale),
            [((events * size * GROUP_ROWS, 128), F32), ((size * 2 * GROUP_ROWS, 128), BF16)],
            (lists, counts, *got[begin : begin + size], dup, square, energy, table),
            scratch=weight_scratch(size * half, freq),
            specs=[smem] * 2 + vmem(size + 4),
            micros=1.0 + 2.3 * size,
        )
        tables.append(table_part)
        tails.append(tail_part)
        begin += size

    weights, terms, geo = call(
        functools.partial(sums_kernel, groups, events, slots),
        [((events * SLOT_ROWS, 128), BF16), ((4, clusters, 8, 128), F32), ((cands, 256), BF16)],
        (hot, hot_turned, mask, partials, local, *tables, *tails),
        scratch=[pltpu.VMEM((events, 128), F32), pltpu.VMEM((2 * events, 128), F32)],
        micros=2.4,
    )
    message_rows = -(-(slots + 1) // 8) * 8
    place = lax.axis_index("sta").astype(jnp.int32).reshape(1)
    shares = call(
        functools.partial(blocks_kernel, events),
        [((message_rows, 128), F32)] * 4,
        (place, hot, weights, geo, partials),
        scratch=[pltpu.VMEM((16 * events, 128), F32)],
        specs=[smem] + vmem(4),
        micros=1.7,
    )
    shares = [shares[0]] + [lax.ppermute(shares[d], "sta", [(i, i ^ d) for i in range(4)]) for d in range(1, 4)]
    terms, shares[1] = lax.optimization_barrier((terms, shares[1]))
    terms = lax.all_to_all(
        terms.reshape(4 * clusters, 8, 128), ("sta", "clu"), split_axis=0, concat_axis=0, tiled=True
    )
    sources = jnp.stack([me] + [jnp.asarray(receiver(g, me), jnp.int32) for g in range(groups)])
    normal, right = call(
        functools.partial(total_kernel, groups, events, slots),
        [((4, events, slots + 1), F32), ((1, events), F32)],
        (sources, *shares, terms, owners),
        specs=[smem] + vmem(6),
    )
    return (normal.transpose(0, 2, 1), right)


def solution(mesh):
    return jax.shard_map(
        on_device,
        mesh=mesh,
        in_specs=(
            P("clu", "sta", None),
            P("clu", None, "sta"),
            P("clu", None),
            P("clu", None, "sta"),
            P("clu", None),
        ),
        out_specs=(P("sta", None, "clu"), P("sta", "clu")),
        check_vma=False,
    )
```

```python
import functools
import math

import jax
import jax.numpy as jnp
import numpy as np
from jax import lax
from jax.experimental import pallas as pl
from jax.experimental.pallas import tpu as pltpu
from jax.sharding import PartitionSpec as P

F32 = jnp.float32
BF16 = jnp.bfloat16
VMEM_LIMIT = 24 * 1024 * 1024
SLOT_ROWS = 64
GROUP_ROWS = 16
BATCH = 8
WIDE = 4
UNROLL = 8
STAGE_SIZES = (2, 2, 2)
LATE = 2


def moment_table(freq_count):
    f = np.arange(freq_count)

    def edge(k):
        out = np.zeros(k.shape)
        live = (k % (2 * freq_count)) != 0
        sign = 1.0 - 2.0 * (k[live] % 2)
        out[live] = -freq_count * sign / np.tan(np.pi * k[live] / (2 * freq_count))
        return out

    table = np.zeros((freq_count + 16, freq_count), np.float32)
    table[:freq_count] = -(edge(f[:, None] + f[None, :]) + edge(f[None, :] - f[:, None]))
    table[freq_count] = (1.0 - 2.0 * (f % 2)) * f * math.pi / freq_count
    return jnp.asarray(table, F32).astype(BF16)


def low_half(shape):
    return lax.broadcasted_iota(jnp.int32, shape, len(shape) - 1) < shape[-1] // 2


def outgoing_kernel(cap, send_group, exports_ref, spec_ref, geo_ref, *refs):
    outs, rows = refs[:-1], refs[-1]
    stations = spec_ref.shape[1]
    body = cap * stations
    rows[...] = jnp.zeros_like(rows)
    for g, out in enumerate(outs):
        h = send_group(g, lax.axis_index("clu"))
        for c in range(cap):
            event = exports_ref[h, c]
            out[c * stations : (c + 1) * stations, :] = spec_ref[event]
            place = c
            geo = geo_ref[event].astype(F32)
            rows[place : place + 1, :] = jnp.concatenate([geo[0:1], geo[1:2]], axis=1)
            place += GROUP_ROWS
            rows[place : place + 1, :] = jnp.concatenate([geo[2:3], geo[3:4]], axis=1)
        out[body : body + 2 * GROUP_ROWS, :] = rows[...].astype(BF16)


def fold(x):
    rows = x.shape[0] // 8
    total = x[0:8]
    for r in range(1, rows):
        total = total + x[8 * r : 8 * r + 8]
    return total


def prepare(natural, bp, bb, eb, pairs, freq):
    for j in range(pairs):
        turned = natural(j).astype(F32).T
        bp[j] = turned
        re, im = turned[:freq], turned[freq:]
        square = re * re + im * im
        bb[j] = square
        eb[j : j + 1, :] = jnp.sum(square, axis=0, keepdims=True)


def listed_pairs(fetch, batches, da, sq, ea, bp, bb, eb, table, work, store, freq, scale):
    xs, reals, rm, rs, rt, rb, rz, re = work
    lead = lax.broadcasted_iota(jnp.int32, (8, 1), 0) == 0
    step = lax.broadcasted_iota(jnp.int32, (8, 1), 0).astype(F32)
    low = low_half((8, 128))
    unit = (math.pi / freq) ** 2

    def split(t, d):
        code = fetch(t * (BATCH // 2) + d)
        return (code >> 12) & 31, code >> 17, ((code >> 6) & 63, code & 63)

    def cross_stage(t, slot):
        for d in range(BATCH // 2):
            j, _, duo = split(t, d)
            squares, sums = [[], []], [None, None]
            for v in range(0, freq, 16):
                br, bi = bp[j, v : v + 16, :], bp[j, freq + v : freq + v + 16, :]
                b2 = bb[j, v : v + 16, :]
                for i, e in enumerate(duo):
                    ar, ai = da[e, v : v + 16, :], da[e, freq + v : freq + v + 16, :]
                    cr = ar * br + ai * bi
                    ci = ai * br - ar * bi
                    both = sq[e, v : v + 16, :] * b2
                    u = 2 * d + i
                    lanes = slice(u * 128, (u + 1) * 128)
                    xs[slot, v : v + 16, lanes] = ci.astype(BF16)
                    reals[slot, v : v + 16, lanes] = cr.astype(BF16)
                    squares[i] += [both[:8], both[8:]]
                    part = cr[:8] + cr[8:]
                    sums[i] = part if v == 0 else sums[i] + part
                    if v == 0:
                        edge = cr[:8] * cr[:8] - ci[:8] * ci[:8]
                        rs[slot, u * 8 : u * 8 + 8, :] = jnp.where(lead, edge, 0.0)
            for i, e in enumerate(duo):
                u = 2 * d + i
                rows = slice(u * 8, u * 8 + 8)
                zero, one, two = squares[i][-1], squares[i][-1], squares[i][-1]
                for v in range(freq // 8 - 2, 0, -1):
                    zero = zero + squares[i][v]
                    one = one + zero
                    two = two + one
                zero = zero + squares[i][0]
                rs[slot, rows, :] += zero
                rb[slot, rows, :] = unit * (64.0 * (2.0 * two - one) + step * (16.0 * one + step * zero))
                rt[slot, rows, :] = sums[i]
                re[slot, u : u + 1, :] = ea[pl.ds(e, 1), :] * eb[pl.ds(j, 1), :]

    def moment_stage(slot):
        for start in range(0, BATCH, WIDE):
            lanes = slice(start * 128, (start + WIDE) * 128)
            z = jnp.dot(table[...], xs[slot, :, lanes], preferred_element_type=F32)
            for i in range(WIDE):
                part = z[:, i * 128 : (i + 1) * 128]
                real = reals[slot, :, (start + i) * 128 : (start + i + 1) * 128].astype(F32)
                rows = slice((start + i) * 8, (start + i + 1) * 8)
                rm[slot, rows, :] = fold(real * part[:freq])
                rz[slot, rows, :] = part[freq : freq + 8]

    def finish_stage(t, slot):
        def pick(ref, k):
            return ref[slot, pl.ds(k, 8, stride=8), :]

        moment, total, alternate, bend = pick(rm, 0), pick(rs, 0), pick(rt, 0), pick(rb, 0)
        for k in range(1, 8):
            moment = moment + pick(rm, k)
            total = total + pick(rs, k)
            bend = bend + pick(rb, k)
            alternate = alternate + pick(rt, k) if k % 2 == 0 else alternate - pick(rt, k)
        tilt = pick(rz, 0)
        inverse = 1.0 / (re[slot] + 1e-06)
        power = (freq * total - alternate * alternate) * inverse
        rough = (freq * bend - tilt * tilt) * inverse
        weight = power / (power + 0.125 * rough + 1e-06) * scale
        moved = weight * (moment * inverse / (power + 1e-06))
        even = jnp.where(low, weight, pltpu.roll(moved, 64, 1))
        odd = jnp.where(low, pltpu.roll(weight, 64, 1), moved)
        return even, odd

    def put(t, even, odd):
        for d in range(BATCH // 2):
            _, column, duo = split(t, d)
            for i, e in enumerate(duo):
                u = 2 * d + i
                store(e, column, even[u : u + 1], odd[u : u + 1])

    cross_stage(0, 0)
    moment_stage(0)
    cross_stage(1, 1)

    @pl.loop(0, (batches + 1) // 2)
    def _(i):
        first = finish_stage(2 * i, 0)
        cross_stage(2 * i + 2, 0)
        moment_stage(1)
        second = finish_stage(2 * i + 1, 1)
        cross_stage(2 * i + 3, 1)
        moment_stage(0)
        put(2 * i, *first)
        put(2 * i + 1, *second)


def local_kernel(freq, events, scale, batches, ids, spec_ref, table, out, da, sq, ea, bp, bb, eb, *work):
    pairs = events // 2
    prepare(lambda j: spec_ref[j], bp, bb, eb, pairs, freq)
    low = low_half((128, 128))
    for j in range(pairs):
        both = bp[j]
        other = pltpu.roll(both, 64, 1)
        da[2 * j] = jnp.where(low, both, other)
        da[2 * j + 1] = jnp.where(low, other, both)
        both = bb[j]
        other = pltpu.roll(both, 64, 1)
        sq[2 * j] = jnp.where(low[:freq], both, other)
        sq[2 * j + 1] = jnp.where(low[:freq], other, both)
    energy = eb[...]
    other = pltpu.roll(energy, 64, 1)
    low = low_half(energy.shape)
    ea[pl.ds(0, pairs, stride=2), :] = jnp.where(low, energy, other)
    ea[pl.ds(1, pairs, stride=2), :] = jnp.where(low, other, energy)
    row = low_half((1, 128))

    def store(e, column, even, odd):
        out[pl.ds(e * events + column, 1), :] = even
        out[pl.ds(e * events + column + 1, 1), :] = odd
        out[pl.ds(column * events + e, 1), :] = jnp.where(row, even, -even)
        out[pl.ds((column + 1) * events + e, 1), :] = jnp.where(row, odd, -odd)

    listed_pairs(lambda n: ids[n], batches, da, sq, ea, bp, bb, eb, table, work, store, freq, scale)


def import_kernel(begin, arrivals, freq, events, cap, scale, ids, counts, *refs):
    got, (da, sq, ea, table, out, tail, bp, bb, eb), work = refs[:arrivals], refs[arrivals : arrivals + 9], refs[arrivals + 9 :]
    pairs = cap // 2

    def natural(j):
        return got[j // pairs][j % pairs * 128 : (j % pairs + 1) * 128, :]

    prepare(natural, bp, bb, eb, arrivals * pairs, freq)
    out[...] = jnp.zeros_like(out)
    for g in range(arrivals):
        tail[2 * GROUP_ROWS * g : 2 * GROUP_ROWS * (g + 1), :] = got[g][pairs * 128 :, :]

    def store(e, column, even, odd):
        out[pl.ds(e * arrivals * GROUP_ROWS + column, 1), :] = even
        out[pl.ds(e * arrivals * GROUP_ROWS + column + 1, 1), :] = odd

    ends = [counts[begin]]
    for g in range(1, arrivals):
        ends.append(ends[-1] + counts[begin + g])

    def fetch(n):
        group, start = 0, 0
        for end in ends[:-1]:
            group = group + jnp.where(n >= end, 1, 0)
            start = jnp.where(n >= end, end, start)
        return ids[begin + group, n - start]

    batches = (ends[-1] + BATCH // 2 - 1) // (BATCH // 2)
    listed_pairs(fetch, batches, da, sq, ea, bp, bb, eb, table, work, store, freq, scale)


def weight_scratch(pairs, freq):
    return (
        [
            pltpu.VMEM((pairs, 2 * freq, 128), F32),
            pltpu.VMEM((pairs, freq, 128), F32),
            pltpu.VMEM((-(-pairs // 8) * 8, 128), F32),
            pltpu.VMEM((2, freq, BATCH * 128), BF16),
            pltpu.VMEM((2, freq, BATCH * 128), BF16),
        ]
        + [pltpu.VMEM((2, BATCH * 8, 128), F32)] * 5
        + [pltpu.VMEM((2, BATCH, 128), F32)]
    )


def two_parts(x):
    high = x.astype(BF16)
    return high, (x - high.astype(F32)).astype(BF16)


def sums_kernel(groups, events, slots, hot, hot_turned, mask, partials, *refs):
    stages = len(STAGE_SIZES)
    tables, tails = refs[: stages + 1], refs[stages + 1 : 2 * stages + 1]
    slots_out, terms_out, geo_out, own, own_geo = refs[2 * stages + 1 :]
    cands = hot.shape[1]
    rest = jnp.zeros((SLOT_ROWS - slots, 128), F32)

    @pl.loop(0, events // UNROLL)
    def _(step):
        for u in range(UNROLL):
            e = step * UNROLL + u
            parts = [tables[0][pl.ds(pl.multiple_of(e * events, 8), events), :]]
            for t, size in zip(tables[1:], STAGE_SIZES):
                rows = size * GROUP_ROWS
                parts.append(t[pl.ds(pl.multiple_of(e * rows, 8), rows), :])
            every = jnp.concatenate(parts, axis=0).astype(BF16)
            rows = pl.ds(pl.multiple_of(e * SLOT_ROWS, SLOT_ROWS), SLOT_ROWS)
            live = mask[pl.ds(e, slots, stride=events), :].astype(F32)
            live = jnp.concatenate([jnp.concatenate([live, live], axis=1), rest], axis=0)
            picked = jnp.dot(hot[rows, :], every, preferred_element_type=F32) * live
            slots_out[rows, :] = picked.astype(BF16)
            own[pl.ds(e, 1), :] = jnp.sum(picked, axis=0, keepdims=True)
            geo = partials[e].astype(F32)
            own_geo[pl.ds(e, 1), :] = jnp.concatenate([geo[0:1], geo[1:2]], axis=1)
            own_geo[pl.ds(events + e, 1), :] = jnp.concatenate([geo[2:3], geo[3:4]], axis=1)

    gathered = jnp.dot(hot_turned[...], slots_out[...], preferred_element_type=F32)
    low = low_half((cands, 128))
    gathered = jnp.where(low, gathered, -gathered)
    totals = jnp.concatenate([gathered[:events] + own[...], gathered[events:]], axis=0)
    turned = pltpu.roll(totals, 64, 1)
    weights = jnp.where(low, totals, turned)
    moves = jnp.where(low, turned, totals)
    ends = [t[start : start + 2 * GROUP_ROWS, :] for t in tails for start in range(0, t.shape[0], 2 * GROUP_ROWS)]
    first = jnp.concatenate([own_geo[:events].astype(BF16)] + [t[:GROUP_ROWS] for t in ends], axis=0)
    second = jnp.concatenate([own_geo[events:].astype(BF16)] + [t[GROUP_ROWS:] for t in ends], axis=0)
    geo_out[:, :128] = first
    geo_out[:, 128:] = second
    blocks = [first.astype(F32), second.astype(F32)]
    singles = []
    for block in blocks:
        other = pltpu.roll(block, 64, 1)
        singles += [jnp.where(low, block, other), jnp.where(low, other, block)]
    half_row = lax.broadcasted_iota(jnp.int32, (8, 128), 0)
    half_lane = lax.broadcasted_iota(jnp.int32, (8, 128), 1) // 64
    picker = jnp.where(half_row == half_lane, 1.0, 0.0).astype(BF16)
    picker = jnp.concatenate([picker, picker], axis=1)

    def halves(values):
        both = jnp.concatenate(two_parts(values), axis=1)
        return lax.dot_general(picker, both, (((1,), (1,)), ((), ())), preferred_element_type=F32)[:2]

    rights = [halves(moves * blocks[0]), halves(moves * blocks[1])]
    for i in range(4):
        scaled = weights * singles[i]
        rows = [halves(scaled * blocks[0]), halves(scaled * blocks[1]), rights[i // 2][i % 2 : i % 2 + 1]]
        share = jnp.concatenate(rows + [jnp.zeros((3, 128), F32)], axis=0)
        for q in range(terms_out.shape[1]):
            terms_out[i, q] = share


def blocks_kernel(events, place, hot, slots, geo, partials, *refs):
    outs, turned = refs[:-1], refs[-1]
    turned[...] = jnp.zeros_like(turned)
    low = low_half((SLOT_ROWS, 128))
    column = lax.broadcasted_iota(jnp.int32, (16, 128), 0) % 4
    block = lax.broadcasted_iota(jnp.int32, (16, 128), 1) // 64

    @pl.loop(0, events // UNROLL)
    def _(step):
        for u in range(UNROLL):
            e = step * UNROLL + u
            rows = pl.ds(pl.multiple_of(e * SLOT_ROWS, SLOT_ROWS), SLOT_ROWS)
            partner = jnp.dot(hot[rows, :], geo[...], preferred_element_type=F32)
            pair = slots[rows, :].astype(F32)
            weights = jnp.where(low, pair, pltpu.roll(pair, 64, 1))
            weighted = jnp.concatenate([weights * partner[:, :128], weights * partner[:, 128:]], axis=1).astype(BF16)
            own = partials[e].astype(F32)
            own = jnp.concatenate([own, own], axis=1)
            own = jnp.concatenate([jnp.broadcast_to(-own[i : i + 1], (4, 128)) for i in range(4)], axis=0)
            left = [jnp.where(column == block, own, 0.0), jnp.where(column == block + 2, own, 0.0)]
            left = jnp.concatenate(left, axis=1).astype(BF16)
            entry = lax.dot_general(left, weighted, (((1,), (1,)), ((), ())), preferred_element_type=F32)
            turned[pl.ds(e, 16, stride=events), 0:SLOT_ROWS] = entry

    for d, out in enumerate(outs):
        share = place[0] ^ d
        rows = pl.ds(pl.multiple_of(share * 4 * events, 128), 4 * events)
        out[...] = turned[rows, :].T[: out.shape[0]]


def total_kernel(groups, events, slots, clusters, own, one, two, three, received, owners, normal, right):
    parts = []
    for g in range(groups + 1):
        part = received[clusters[g]]
        for t in range(1, 4):
            part = part + received[t * (received.shape[0] // 4) + clusters[g]]
        parts.append(part)
    high, low = two_parts(jnp.concatenate(parts, axis=1))
    spread = jnp.dot(high, owners[...], preferred_element_type=F32) + jnp.dot(low, owners[...], preferred_element_type=F32)
    block = lax.broadcasted_iota(jnp.int32, (1, 128), 1) // events
    diagonal = jnp.zeros((1, 128), F32)
    for j in range(4):
        diagonal = jnp.where(block == j, spread[j : j + 1], diagonal)
    right[...] = spread[4:5, :events]
    total = pltpu.roll((own[...] + one[...]) + (two[...] + three[...]), 1, 0)
    top = lax.broadcasted_iota(jnp.int32, total.shape, 0) == 0
    total = jnp.where(top, diagonal, total)
    turned = total.T
    for j in range(4):
        normal[j] = turned[j * events : (j + 1) * events, : slots + 1]


def vmem(n):
    return [pl.BlockSpec(memory_space=pltpu.VMEM)] * n


def call(kernel, outs, inputs, scratch=(), specs=None, micros=1.0, limit=VMEM_LIMIT):
    shapes = [jax.ShapeDtypeStruct(s, t) for s, t in outs]
    return pl.pallas_call(
        kernel,
        out_shape=shapes,
        in_specs=specs if specs is not None else vmem(len(inputs)),
        out_specs=vmem(len(outs)),
        scratch_shapes=list(scratch),
        compiler_params=pltpu.CompilerParams(vmem_limit_bytes=limit),
        cost_estimate=pl.CostEstimate(flops=int(micros * 1e9), bytes_accessed=1024, transcendentals=0),
    )(*inputs)


def on_device(spectra, partials, pair_list, station_mask, exports):
    events, stations, two_freq = spectra.shape
    freq = two_freq // 2
    groups, cap = exports.shape
    half_span = groups // 2
    slots = pair_list.shape[1]
    sta_groups = lax.axis_size("sta")
    scale = 1.0 / (stations * sta_groups)
    offsets = [h - half_span + (1 if h >= half_span else 0) for h in range(groups)]
    cands = events + groups * GROUP_ROWS
    half = cap // 2
    table = moment_table(freq)
    smem = pl.BlockSpec(memory_space=pltpu.SMEM)
    clusters = lax.axis_size("clu")

    paired = clusters == groups + 2 and clusters & (clusters - 1) == 0
    if paired:
        masks = [m for m in range(1, clusters) if m != clusters // 2]
        routes = [[(i, i ^ m) for i in range(clusters)] for m in masks]
    else:
        order = sorted(range(groups), key=lambda h: abs(offsets[h]))
        routes = [[(i, (i + offsets[h]) % clusters) for i in range(clusters)] for h in order]

    def group_of(offset):
        offset = offset & (clusters - 1)
        return jnp.where(offset < clusters // 2, offset + half_span - 1, offset - clusters + half_span)

    def send_group(g, p):
        return group_of((p ^ masks[g]) - p) if paired else order[g]

    def receive_group(g, p):
        return group_of(p - (p ^ masks[g])) if paired else order[g]

    def receiver(g, p):
        return p ^ masks[g] if paired else (p + offsets[order[g]]) % clusters

    out_rows = cap * stations + 2 * GROUP_ROWS
    outgoing = call(
        functools.partial(outgoing_kernel, cap, send_group),
        [((out_rows, 128), BF16)] * groups,
        (exports, spectra, partials),
        scratch=[pltpu.VMEM((2 * GROUP_ROWS, 128), F32)],
        specs=[smem] + vmem(2),
        micros=2.0,
        limit=60 * 1024 * 1024,
    )
    got = [None] * groups
    for g in [0] + list(range(groups - 1, 0, -1)):
        block = outgoing[g]
        if g == LATE:
            block, got[0] = lax.optimization_barrier((block, got[0]))
        got[g] = lax.ppermute(block, "clu", routes[g])
    me = lax.axis_index("clu").astype(jnp.int32)
    sent = jnp.stack([jnp.asarray(send_group(g, me), jnp.int32) for g in range(groups)])
    came = jnp.stack([jnp.asarray(receive_group(g, me), jnp.int32) for g in range(groups)])

    duos = [j << 18 | j << 12 | e << 6 | e + 1 for j in range(events // 2) for e in range(0, 2 * j + 2, 2)]
    batches = -(-len(duos) // BATCH) * 2
    duos = duos + [1] * ((batches + 3) * (BATCH // 2) - len(duos))
    natural, got[0] = lax.optimization_barrier((spectra, got[0]))
    local, dup, square, energy = call(
        functools.partial(local_kernel, freq, events, scale, batches),
        [
            ((events * events, 128), F32),
            ((events, 128, 128), F32),
            ((events, freq, 128), F32),
            ((events, 128), F32),
        ],
        (jnp.asarray(duos, jnp.int32), natural.reshape(events // 2, 2 * stations, two_freq), table),
        scratch=weight_scratch(events // 2, freq),
        specs=[smem] + vmem(2),
        micros=8.0,
    )

    far = jnp.maximum(pair_list - events, 0)
    far_group = far // cap
    arrival = jnp.sum(jnp.where(far_group[:, :, None] == came[None, None, :], jnp.arange(groups, dtype=jnp.int32), 0), axis=2)
    entry = far % cap
    named = jnp.where(pair_list < events, -1, arrival * half + entry // 2)
    wanted = jnp.any(named[:, :, None] == jnp.arange(groups * half, dtype=jnp.int32)[None, None, :], axis=1)
    wanted = wanted.astype(F32).T.reshape(groups, half, events)
    ranks = np.arange(events)
    rank = jnp.einsum("gje,ef->gjf", wanted, jnp.asarray(ranks[:, None] < ranks[None, :], F32))
    rounded = jnp.ceil(jnp.sum(wanted, axis=2) * 0.5)
    ranks = np.arange(half)
    start = jnp.sum(rounded[:, :, None] * jnp.asarray(ranks[:, None] < ranks[None, :], F32)[None], axis=1)
    rank = rank.astype(jnp.int32)
    spot = jnp.where(wanted > 0, start.astype(jnp.int32)[:, :, None] + (rank >> 1), -1).reshape(groups, half * events)
    event_ids = jnp.arange(events, dtype=jnp.int32)[None, None, :]
    inside = np.concatenate([np.arange(size) for size in STAGE_SIZES])[:, None]
    pair_codes = jnp.asarray(((inside * GROUP_ROWS + 2 * ranks) << 17) + ((inside * half + ranks) << 12), jnp.int32)
    code = jnp.where(rank & 1 == 0, pair_codes[:, :, None] + (event_ids << 6), event_ids).reshape(groups, half * events)
    longest = half * events // 2 + 4 * BATCH // 2
    lists = jnp.sum(
        jnp.where(spot[:, None, :] == jnp.arange(longest, dtype=jnp.int32)[None, :, None], code[:, None, :], 0), axis=2
    )
    counts = jnp.sum(rounded, axis=1).astype(jnp.int32)

    column = jnp.where(pair_list < events, pair_list, events + GROUP_ROWS * arrival + entry)
    column = jnp.pad(column, ((0, 0), (0, SLOT_ROWS - slots)), constant_values=-1).reshape(-1)
    cand_ids = jnp.arange(cands, dtype=jnp.int32)
    hot = (column[:, None] == cand_ids[None, :]).astype(BF16)
    hot_turned = (cand_ids[:, None] == column[None, :]).astype(BF16)
    mask = station_mask.transpose(1, 0, 2).reshape(slots * events, stations)
    owner_rows = [jnp.asarray(np.where(np.arange(cands) < events, np.arange(cands), -1), jnp.int32)]
    hot_sent = sent[:, None] == jnp.arange(groups, dtype=jnp.int32)[None, :]
    rows_sent = jnp.sum(jnp.where(hot_sent[:, :, None], exports[None], 0), axis=1)
    for g in range(groups):
        start = events + GROUP_ROWS * g
        owner_rows.append(jnp.pad(rows_sent[g], (start, cands - start - cap), constant_values=-1))
    owners = jnp.concatenate(owner_rows)[:, None] == (jnp.arange(128, dtype=jnp.int32) % events)[None, :]
    owners = owners.astype(BF16)

    tables, tails, begin = [], [], 0
    for size in STAGE_SIZES:
        if tables:
            lists, tables[-1] = lax.optimization_barrier((lists, tables[-1]))
        table_part, tail_part = call(
            functools.partial(import_kernel, begin, size, freq, events, cap, scale),
            [((events * size * GROUP_ROWS, 128), F32), ((size * 2 * GROUP_ROWS, 128), BF16)],
            (lists, counts, *got[begin : begin + size], dup, square, energy, table),
            scratch=weight_scratch(size * half, freq),
            specs=[smem] * 2 + vmem(size + 4),
            micros=1.0 + 2.3 * size,
        )
        tables.append(table_part)
        tails.append(tail_part)
        begin += size

    weights, terms, geo = call(
        functools.partial(sums_kernel, groups, events, slots),
        [((events * SLOT_ROWS, 128), BF16), ((4, clusters, 8, 128), F32), ((cands, 256), BF16)],
        (hot, hot_turned, mask, partials, local, *tables, *tails),
        scratch=[pltpu.VMEM((events, 128), F32), pltpu.VMEM((2 * events, 128), F32)],
        micros=2.4,
    )
    message_rows = -(-(slots + 1) // 8) * 8
    place = lax.axis_index("sta").astype(jnp.int32).reshape(1)
    shares = call(
        functools.partial(blocks_kernel, events),
        [((message_rows, 128), F32)] * 4,
        (place, hot, weights, geo, partials),
        scratch=[pltpu.VMEM((16 * events, 128), F32)],
        specs=[smem] + vmem(4),
        micros=1.7,
    )
    shares = [shares[0]] + [lax.ppermute(shares[d], "sta", [(i, i ^ d) for i in range(4)]) for d in range(1, 4)]
    terms = lax.all_to_all(
        terms.reshape(4 * clusters, 8, 128), ("sta", "clu"), split_axis=0, concat_axis=0, tiled=True
    )
    sources = jnp.stack([me] + [jnp.asarray(receiver(g, me), jnp.int32) for g in range(groups)])
    normal, right = call(
        functools.partial(total_kernel, groups, events, slots),
        [((4, events, slots + 1), F32), ((1, events), F32)],
        (sources, *shares, terms, owners),
        specs=[smem] + vmem(6),
    )
    return (normal.transpose(0, 2, 1), right)


def solution(mesh):
    return jax.shard_map(
        on_device,
        mesh=mesh,
        in_specs=(
            P("clu", "sta", None),
            P("clu", None, "sta"),
            P("clu", None),
            P("clu", None, "sta"),
            P("clu", None),
        ),
        out_specs=(P("sta", None, "clu"), P("sta", "clu")),
        check_vma=False,
    )
```

```python
import functools
import math

import jax
import jax.numpy as jnp
import numpy as np
from jax import lax
from jax.experimental import pallas as pl
from jax.experimental.pallas import tpu as pltpu
from jax.sharding import PartitionSpec as P

F32 = jnp.float32
BF16 = jnp.bfloat16
VMEM_LIMIT = 24 * 1024 * 1024
SLOT_ROWS = 64
GROUP_ROWS = 16
BATCH = 8
WIDE = 4
UNROLL = 8
STAGE_SIZES = (2, 2, 2)
LATE = 2


def moment_table(freq_count):
    f = np.arange(freq_count)

    def edge(k):
        out = np.zeros(k.shape)
        live = (k % (2 * freq_count)) != 0
        sign = 1.0 - 2.0 * (k[live] % 2)
        out[live] = -freq_count * sign / np.tan(np.pi * k[live] / (2 * freq_count))
        return out

    table = np.zeros((freq_count + 16, freq_count), np.float32)
    table[:freq_count] = -(edge(f[:, None] + f[None, :]) + edge(f[None, :] - f[:, None]))
    table[freq_count] = (1.0 - 2.0 * (f % 2)) * f * math.pi / freq_count
    return jnp.asarray(table, F32).astype(BF16)


def low_half(shape):
    return lax.broadcasted_iota(jnp.int32, shape, len(shape) - 1) < shape[-1] // 2


def outgoing_kernel(cap, send_group, exports_ref, spec_ref, geo_ref, *refs):
    outs, rows = refs[:-1], refs[-1]
    stations = spec_ref.shape[1]
    body = cap * stations
    rows[...] = jnp.zeros_like(rows)
    for g, out in enumerate(outs):
        h = send_group(g, lax.axis_index("clu"))
        for c in range(cap):
            event = exports_ref[h, c]
            out[c * stations : (c + 1) * stations, :] = spec_ref[event]
            place = c
            geo = geo_ref[event].astype(F32)
            rows[place : place + 1, :] = jnp.concatenate([geo[0:1], geo[1:2]], axis=1)
            place += GROUP_ROWS
            rows[place : place + 1, :] = jnp.concatenate([geo[2:3], geo[3:4]], axis=1)
        out[body : body + 2 * GROUP_ROWS, :] = rows[...].astype(BF16)


def fold(x):
    rows = x.shape[0] // 8
    total = x[0:8]
    for r in range(1, rows):
        total = total + x[8 * r : 8 * r + 8]
    return total


def prepare(natural, bp, bb, eb, pairs, freq):
    for j in range(pairs):
        turned = natural(j).astype(F32).T
        bp[j] = turned
        re, im = turned[:freq], turned[freq:]
        square = re * re + im * im
        bb[j] = square
        eb[j : j + 1, :] = jnp.sum(square, axis=0, keepdims=True)


def listed_pairs(fetch, batches, da, sq, ea, bp, bb, eb, table, work, store, freq, scale):
    xs, reals, rm, rs, rt, rb, rz, re = work
    lead = lax.broadcasted_iota(jnp.int32, (8, 1), 0) == 0
    step = lax.broadcasted_iota(jnp.int32, (8, 1), 0).astype(F32)
    low = low_half((8, 128))
    unit = (math.pi / freq) ** 2

    def split(t, d):
        code = fetch(t * (BATCH // 2) + d)
        return (code >> 12) & 31, code >> 17, ((code >> 6) & 63, code & 63)

    def cross_stage(t, slot):
        for d in range(BATCH // 2):
            j, _, duo = split(t, d)
            squares, sums = [[], []], [None, None]
            for v in range(0, freq, 16):
                br, bi = bp[j, v : v + 16, :], bp[j, freq + v : freq + v + 16, :]
                b2 = bb[j, v : v + 16, :]
                for i, e in enumerate(duo):
                    ar, ai = da[e, v : v + 16, :], da[e, freq + v : freq + v + 16, :]
                    cr = ar * br + ai * bi
                    ci = ai * br - ar * bi
                    both = sq[e, v : v + 16, :] * b2
                    u = 2 * d + i
                    lanes = slice(u * 128, (u + 1) * 128)
                    xs[slot, v : v + 16, lanes] = ci.astype(BF16)
                    reals[slot, v : v + 16, lanes] = cr.astype(BF16)
                    squares[i] += [both[:8], both[8:]]
                    part = cr[:8] + cr[8:]
                    sums[i] = part if v == 0 else sums[i] + part
                    if v == 0:
                        edge = cr[:8] * cr[:8] - ci[:8] * ci[:8]
                        rs[slot, u * 8 : u * 8 + 8, :] = jnp.where(lead, edge, 0.0)
            for i, e in enumerate(duo):
                u = 2 * d + i
                rows = slice(u * 8, u * 8 + 8)
                zero, one, two = squares[i][-1], squares[i][-1], squares[i][-1]
                for v in range(freq // 8 - 2, 0, -1):
                    zero = zero + squares[i][v]
                    one = one + zero
                    two = two + one
                zero = zero + squares[i][0]
                rs[slot, rows, :] += zero
                rb[slot, rows, :] = unit * (64.0 * (2.0 * two - one) + step * (16.0 * one + step * zero))
                rt[slot, rows, :] = sums[i]
                re[slot, u : u + 1, :] = ea[pl.ds(e, 1), :] * eb[pl.ds(j, 1), :]

    def moment_stage(slot):
        for start in range(0, BATCH, WIDE):
            lanes = slice(start * 128, (start + WIDE) * 128)
            z = jnp.dot(table[...], xs[slot, :, lanes], preferred_element_type=F32)
            for i in range(WIDE):
                part = z[:, i * 128 : (i + 1) * 128]
                real = reals[slot, :, (start + i) * 128 : (start + i + 1) * 128].astype(F32)
                rows = slice((start + i) * 8, (start + i + 1) * 8)
                rm[slot, rows, :] = fold(real * part[:freq])
                rz[slot, rows, :] = part[freq : freq + 8]

    def finish_stage(t, slot):
        def pick(ref, k):
            return ref[slot, pl.ds(k, 8, stride=8), :]

        moment, total, alternate, bend = pick(rm, 0), pick(rs, 0), pick(rt, 0), pick(rb, 0)
        for k in range(1, 8):
            moment = moment + pick(rm, k)
            total = total + pick(rs, k)
            bend = bend + pick(rb, k)
            alternate = alternate + pick(rt, k) if k % 2 == 0 else alternate - pick(rt, k)
        tilt = pick(rz, 0)
        inverse = 1.0 / (re[slot] + 1e-06)
        power = (freq * total - alternate * alternate) * inverse
        rough = (freq * bend - tilt * tilt) * inverse
        weight = power / (power + 0.125 * rough + 1e-06) * scale
        moved = weight * (moment * inverse / (power + 1e-06))
        even = jnp.where(low, weight, pltpu.roll(moved, 64, 1))
        odd = jnp.where(low, pltpu.roll(weight, 64, 1), moved)
        return even, odd

    def put(t, even, odd):
        for d in range(BATCH // 2):
            _, column, duo = split(t, d)
            for i, e in enumerate(duo):
                u = 2 * d + i
                store(e, column, even[u : u + 1], odd[u : u + 1])

    cross_stage(0, 0)
    moment_stage(0)
    cross_stage(1, 1)

    @pl.loop(0, (batches + 1) // 2)
    def _(i):
        first = finish_stage(2 * i, 0)
        cross_stage(2 * i + 2, 0)
        moment_stage(1)
        second = finish_stage(2 * i + 1, 1)
        cross_stage(2 * i + 3, 1)
        moment_stage(0)
        put(2 * i, *first)
        put(2 * i + 1, *second)


def local_kernel(freq, events, scale, batches, ids, spec_ref, table, out, da, sq, ea, bp, bb, eb, *work):
    pairs = events // 2
    prepare(lambda j: spec_ref[j], bp, bb, eb, pairs, freq)
    low = low_half((128, 128))
    for j in range(pairs):
        both = bp[j]
        other = pltpu.roll(both, 64, 1)
        da[2 * j] = jnp.where(low, both, other)
        da[2 * j + 1] = jnp.where(low, other, both)
        both = bb[j]
        other = pltpu.roll(both, 64, 1)
        sq[2 * j] = jnp.where(low[:freq], both, other)
        sq[2 * j + 1] = jnp.where(low[:freq], other, both)
    energy = eb[...]
    other = pltpu.roll(energy, 64, 1)
    low = low_half(energy.shape)
    ea[pl.ds(0, pairs, stride=2), :] = jnp.where(low, energy, other)
    ea[pl.ds(1, pairs, stride=2), :] = jnp.where(low, other, energy)
    row = low_half((1, 128))

    def store(e, column, even, odd):
        out[pl.ds(e * events + column, 1), :] = even
        out[pl.ds(e * events + column + 1, 1), :] = odd
        out[pl.ds(column * events + e, 1), :] = jnp.where(row, even, -even)
        out[pl.ds((column + 1) * events + e, 1), :] = jnp.where(row, odd, -odd)

    listed_pairs(lambda n: ids[n], batches, da, sq, ea, bp, bb, eb, table, work, store, freq, scale)


def import_kernel(begin, arrivals, freq, events, cap, scale, ids, counts, *refs):
    got, (da, sq, ea, table, out, tail, bp, bb, eb), work = refs[:arrivals], refs[arrivals : arrivals + 9], refs[arrivals + 9 :]
    pairs = cap // 2

    def natural(j):
        return got[j // pairs][j % pairs * 128 : (j % pairs + 1) * 128, :]

    prepare(natural, bp, bb, eb, arrivals * pairs, freq)
    out[...] = jnp.zeros_like(out)
    for g in range(arrivals):
        tail[2 * GROUP_ROWS * g : 2 * GROUP_ROWS * (g + 1), :] = got[g][pairs * 128 :, :]

    def store(e, column, even, odd):
        out[pl.ds(e * arrivals * GROUP_ROWS + column, 1), :] = even
        out[pl.ds(e * arrivals * GROUP_ROWS + column + 1, 1), :] = odd

    ends = [counts[begin]]
    for g in range(1, arrivals):
        ends.append(ends[-1] + counts[begin + g])

    def fetch(n):
        group, start = 0, 0
        for end in ends[:-1]:
            group = group + jnp.where(n >= end, 1, 0)
            start = jnp.where(n >= end, end, start)
        return ids[begin + group, n - start]

    batches = (ends[-1] + BATCH // 2 - 1) // (BATCH // 2)
    listed_pairs(fetch, batches, da, sq, ea, bp, bb, eb, table, work, store, freq, scale)


def weight_scratch(pairs, freq):
    return (
        [
            pltpu.VMEM((pairs, 2 * freq, 128), F32),
            pltpu.VMEM((pairs, freq, 128), F32),
            pltpu.VMEM((-(-pairs // 8) * 8, 128), F32),
            pltpu.VMEM((2, freq, BATCH * 128), BF16),
            pltpu.VMEM((2, freq, BATCH * 128), BF16),
        ]
        + [pltpu.VMEM((2, BATCH * 8, 128), F32)] * 5
        + [pltpu.VMEM((2, BATCH, 128), F32)]
    )


def two_parts(x):
    high = x.astype(BF16)
    return high, (x - high.astype(F32)).astype(BF16)


def sums_kernel(groups, events, slots, hot, hot_turned, mask, partials, *refs):
    stages = len(STAGE_SIZES)
    tables, tails = refs[: stages + 1], refs[stages + 1 : 2 * stages + 1]
    slots_out, terms_out, geo_out, own, own_geo = refs[2 * stages + 1 :]
    cands = hot.shape[1]
    rest = jnp.zeros((SLOT_ROWS - slots, 128), F32)

    @pl.loop(0, events // UNROLL)
    def _(step):
        for u in range(UNROLL):
            e = step * UNROLL + u
            parts = [tables[0][pl.ds(pl.multiple_of(e * events, 8), events), :]]
            for t, size in zip(tables[1:], STAGE_SIZES):
                rows = size * GROUP_ROWS
                parts.append(t[pl.ds(pl.multiple_of(e * rows, 8), rows), :])
            every = jnp.concatenate(parts, axis=0).astype(BF16)
            rows = pl.ds(pl.multiple_of(e * SLOT_ROWS, SLOT_ROWS), SLOT_ROWS)
            live = mask[pl.ds(e, slots, stride=events), :].astype(F32)
            live = jnp.concatenate([jnp.concatenate([live, live], axis=1), rest], axis=0)
            picked = jnp.dot(hot[rows, :], every, preferred_element_type=F32) * live
            slots_out[rows, :] = picked.astype(BF16)
            own[pl.ds(e, 1), :] = jnp.sum(picked, axis=0, keepdims=True)
            geo = partials[e].astype(F32)
            own_geo[pl.ds(e, 1), :] = jnp.concatenate([geo[0:1], geo[1:2]], axis=1)
            own_geo[pl.ds(events + e, 1), :] = jnp.concatenate([geo[2:3], geo[3:4]], axis=1)

    gathered = jnp.dot(hot_turned[...], slots_out[...], preferred_element_type=F32)
    low = low_half((cands, 128))
    gathered = jnp.where(low, gathered, -gathered)
    totals = jnp.concatenate([gathered[:events] + own[...], gathered[events:]], axis=0)
    turned = pltpu.roll(totals, 64, 1)
    weights = jnp.where(low, totals, turned)
    moves = jnp.where(low, turned, totals)
    ends = [t[start : start + 2 * GROUP_ROWS, :] for t in tails for start in range(0, t.shape[0], 2 * GROUP_ROWS)]
    first = jnp.concatenate([own_geo[:events].astype(BF16)] + [t[:GROUP_ROWS] for t in ends], axis=0)
    second = jnp.concatenate([own_geo[events:].astype(BF16)] + [t[GROUP_ROWS:] for t in ends], axis=0)
    geo_out[:, :128] = first
    geo_out[:, 128:] = second
    blocks = [first.astype(F32), second.astype(F32)]
    singles = []
    for block in blocks:
        other = pltpu.roll(block, 64, 1)
        singles += [jnp.where(low, block, other), jnp.where(low, other, block)]
    half_row = lax.broadcasted_iota(jnp.int32, (8, 128), 0)
    half_lane = lax.broadcasted_iota(jnp.int32, (8, 128), 1) // 64
    picker = jnp.where(half_row == half_lane, 1.0, 0.0).astype(BF16)
    picker = jnp.concatenate([picker, picker], axis=1)

    def halves(values):
        both = jnp.concatenate(two_parts(values), axis=1)
        return lax.dot_general(picker, both, (((1,), (1,)), ((), ())), preferred_element_type=F32)[:2]

    rights = [halves(moves * blocks[0]), halves(moves * blocks[1])]
    for i in range(4):
        scaled = weights * singles[i]
        rows = [halves(scaled * blocks[0]), halves(scaled * blocks[1]), rights[i // 2][i % 2 : i % 2 + 1]]
        share = jnp.concatenate(rows + [jnp.zeros((3, 128), F32)], axis=0)
        for q in range(terms_out.shape[1]):
            terms_out[i, q] = share


def blocks_kernel(events, place, hot, slots, geo, partials, *refs):
    outs, turned = refs[:-1], refs[-1]
    turned[...] = jnp.zeros_like(turned)
    low = low_half((SLOT_ROWS, 128))
    column = lax.broadcasted_iota(jnp.int32, (16, 128), 0) % 4
    block = lax.broadcasted_iota(jnp.int32, (16, 128), 1) // 64

    @pl.loop(0, events // UNROLL)
    def _(step):
        for u in range(UNROLL):
            e = step * UNROLL + u
            rows = pl.ds(pl.multiple_of(e * SLOT_ROWS, SLOT_ROWS), SLOT_ROWS)
            partner = jnp.dot(hot[rows, :], geo[...], preferred_element_type=F32)
            pair = slots[rows, :].astype(F32)
            weights = jnp.where(low, pair, pltpu.roll(pair, 64, 1))
            weighted = jnp.concatenate([weights * partner[:, :128], weights * partner[:, 128:]], axis=1).astype(BF16)
            own = partials[e].astype(F32)
            own = jnp.concatenate([own, own], axis=1)
            own = jnp.concatenate([jnp.broadcast_to(-own[i : i + 1], (4, 128)) for i in range(4)], axis=0)
            left = [jnp.where(column == block, own, 0.0), jnp.where(column == block + 2, own, 0.0)]
            left = jnp.concatenate(left, axis=1).astype(BF16)
            entry = lax.dot_general(left, weighted, (((1,), (1,)), ((), ())), preferred_element_type=F32)
            turned[pl.ds(e, 16, stride=events), 0:SLOT_ROWS] = entry

    for d, out in enumerate(outs):
        share = place[0] ^ d
        rows = pl.ds(pl.multiple_of(share * 4 * events, 128), 4 * events)
        out[...] = turned[rows, :].T[: out.shape[0]]


def spread_kernel(groups, clusters, received, owners, out):
    parts = []
    for g in range(groups + 1):
        part = received[clusters[g]]
        for t in range(1, 4):
            part = part + received[t * (received.shape[0] // 4) + clusters[g]]
        parts.append(part)
    high, low = two_parts(jnp.concatenate(parts, axis=1))
    out[...] = jnp.dot(high, owners[...], preferred_element_type=F32) + jnp.dot(low, owners[...], preferred_element_type=F32)


def total_kernel(events, slots, own, one, two, three, spread, normal, right):
    block = lax.broadcasted_iota(jnp.int32, (1, 128), 1) // events
    diagonal = jnp.zeros((1, 128), F32)
    for j in range(4):
        diagonal = jnp.where(block == j, spread[j : j + 1, :], diagonal)
    right[...] = spread[4:5, :events]
    total = pltpu.roll((own[...] + one[...]) + (two[...] + three[...]), 1, 0)
    top = lax.broadcasted_iota(jnp.int32, total.shape, 0) == 0
    total = jnp.where(top, diagonal, total)
    turned = total.T
    for j in range(4):
        normal[j] = turned[j * events : (j + 1) * events, : slots + 1]


def vmem(n):
    return [pl.BlockSpec(memory_space=pltpu.VMEM)] * n


def call(kernel, outs, inputs, scratch=(), specs=None, micros=1.0, limit=VMEM_LIMIT):
    shapes = [jax.ShapeDtypeStruct(s, t) for s, t in outs]
    return pl.pallas_call(
        kernel,
        out_shape=shapes,
        in_specs=specs if specs is not None else vmem(len(inputs)),
        out_specs=vmem(len(outs)),
        scratch_shapes=list(scratch),
        compiler_params=pltpu.CompilerParams(vmem_limit_bytes=limit),
        cost_estimate=pl.CostEstimate(flops=int(micros * 1e9), bytes_accessed=1024, transcendentals=0),
    )(*inputs)


def on_device(spectra, partials, pair_list, station_mask, exports):
    events, stations, two_freq = spectra.shape
    freq = two_freq // 2
    groups, cap = exports.shape
    half_span = groups // 2
    slots = pair_list.shape[1]
    sta_groups = lax.axis_size("sta")
    scale = 1.0 / (stations * sta_groups)
    offsets = [h - half_span + (1 if h >= half_span else 0) for h in range(groups)]
    cands = events + groups * GROUP_ROWS
    half = cap // 2
    table = moment_table(freq)
    smem = pl.BlockSpec(memory_space=pltpu.SMEM)
    clusters = lax.axis_size("clu")

    paired = clusters == groups + 2 and clusters & (clusters - 1) == 0
    if paired:
        masks = [m for m in range(1, clusters) if m != clusters // 2]
        routes = [[(i, i ^ m) for i in range(clusters)] for m in masks]
    else:
        order = sorted(range(groups), key=lambda h: abs(offsets[h]))
        routes = [[(i, (i + offsets[h]) % clusters) for i in range(clusters)] for h in order]

    def group_of(offset):
        offset = offset & (clusters - 1)
        return jnp.where(offset < clusters // 2, offset + half_span - 1, offset - clusters + half_span)

    def send_group(g, p):
        return group_of((p ^ masks[g]) - p) if paired else order[g]

    def receive_group(g, p):
        return group_of(p - (p ^ masks[g])) if paired else order[g]

    def receiver(g, p):
        return p ^ masks[g] if paired else (p + offsets[order[g]]) % clusters

    out_rows = cap * stations + 2 * GROUP_ROWS
    outgoing = call(
        functools.partial(outgoing_kernel, cap, send_group),
        [((out_rows, 128), BF16)] * groups,
        (exports, spectra, partials),
        scratch=[pltpu.VMEM((2 * GROUP_ROWS, 128), F32)],
        specs=[smem] + vmem(2),
        micros=2.0,
        limit=60 * 1024 * 1024,
    )
    got = [None] * groups
    for g in [0] + list(range(groups - 1, 0, -1)):
        block = outgoing[g]
        if g == LATE:
            block, got[0] = lax.optimization_barrier((block, got[0]))
        got[g] = lax.ppermute(block, "clu", routes[g])
    me = lax.axis_index("clu").astype(jnp.int32)
    sent = jnp.stack([jnp.asarray(send_group(g, me), jnp.int32) for g in range(groups)])
    came = jnp.stack([jnp.asarray(receive_group(g, me), jnp.int32) for g in range(groups)])

    duos = [j << 18 | j << 12 | e << 6 | e + 1 for j in range(events // 2) for e in range(0, 2 * j + 2, 2)]
    batches = -(-len(duos) // BATCH) * 2
    duos = duos + [1] * ((batches + 3) * (BATCH // 2) - len(duos))
    natural, got[0] = lax.optimization_barrier((spectra, got[0]))
    local, dup, square, energy = call(
        functools.partial(local_kernel, freq, events, scale, batches),
        [
            ((events * events, 128), F32),
            ((events, 128, 128), F32),
            ((events, freq, 128), F32),
            ((events, 128), F32),
        ],
        (jnp.asarray(duos, jnp.int32), natural.reshape(events // 2, 2 * stations, two_freq), table),
        scratch=weight_scratch(events // 2, freq),
        specs=[smem] + vmem(2),
        micros=0.5,
    )

    far = jnp.maximum(pair_list - events, 0)
    far_group = far // cap
    arrival = jnp.sum(jnp.where(far_group[:, :, None] == came[None, None, :], jnp.arange(groups, dtype=jnp.int32), 0), axis=2)
    entry = far % cap
    named = jnp.where(pair_list < events, -1, arrival * half + entry // 2)
    wanted = jnp.any(named[:, :, None] == jnp.arange(groups * half, dtype=jnp.int32)[None, None, :], axis=1)
    wanted = wanted.astype(F32).T.reshape(groups, half, events)
    ranks = np.arange(events)
    rank = jnp.einsum("gje,ef->gjf", wanted, jnp.asarray(ranks[:, None] < ranks[None, :], F32))
    rounded = jnp.ceil(jnp.sum(wanted, axis=2) * 0.5)
    ranks = np.arange(half)
    start = jnp.sum(rounded[:, :, None] * jnp.asarray(ranks[:, None] < ranks[None, :], F32)[None], axis=1)
    rank = rank.astype(jnp.int32)
    spot = jnp.where(wanted > 0, start.astype(jnp.int32)[:, :, None] + (rank >> 1), -1).reshape(groups, half * events)
    event_ids = jnp.arange(events, dtype=jnp.int32)[None, None, :]
    inside = np.concatenate([np.arange(size) for size in STAGE_SIZES])[:, None]
    pair_codes = jnp.asarray(((inside * GROUP_ROWS + 2 * ranks) << 17) + ((inside * half + ranks) << 12), jnp.int32)
    code = jnp.where(rank & 1 == 0, pair_codes[:, :, None] + (event_ids << 6), event_ids).reshape(groups, half * events)
    longest = half * events // 2 + 4 * BATCH // 2
    lists = jnp.sum(
        jnp.where(spot[:, None, :] == jnp.arange(longest, dtype=jnp.int32)[None, :, None], code[:, None, :], 0), axis=2
    )
    counts = jnp.sum(rounded, axis=1).astype(jnp.int32)

    column = jnp.where(pair_list < events, pair_list, events + GROUP_ROWS * arrival + entry)
    column = jnp.pad(column, ((0, 0), (0, SLOT_ROWS - slots)), constant_values=-1).reshape(-1)
    mask = station_mask.transpose(1, 0, 2).reshape(slots * events, stations)
    owner_rows = [jnp.asarray(np.where(np.arange(cands) < events, np.arange(cands), -1), jnp.int32)]
    hot_sent = sent[:, None] == jnp.arange(groups, dtype=jnp.int32)[None, :]
    rows_sent = jnp.sum(jnp.where(hot_sent[:, :, None], exports[None], 0), axis=1)
    for g in range(groups):
        start = events + GROUP_ROWS * g
        owner_rows.append(jnp.pad(rows_sent[g], (start, cands - start - cap), constant_values=-1))
    owners = jnp.concatenate(owner_rows)[:, None] == (jnp.arange(128, dtype=jnp.int32) % events)[None, :]
    owners = owners.astype(BF16)

    tables, tails, begin = [], [], 0
    for size in STAGE_SIZES:
        if tables:
            lists, column, tables[-1] = lax.optimization_barrier((lists, column, tables[-1]))
        table_part, tail_part = call(
            functools.partial(import_kernel, begin, size, freq, events, cap, scale),
            [((events * size * GROUP_ROWS, 128), F32), ((size * 2 * GROUP_ROWS, 128), BF16)],
            (lists, counts, *got[begin : begin + size], dup, square, energy, table),
            scratch=weight_scratch(size * half, freq),
            specs=[smem] * 2 + vmem(size + 4),
            micros=0.5,
        )
        tables.append(table_part)
        tails.append(tail_part)
        begin += size

    cand_ids = jnp.arange(cands, dtype=jnp.int32)
    hot = (column[:, None] == cand_ids[None, :]).astype(BF16)
    hot_turned = (cand_ids[:, None] == column[None, :]).astype(BF16)
    weights, terms, geo = call(
        functools.partial(sums_kernel, groups, events, slots),
        [((events * SLOT_ROWS, 128), BF16), ((4, clusters, 8, 128), F32), ((cands, 256), BF16)],
        (hot, hot_turned, mask, partials, local, *tables, *tails),
        scratch=[pltpu.VMEM((events, 128), F32), pltpu.VMEM((2 * events, 128), F32)],
        micros=2.4,
    )
    message_rows = -(-(slots + 1) // 8) * 8
    place = lax.axis_index("sta").astype(jnp.int32).reshape(1)
    shares = call(
        functools.partial(blocks_kernel, events),
        [((message_rows, 128), F32)] * 4,
        (place, hot, weights, geo, partials),
        scratch=[pltpu.VMEM((16 * events, 128), F32)],
        specs=[smem] + vmem(4),
        micros=1.7,
    )
    shares = [shares[0]] + [lax.ppermute(shares[d], "sta", [(i, i ^ d) for i in range(4)]) for d in range(1, 4)]
    terms = lax.all_to_all(
        terms.reshape(4 * clusters, 8, 128), ("sta", "clu"), split_axis=0, concat_axis=0, tiled=True
    )
    sources = jnp.stack([me] + [jnp.asarray(receiver(g, me), jnp.int32) for g in range(groups)])
    (spread,) = call(
        functools.partial(spread_kernel, groups),
        [((8, 128), F32)],
        (sources, terms, owners),
        specs=[smem] + vmem(2),
    )
    normal, right = call(
        functools.partial(total_kernel, events, slots),
        [((4, events, slots + 1), F32), ((1, events), F32)],
        (*shares, spread),
    )
    return (normal.transpose(0, 2, 1), right)


def solution(mesh):
    return jax.shard_map(
        on_device,
        mesh=mesh,
        in_specs=(
            P("clu", "sta", None),
            P("clu", None, "sta"),
            P("clu", None),
            P("clu", None, "sta"),
            P("clu", None),
        ),
        out_specs=(P("sta", None, "clu"), P("sta", "clu")),
        check_vma=False,
    )
```

```python
import functools
import math

import jax
import jax.numpy as jnp
import numpy as np
from jax import lax
from jax.experimental import pallas as pl
from jax.experimental.pallas import tpu as pltpu
from jax.sharding import PartitionSpec as P

F32 = jnp.float32
BF16 = jnp.bfloat16
VMEM_LIMIT = 24 * 1024 * 1024
SLOT_ROWS = 64
GROUP_ROWS = 16
BATCH = 8
WIDE = 4
UNROLL = 8
STAGE_SIZES = (2, 2, 2)
LATE = 2


def moment_table(freq_count):
    f = np.arange(freq_count)

    def edge(k):
        out = np.zeros(k.shape)
        live = (k % (2 * freq_count)) != 0
        sign = 1.0 - 2.0 * (k[live] % 2)
        out[live] = -freq_count * sign / np.tan(np.pi * k[live] / (2 * freq_count))
        return out

    table = np.zeros((freq_count + 16, freq_count), np.float32)
    table[:freq_count] = -(edge(f[:, None] + f[None, :]) + edge(f[None, :] - f[:, None]))
    table[freq_count] = (1.0 - 2.0 * (f % 2)) * f * math.pi / freq_count
    return jnp.asarray(table, F32).astype(BF16)


def low_half(shape):
    return lax.broadcasted_iota(jnp.int32, shape, len(shape) - 1) < shape[-1] // 2


def outgoing_kernel(cap, send_group, exports_ref, spec_ref, geo_ref, *refs):
    outs, rows = refs[:-1], refs[-1]
    stations = spec_ref.shape[1]
    body = cap * stations
    rows[...] = jnp.zeros_like(rows)
    for g, out in enumerate(outs):
        h = send_group(g, lax.axis_index("clu"))
        for c in range(cap):
            event = exports_ref[h, c]
            out[c * stations : (c + 1) * stations, :] = spec_ref[event]
            place = c
            geo = geo_ref[event].astype(F32)
            rows[place : place + 1, :] = jnp.concatenate([geo[0:1], geo[1:2]], axis=1)
            place += GROUP_ROWS
            rows[place : place + 1, :] = jnp.concatenate([geo[2:3], geo[3:4]], axis=1)
        out[body : body + 2 * GROUP_ROWS, :] = rows[...].astype(BF16)


def fold(x):
    rows = x.shape[0] // 8
    total = x[0:8]
    for r in range(1, rows):
        total = total + x[8 * r : 8 * r + 8]
    return total


def prepare(natural, bp, bb, eb, pairs, freq):
    for j in range(pairs):
        turned = natural(j).astype(F32).T
        bp[j] = turned
        re, im = turned[:freq], turned[freq:]
        square = re * re + im * im
        bb[j] = square
        eb[j : j + 1, :] = jnp.sum(square, axis=0, keepdims=True)


def listed_pairs(fetch, batches, da, sq, ea, bp, bb, eb, table, work, store, freq, scale):
    xs, reals, rm, rs, rt, rb, rz, re = work
    lead = lax.broadcasted_iota(jnp.int32, (8, 1), 0) == 0
    step = lax.broadcasted_iota(jnp.int32, (8, 1), 0).astype(F32)
    low = low_half((8, 128))
    unit = (math.pi / freq) ** 2

    def split(t, d):
        code = fetch(t * (BATCH // 2) + d)
        return (code >> 12) & 31, code >> 17, ((code >> 6) & 63, code & 63)

    def cross_stage(t, slot):
        for d in range(BATCH // 2):
            j, _, duo = split(t, d)
            squares, sums = [[], []], [None, None]
            for v in range(0, freq, 16):
                br, bi = bp[j, v : v + 16, :], bp[j, freq + v : freq + v + 16, :]
                b2 = bb[j, v : v + 16, :]
                for i, e in enumerate(duo):
                    ar, ai = da[e, v : v + 16, :], da[e, freq + v : freq + v + 16, :]
                    cr = ar * br + ai * bi
                    ci = ai * br - ar * bi
                    both = sq[e, v : v + 16, :] * b2
                    u = 2 * d + i
                    lanes = slice(u * 128, (u + 1) * 128)
                    xs[slot, v : v + 16, lanes] = ci.astype(BF16)
                    reals[slot, v : v + 16, lanes] = cr.astype(BF16)
                    squares[i] += [both[:8], both[8:]]
                    part = cr[:8] + cr[8:]
                    sums[i] = part if v == 0 else sums[i] + part
                    if v == 0:
                        edge = cr[:8] * cr[:8] - ci[:8] * ci[:8]
                        rs[slot, u * 8 : u * 8 + 8, :] = jnp.where(lead, edge, 0.0)
            for i, e in enumerate(duo):
                u = 2 * d + i
                rows = slice(u * 8, u * 8 + 8)
                zero, one, two = squares[i][-1], squares[i][-1], squares[i][-1]
                for v in range(freq // 8 - 2, 0, -1):
                    zero = zero + squares[i][v]
                    one = one + zero
                    two = two + one
                zero = zero + squares[i][0]
                rs[slot, rows, :] += zero
                rb[slot, rows, :] = unit * (64.0 * (2.0 * two - one) + step * (16.0 * one + step * zero))
                rt[slot, rows, :] = sums[i]
                re[slot, u : u + 1, :] = ea[pl.ds(e, 1), :] * eb[pl.ds(j, 1), :]

    def moment_stage(slot):
        for start in range(0, BATCH, WIDE):
            lanes = slice(start * 128, (start + WIDE) * 128)
            z = jnp.dot(table[...], xs[slot, :, lanes], preferred_element_type=F32)
            for i in range(WIDE):
                part = z[:, i * 128 : (i + 1) * 128]
                real = reals[slot, :, (start + i) * 128 : (start + i + 1) * 128].astype(F32)
                rows = slice((start + i) * 8, (start + i + 1) * 8)
                rm[slot, rows, :] = fold(real * part[:freq])
                rz[slot, rows, :] = part[freq : freq + 8]

    def finish_stage(t, slot):
        def pick(ref, k):
            return ref[slot, pl.ds(k, 8, stride=8), :]

        moment, total, alternate, bend = pick(rm, 0), pick(rs, 0), pick(rt, 0), pick(rb, 0)
        for k in range(1, 8):
            moment = moment + pick(rm, k)
            total = total + pick(rs, k)
            bend = bend + pick(rb, k)
            alternate = alternate + pick(rt, k) if k % 2 == 0 else alternate - pick(rt, k)
        tilt = pick(rz, 0)
        inverse = 1.0 / (re[slot] + 1e-06)
        power = (freq * total - alternate * alternate) * inverse
        rough = (freq * bend - tilt * tilt) * inverse
        weight = power / (power + 0.125 * rough + 1e-06) * scale
        moved = weight * (moment * inverse / (power + 1e-06))
        even = jnp.where(low, weight, pltpu.roll(moved, 64, 1))
        odd = jnp.where(low, pltpu.roll(weight, 64, 1), moved)
        return even, odd

    def put(t, even, odd):
        for d in range(BATCH // 2):
            _, column, duo = split(t, d)
            for i, e in enumerate(duo):
                u = 2 * d + i
                store(e, column, even[u : u + 1], odd[u : u + 1])

    cross_stage(0, 0)
    moment_stage(0)
    cross_stage(1, 1)

    @pl.loop(0, (batches + 1) // 2)
    def _(i):
        first = finish_stage(2 * i, 0)
        cross_stage(2 * i + 2, 0)
        moment_stage(1)
        second = finish_stage(2 * i + 1, 1)
        cross_stage(2 * i + 3, 1)
        moment_stage(0)
        put(2 * i, *first)
        put(2 * i + 1, *second)


def local_kernel(freq, events, scale, batches, ids, spec_ref, table, out, da, sq, ea, bp, bb, eb, *work):
    pairs = events // 2
    prepare(lambda j: spec_ref[j], bp, bb, eb, pairs, freq)
    low = low_half((128, 128))
    for j in range(pairs):
        both = bp[j]
        other = pltpu.roll(both, 64, 1)
        da[2 * j] = jnp.where(low, both, other)
        da[2 * j + 1] = jnp.where(low, other, both)
        both = bb[j]
        other = pltpu.roll(both, 64, 1)
        sq[2 * j] = jnp.where(low[:freq], both, other)
        sq[2 * j + 1] = jnp.where(low[:freq], other, both)
    energy = eb[...]
    other = pltpu.roll(energy, 64, 1)
    low = low_half(energy.shape)
    ea[pl.ds(0, pairs, stride=2), :] = jnp.where(low, energy, other)
    ea[pl.ds(1, pairs, stride=2), :] = jnp.where(low, other, energy)
    row = low_half((1, 128))

    def store(e, column, even, odd):
        out[pl.ds(e * events + column, 1), :] = even
        out[pl.ds(e * events + column + 1, 1), :] = odd
        out[pl.ds(column * events + e, 1), :] = jnp.where(row, even, -even)
        out[pl.ds((column + 1) * events + e, 1), :] = jnp.where(row, odd, -odd)

    listed_pairs(lambda n: ids[n], batches, da, sq, ea, bp, bb, eb, table, work, store, freq, scale)


def import_kernel(begin, arrivals, freq, events, cap, scale, ids, counts, *refs):
    got, (da, sq, ea, table, out, tail, bp, bb, eb), work = refs[:arrivals], refs[arrivals : arrivals + 9], refs[arrivals + 9 :]
    pairs = cap // 2

    def natural(j):
        return got[j // pairs][j % pairs * 128 : (j % pairs + 1) * 128, :]

    prepare(natural, bp, bb, eb, arrivals * pairs, freq)
    out[...] = jnp.zeros_like(out)
    for g in range(arrivals):
        tail[2 * GROUP_ROWS * g : 2 * GROUP_ROWS * (g + 1), :] = got[g][pairs * 128 :, :]

    def store(e, column, even, odd):
        out[pl.ds(e * arrivals * GROUP_ROWS + column, 1), :] = even
        out[pl.ds(e * arrivals * GROUP_ROWS + column + 1, 1), :] = odd

    ends = [counts[begin]]
    for g in range(1, arrivals):
        ends.append(ends[-1] + counts[begin + g])

    def fetch(n):
        group, start = 0, 0
        for end in ends[:-1]:
            group = group + jnp.where(n >= end, 1, 0)
            start = jnp.where(n >= end, end, start)
        return ids[begin + group, n - start]

    batches = (ends[-1] + BATCH // 2 - 1) // (BATCH // 2)
    listed_pairs(fetch, batches, da, sq, ea, bp, bb, eb, table, work, store, freq, scale)


def weight_scratch(pairs, freq):
    return (
        [
            pltpu.VMEM((pairs, 2 * freq, 128), F32),
            pltpu.VMEM((pairs, freq, 128), F32),
            pltpu.VMEM((-(-pairs // 8) * 8, 128), F32),
            pltpu.VMEM((2, freq, BATCH * 128), BF16),
            pltpu.VMEM((2, freq, BATCH * 128), BF16),
        ]
        + [pltpu.VMEM((2, BATCH * 8, 128), F32)] * 5
        + [pltpu.VMEM((2, BATCH, 128), F32)]
    )


def two_parts(x):
    high = x.astype(BF16)
    return high, (x - high.astype(F32)).astype(BF16)


def sums_kernel(groups, events, slots, hot, hot_turned, mask, partials, *refs):
    stages = len(STAGE_SIZES)
    tables, tails = refs[: stages + 1], refs[stages + 1 : 2 * stages + 1]
    slots_out, terms_out, geo_out, own, own_geo = refs[2 * stages + 1 :]
    cands = hot.shape[1]
    rest = jnp.zeros((SLOT_ROWS - slots, 128), F32)

    @pl.loop(0, events // UNROLL)
    def _(step):
        for u in range(UNROLL):
            e = step * UNROLL + u
            parts = [tables[0][pl.ds(pl.multiple_of(e * events, 8), events), :]]
            for t, size in zip(tables[1:], STAGE_SIZES):
                rows = size * GROUP_ROWS
                parts.append(t[pl.ds(pl.multiple_of(e * rows, 8), rows), :])
            every = jnp.concatenate(parts, axis=0).astype(BF16)
            rows = pl.ds(pl.multiple_of(e * SLOT_ROWS, SLOT_ROWS), SLOT_ROWS)
            live = mask[pl.ds(e, slots, stride=events), :].astype(F32)
            live = jnp.concatenate([jnp.concatenate([live, live], axis=1), rest], axis=0)
            picked = jnp.dot(hot[rows, :], every, preferred_element_type=F32) * live
            slots_out[rows, :] = picked.astype(BF16)
            own[pl.ds(e, 1), :] = jnp.sum(picked, axis=0, keepdims=True)
            geo = partials[e].astype(F32)
            own_geo[pl.ds(e, 1), :] = jnp.concatenate([geo[0:1], geo[1:2]], axis=1)
            own_geo[pl.ds(events + e, 1), :] = jnp.concatenate([geo[2:3], geo[3:4]], axis=1)

    gathered = jnp.dot(hot_turned[...], slots_out[...], preferred_element_type=F32)
    low = low_half((cands, 128))
    gathered = jnp.where(low, gathered, -gathered)
    totals = jnp.concatenate([gathered[:events] + own[...], gathered[events:]], axis=0)
    turned = pltpu.roll(totals, 64, 1)
    weights = jnp.where(low, totals, turned)
    moves = jnp.where(low, turned, totals)
    ends = [t[start : start + 2 * GROUP_ROWS, :] for t in tails for start in range(0, t.shape[0], 2 * GROUP_ROWS)]
    first = jnp.concatenate([own_geo[:events].astype(BF16)] + [t[:GROUP_ROWS] for t in ends], axis=0)
    second = jnp.concatenate([own_geo[events:].astype(BF16)] + [t[GROUP_ROWS:] for t in ends], axis=0)
    geo_out[:, :128] = first
    geo_out[:, 128:] = second
    blocks = [first.astype(F32), second.astype(F32)]
    singles = []
    for block in blocks:
        other = pltpu.roll(block, 64, 1)
        singles += [jnp.where(low, block, other), jnp.where(low, other, block)]
    half_row = lax.broadcasted_iota(jnp.int32, (8, 128), 0)
    half_lane = lax.broadcasted_iota(jnp.int32, (8, 128), 1) // 64
    picker = jnp.where(half_row == half_lane, 1.0, 0.0).astype(BF16)
    picker = jnp.concatenate([picker, picker], axis=1)

    def halves(values):
        both = jnp.concatenate(two_parts(values), axis=1)
        return lax.dot_general(picker, both, (((1,), (1,)), ((), ())), preferred_element_type=F32)[:2]

    rights = [halves(moves * blocks[0]), halves(moves * blocks[1])]
    for i in range(4):
        scaled = weights * singles[i]
        rows = [halves(scaled * blocks[0]), halves(scaled * blocks[1]), rights[i // 2][i % 2 : i % 2 + 1]]
        share = jnp.concatenate(rows + [jnp.zeros((3, 128), F32)], axis=0)
        for q in range(terms_out.shape[1]):
            terms_out[i, q] = share


def blocks_kernel(events, place, hot, slots, geo, partials, *refs):
    outs, turned = refs[:-1], refs[-1]
    turned[...] = jnp.zeros_like(turned)
    low = low_half((SLOT_ROWS, 128))
    column = lax.broadcasted_iota(jnp.int32, (16, 128), 0) % 4
    block = lax.broadcasted_iota(jnp.int32, (16, 128), 1) // 64

    @pl.loop(0, events // UNROLL)
    def _(step):
        for u in range(UNROLL):
            e = step * UNROLL + u
            rows = pl.ds(pl.multiple_of(e * SLOT_ROWS, SLOT_ROWS), SLOT_ROWS)
            partner = jnp.dot(hot[rows, :], geo[...], preferred_element_type=F32)
            pair = slots[rows, :].astype(F32)
            weights = jnp.where(low, pair, pltpu.roll(pair, 64, 1))
            weighted = jnp.concatenate([weights * partner[:, :128], weights * partner[:, 128:]], axis=1).astype(BF16)
            own = partials[e].astype(F32)
            own = jnp.concatenate([own, own], axis=1)
            own = jnp.concatenate([jnp.broadcast_to(-own[i : i + 1], (4, 128)) for i in range(4)], axis=0)
            left = [jnp.where(column == block, own, 0.0), jnp.where(column == block + 2, own, 0.0)]
            left = jnp.concatenate(left, axis=1).astype(BF16)
            entry = lax.dot_general(left, weighted, (((1,), (1,)), ((), ())), preferred_element_type=F32)
            turned[pl.ds(e, 16, stride=events), 0:SLOT_ROWS] = entry

    for d, out in enumerate(outs):
        share = place[0] ^ d
        rows = pl.ds(pl.multiple_of(share * 4 * events, 128), 4 * events)
        out[...] = turned[rows, :].T[: out.shape[0]]


def spread_kernel(groups, clusters, received, owners, out):
    parts = []
    for g in range(groups + 1):
        part = received[clusters[g]]
        for t in range(1, 4):
            part = part + received[t * (received.shape[0] // 4) + clusters[g]]
        parts.append(part)
    high, low = two_parts(jnp.concatenate(parts, axis=1))
    out[...] = jnp.dot(high, owners[...], preferred_element_type=F32) + jnp.dot(low, owners[...], preferred_element_type=F32)


def total_kernel(events, slots, own, one, two, three, spread, normal, right):
    block = lax.broadcasted_iota(jnp.int32, (1, 128), 1) // events
    diagonal = jnp.zeros((1, 128), F32)
    for j in range(4):
        diagonal = jnp.where(block == j, spread[j : j + 1, :], diagonal)
    right[...] = spread[4:5, :events]
    total = pltpu.roll((own[...] + one[...]) + (two[...] + three[...]), 1, 0)
    top = lax.broadcasted_iota(jnp.int32, total.shape, 0) == 0
    total = jnp.where(top, diagonal, total)
    turned = total.T
    for j in range(4):
        normal[j] = turned[j * events : (j + 1) * events, : slots + 1]


def vmem(n):
    return [pl.BlockSpec(memory_space=pltpu.VMEM)] * n


def call(kernel, outs, inputs, scratch=(), specs=None, micros=1.0, limit=VMEM_LIMIT):
    shapes = [jax.ShapeDtypeStruct(s, t) for s, t in outs]
    return pl.pallas_call(
        kernel,
        out_shape=shapes,
        in_specs=specs if specs is not None else vmem(len(inputs)),
        out_specs=vmem(len(outs)),
        scratch_shapes=list(scratch),
        compiler_params=pltpu.CompilerParams(vmem_limit_bytes=limit),
        cost_estimate=pl.CostEstimate(flops=int(micros * 1e9), bytes_accessed=1024, transcendentals=0),
    )(*inputs)


def on_device(spectra, partials, pair_list, station_mask, exports):
    events, stations, two_freq = spectra.shape
    freq = two_freq // 2
    groups, cap = exports.shape
    half_span = groups // 2
    slots = pair_list.shape[1]
    sta_groups = lax.axis_size("sta")
    scale = 1.0 / (stations * sta_groups)
    offsets = [h - half_span + (1 if h >= half_span else 0) for h in range(groups)]
    cands = events + groups * GROUP_ROWS
    half = cap // 2
    table = moment_table(freq)
    smem = pl.BlockSpec(memory_space=pltpu.SMEM)
    clusters = lax.axis_size("clu")

    paired = clusters == groups + 2 and clusters & (clusters - 1) == 0
    if paired:
        masks = [m for m in range(1, clusters) if m != clusters // 2]
        routes = [[(i, i ^ m) for i in range(clusters)] for m in masks]
    else:
        order = sorted(range(groups), key=lambda h: abs(offsets[h]))
        routes = [[(i, (i + offsets[h]) % clusters) for i in range(clusters)] for h in order]

    def group_of(offset):
        offset = offset & (clusters - 1)
        return jnp.where(offset < clusters // 2, offset + half_span - 1, offset - clusters + half_span)

    def send_group(g, p):
        return group_of((p ^ masks[g]) - p) if paired else order[g]

    def receive_group(g, p):
        return group_of(p - (p ^ masks[g])) if paired else order[g]

    def receiver(g, p):
        return p ^ masks[g] if paired else (p + offsets[order[g]]) % clusters

    out_rows = cap * stations + 2 * GROUP_ROWS
    outgoing = call(
        functools.partial(outgoing_kernel, cap, send_group),
        [((out_rows, 128), BF16)] * groups,
        (exports, spectra, partials),
        scratch=[pltpu.VMEM((2 * GROUP_ROWS, 128), F32)],
        specs=[smem] + vmem(2),
        micros=2.0,
        limit=60 * 1024 * 1024,
    )
    got = [None] * groups
    for g in [0] + list(range(groups - 1, 0, -1)):
        block = outgoing[g]
        if g == LATE:
            block, got[0] = lax.optimization_barrier((block, got[0]))
        got[g] = lax.ppermute(block, "clu", routes[g])
    me = lax.axis_index("clu").astype(jnp.int32)
    sent = jnp.stack([jnp.asarray(send_group(g, me), jnp.int32) for g in range(groups)])
    came = jnp.stack([jnp.asarray(receive_group(g, me), jnp.int32) for g in range(groups)])

    duos = [j << 18 | j << 12 | e << 6 | e + 1 for j in range(events // 2) for e in range(0, 2 * j + 2, 2)]
    batches = -(-len(duos) // BATCH) * 2
    duos = duos + [1] * ((batches + 3) * (BATCH // 2) - len(duos))
    natural, got[0] = lax.optimization_barrier((spectra, got[0]))
    local, dup, square, energy = call(
        functools.partial(local_kernel, freq, events, scale, batches),
        [
            ((events * events, 128), F32),
            ((events, 128, 128), F32),
            ((events, freq, 128), F32),
            ((events, 128), F32),
        ],
        (jnp.asarray(duos, jnp.int32), natural.reshape(events // 2, 2 * stations, two_freq), table),
        scratch=weight_scratch(events // 2, freq),
        specs=[smem] + vmem(2),
        micros=8.0,
    )

    far = jnp.maximum(pair_list - events, 0)
    far_group = far // cap
    arrival = jnp.sum(jnp.where(far_group[:, :, None] == came[None, None, :], jnp.arange(groups, dtype=jnp.int32), 0), axis=2)
    entry = far % cap
    named = jnp.where(pair_list < events, -1, arrival * half + entry // 2)
    wanted = jnp.any(named[:, :, None] == jnp.arange(groups * half, dtype=jnp.int32)[None, None, :], axis=1)
    wanted = wanted.astype(F32).T.reshape(groups, half, events)
    ranks = np.arange(events)
    rank = jnp.einsum("gje,ef->gjf", wanted, jnp.asarray(ranks[:, None] < ranks[None, :], F32))
    rounded = jnp.ceil(jnp.sum(wanted, axis=2) * 0.5)
    ranks = np.arange(half)
    start = jnp.sum(rounded[:, :, None] * jnp.asarray(ranks[:, None] < ranks[None, :], F32)[None], axis=1)
    rank = rank.astype(jnp.int32)
    spot = jnp.where(wanted > 0, start.astype(jnp.int32)[:, :, None] + (rank >> 1), -1).reshape(groups, half * events)
    event_ids = jnp.arange(events, dtype=jnp.int32)[None, None, :]
    inside = np.concatenate([np.arange(size) for size in STAGE_SIZES])[:, None]
    pair_codes = jnp.asarray(((inside * GROUP_ROWS + 2 * ranks) << 17) + ((inside * half + ranks) << 12), jnp.int32)
    code = jnp.where(rank & 1 == 0, pair_codes[:, :, None] + (event_ids << 6), event_ids).reshape(groups, half * events)
    longest = half * events // 2 + 4 * BATCH // 2
    lists = jnp.sum(
        jnp.where(spot[:, None, :] == jnp.arange(longest, dtype=jnp.int32)[None, :, None], code[:, None, :], 0), axis=2
    )
    counts = jnp.sum(rounded, axis=1).astype(jnp.int32)

    column = jnp.where(pair_list < events, pair_list, events + GROUP_ROWS * arrival + entry)
    column = jnp.pad(column, ((0, 0), (0, SLOT_ROWS - slots)), constant_values=-1).reshape(-1)
    cand_ids = jnp.arange(cands, dtype=jnp.int32)
    hot = (column[:, None] == cand_ids[None, :]).astype(BF16)
    hot_turned = (cand_ids[:, None] == column[None, :]).astype(BF16)
    mask = station_mask.transpose(1, 0, 2).reshape(slots * events, stations)
    owner_rows = [jnp.asarray(np.where(np.arange(cands) < events, np.arange(cands), -1), jnp.int32)]
    hot_sent = sent[:, None] == jnp.arange(groups, dtype=jnp.int32)[None, :]
    rows_sent = jnp.sum(jnp.where(hot_sent[:, :, None], exports[None], 0), axis=1)
    for g in range(groups):
        start = events + GROUP_ROWS * g
        owner_rows.append(jnp.pad(rows_sent[g], (start, cands - start - cap), constant_values=-1))
    owners = jnp.concatenate(owner_rows)[:, None] == (jnp.arange(128, dtype=jnp.int32) % events)[None, :]
    owners = owners.astype(BF16)

    tables, tails, begin = [], [], 0
    for size in STAGE_SIZES:
        if tables:
            lists, tables[-1] = lax.optimization_barrier((lists, tables[-1]))
        table_part, tail_part = call(
            functools.partial(import_kernel, begin, size, freq, events, cap, scale),
            [((events * size * GROUP_ROWS, 128), F32), ((size * 2 * GROUP_ROWS, 128), BF16)],
            (lists, counts, *got[begin : begin + size], dup, square, energy, table),
            scratch=weight_scratch(size * half, freq),
            specs=[smem] * 2 + vmem(size + 4),
            micros=1.0 + 2.3 * size,
        )
        tables.append(table_part)
        tails.append(tail_part)
        begin += size

    weights, terms, geo = call(
        functools.partial(sums_kernel, groups, events, slots),
        [((events * SLOT_ROWS, 128), BF16), ((4, clusters, 8, 128), F32), ((cands, 256), BF16)],
        (hot, hot_turned, mask, partials, local, *tables, *tails),
        scratch=[pltpu.VMEM((events, 128), F32), pltpu.VMEM((2 * events, 128), F32)],
        micros=2.4,
    )
    message_rows = -(-(slots + 1) // 8) * 8
    place = lax.axis_index("sta").astype(jnp.int32).reshape(1)
    shares = call(
        functools.partial(blocks_kernel, events),
        [((message_rows, 128), F32)] * 4,
        (place, hot, weights, geo, partials),
        scratch=[pltpu.VMEM((16 * events, 128), F32)],
        specs=[smem] + vmem(4),
        micros=1.7,
    )
    shares = [shares[0]] + [lax.ppermute(shares[d], "sta", [(i, i ^ d) for i in range(4)]) for d in range(1, 4)]
    terms = lax.all_to_all(
        terms.reshape(4 * clusters, 8, 128), ("sta", "clu"), split_axis=0, concat_axis=0, tiled=True
    )
    sources = jnp.stack([me] + [jnp.asarray(receiver(g, me), jnp.int32) for g in range(groups)])
    (spread,) = call(
        functools.partial(spread_kernel, groups),
        [((8, 128), F32)],
        (sources, terms, owners),
        specs=[smem] + vmem(2),
    )
    normal, right = call(
        functools.partial(total_kernel, events, slots),
        [((4, events, slots + 1), F32), ((1, events), F32)],
        (*shares, spread),
    )
    return (normal.transpose(0, 2, 1), right)


def solution(mesh):
    return jax.shard_map(
        on_device,
        mesh=mesh,
        in_specs=(
            P("clu", "sta", None),
            P("clu", None, "sta"),
            P("clu", None),
            P("clu", None, "sta"),
            P("clu", None),
        ),
        out_specs=(P("sta", None, "clu"), P("sta", "clu")),
        check_vma=False,
    )
```
